128 devices in a mesh: dp: 32 (over y, z, core), tensor: 4 (over x).
Axes of the slice: x: 4, y: 4, z: 4, core: 2. Of those that a mesh axis runs over, the one named last changes fastest.
Arguments:
- tokens: bfloat16 [32768, 1536], P(('dp', 'tensor')), may hold values from -6 to 6
- norm_gains: float32 [2, 1536], replicated, may hold values from 0.5 to 1.5
- query_matrix: bfloat16 [1536, 1536], P(None, 'tensor'), may hold values from -0.15625 to 0.15625
- key_value_weight: bfloat16 [1536, 2, 512], P(None, None, 'tensor'), may hold values from -0.15625 to 0.15625
- output_weight: bfloat16 [1536, 1536], P('tensor'), may hold values from -0.625 to 0.625
- router: bfloat16 [32, 1536], replicated, may hold values from -0.078125 to 0.078125
- expert_up: bfloat16 [32, 1536, 1024], P('dp'), may hold values from -0.15625 to 0.15625
- expert_down: bfloat16 [32, 512, 1536], P('dp'), may hold values from -1 to 1
- routes: int32 [32768, 8], P(('dp', 'tensor')), may hold values from 0 to 31, all different within a row; in each aligned block of 256 rows (0 to 255, 256 to 511, ...) at most 68 rows name the same one
- cotangent: bfloat16 [32768, 1536], P(('dp', 'tensor')), may hold values from -6 to 6
Outputs:
- layer_out: bfloat16 [32768, 1536], P(('dp', 'tensor'))
- tokens_grad: float32 [32768, 1536], P(('dp', 'tensor'))
- gains_grad: float32 [2, 1536], P(None, ('dp', 'tensor'))
- query_weight_grad: float32 [1536, 1536], P('dp', 'tensor')
- keyval_weight_grad: float32 [1536, 2, 512], P('dp', None, 'tensor')
- output_weight_grad: float32 [1536, 1536], P('tensor', 'dp')
- router_grad: float32 [32, 1536], P(None, ('dp', 'tensor'))
- expert_up_grad: float32 [32, 1536, 1024], P('dp', 'tensor')
- expert_down_grad: float32 [32, 512, 1536], P('dp', None, 'tensor')
The draws below stay inside these ranges and needn't reach their ends.
Inputs may be any that keep to these rules, and one draw needn't show every extreme that they name: `routes`: each row names 8 different experts; in each aligned block of 256 rows (one device's tokens) no expert is named by more than 68 rows, a bound that some block reaches.
All inputs are finite; a program needn't handle non-finite values.
Results may differ from the reference program's by a relative error of at most 0.025.
Values may be sent and summed in bfloat16 or wider, within the bound.
No kernel may reach another device: no remote copies, remote signals or barrier semaphores. Data moves between devices by JAX's collectives and lax.ppermute only.
A program may use at most 192 MiB of HBM per device.

```python
import math
import jax
import jax.numpy as jnp
import numpy as np
from jax import lax

MODEL_DIM = 1536
QUERY_HEADS = 24
KEY_VALUE_HEADS = 8
HEAD_DIM = 64
FF = 512
TOPK = 8
EXPERTS = 32
TOK_DEV = 256
SEQ_LEN = 1024
TOKENS = 32768
CAP = 68
N_DP = 32
N_TENSOR = 4


def levels(key, extent, cuts, low, high):
    def one(dim, shards_of):
        steps = jax.random.uniform(jax.random.fold_in(jax.random.fold_in(key, 6), dim), (shards_of,), jnp.float32, low / len(cuts), high / len(cuts))
        return jnp.repeat(jnp.exp(steps), extent[dim] // shards_of).reshape((-1,) + (1,) * (len(extent) - dim - 1))

    gain = one(*cuts[0])
    for cut in cuts[1:]:
        gain = gain * one(*cut)
    return gain


def deal_out(own_key, own, number, rows, number_of, top, most, lean):
    sequence = jax.random.permutation(own_key, number_of)
    heavy_load, usual = portions_of(number_of, rows * top, most, lean, True), portions_of(number_of, rows * top, most, lean, False)
    places = jnp.arange(number_of)

    def named(lengths, offset_by):
        used = int((lengths > 0).sum())
        fixed = max(1, used // 4)
        shifted = fixed + (places - fixed + offset_by * (used - fixed)) % max(1, number_of - fixed)
        return jnp.zeros((number_of,), jnp.int32).at[sequence[jnp.where(places < fixed, places, shifted)]].set(jnp.asarray(lengths, jnp.int32))

    lengths = jnp.where(number % 4 == 0, named(heavy_load, number // 4), named(usual, number - number // 4 - 1))
    mixed = jax.random.permutation(jax.random.fold_in(own, 3), number_of)
    giver, sink = mixed[0:number_of // 2 * 2:2], mixed[1:number_of // 2 * 2:2]
    room = jnp.minimum(lengths[giver] - 1, most - lengths[sink]) // 2
    room = jnp.where((giver == sequence[0]) | (sink == sequence[0]) | (lengths[sink] == 0), 0, jnp.maximum(room, 0))
    shifted = jax.random.randint(jax.random.fold_in(own, 4), (number_of // 2,), 0, 1 << 20) % (room + 1)
    lengths = lengths.at[giver].add(-shifted).at[sink].add(shifted)
    members = jnp.searchsorted(jnp.cumsum(lengths), jnp.arange(rows * top), side="right").astype(jnp.int32)
    listing = members.reshape(top, rows).T
    listing = listing[jax.random.permutation(jax.random.fold_in(own, 1), rows)]
    offset_by = jax.random.randint(jax.random.fold_in(own, 2), (rows, 1), 0, top)
    return jnp.take_along_axis(listing, (jnp.arange(top)[None, :] + offset_by) % top, axis=1)


def portions_of(number_of, total, limit, skew, full):
    portions = [(1 << 20) // math.isqrt(standing ** skew) + 1 for standing in range(1, number_of + 1)]
    largest = limit if full else min(limit, max(-(-total // number_of), total * portions[0] // sum(portions)))
    least = 1 if total - largest >= number_of - 1 else 0
    holding, spare = [largest] + [least] * (number_of - 1), total - largest - least * (number_of - 1)
    while spare > 0:
        free = [i for i in range(1, number_of) if holding[i] < largest] or [i for i in range(1, number_of) if holding[i] < limit]
        whole, remaining = sum([portions[i] for i in free]), spare
        for i in free:
            more = min(limit - holding[i], max(1, remaining * portions[i] // whole), spare)
            holding[i] = holding[i] + more
            spare = spare - more
    return np.array(holding)


def bell_draw(own_key, dims, spread, bound, split=(), held_as=jnp.bfloat16):
    loudness = levels(own_key, dims, split, -0.22, 0.18) if split else 1.0
    entries = jax.random.normal(own_key, dims, jnp.float32) * spread * loudness
    return jnp.minimum(jnp.maximum(entries, -bound), bound).astype(held_as)


def setup_inputs(seed: int = 0) -> dict:
    seeds = jax.random.split(jax.random.key(seed), 11)
    tokens = bell_draw(seeds[0], (TOKENS, MODEL_DIM), 1.0, 6.0, ((0, 128),))
    norm_gains = jnp.clip(1.0 + 0.1 * jax.random.normal(seeds[1], (2, MODEL_DIM), jnp.float32), 0.5, 1.5)
    query_matrix = bell_draw(seeds[2], (MODEL_DIM, QUERY_HEADS * HEAD_DIM), MODEL_DIM ** -0.5, 0.15625, ((1, 4),))
    key_value_weight = bell_draw(seeds[3], (MODEL_DIM, 2, KEY_VALUE_HEADS * HEAD_DIM), MODEL_DIM ** -0.5, 0.15625, ((2, 4),))
    output_weight = bell_draw(seeds[4], (QUERY_HEADS * HEAD_DIM, MODEL_DIM), (QUERY_HEADS * HEAD_DIM // 16) ** -0.5, 0.625, ((0, 4),))
    router = bell_draw(seeds[5], (EXPERTS, MODEL_DIM), (4 * MODEL_DIM) ** -0.5, 0.078125)
    expert_up = bell_draw(seeds[6], (EXPERTS, MODEL_DIM, 2 * FF), MODEL_DIM ** -0.5, 0.15625, ((0, 32),))
    expert_down = bell_draw(seeds[7], (EXPERTS, FF, MODEL_DIM), (FF // 16) ** -0.5, 1.0, ((0, 32),))
    routes_keys = jax.random.split(jax.random.fold_in(seeds[8], 1), TOKENS // TOK_DEV)
    routes_turns = jax.random.permutation(jax.random.fold_in(seeds[8], 3), TOKENS // TOK_DEV)
    routes = jax.vmap(lambda own, number: deal_out(jax.random.fold_in(seeds[8], 2), own, number, TOK_DEV, EXPERTS, TOPK, CAP, 2))(routes_keys, routes_turns).reshape((TOKENS, TOPK))
    cotangent = bell_draw(seeds[9], (TOKENS, MODEL_DIM), 1.0, 6.0, ((0, 128),))
    return dict(tokens=tokens, norm_gains=norm_gains, query_matrix=query_matrix, key_value_weight=key_value_weight, output_weight=output_weight, router=router, expert_up=expert_up, expert_down=expert_down, routes=routes, cotangent=cotangent)


@jax.custom_vjp
def reduced_precision(v):
    return lax.optimization_barrier(v.astype(jnp.bfloat16)).astype(jnp.float32)

@jax.custom_vjp
def low_back(v):
    return v

def low_keep(v):
    return (reduced_precision(v), None)

def low_pass(kept, grad):
    return (grad,)

def back_keep(v):
    return (v, None)

def back_low(kept, grad):
    return (reduced_precision(grad),)
reduced_precision.defvjp(low_keep, low_pass)
low_back.defvjp(back_keep, back_low)
epsilon = 1e-06
theta = 10000.0
highest = lax.Precision.HIGHEST

def rms_normed(values, gain_row):
    return values * lax.rsqrt(lax.optimization_barrier(jnp.mean(values * values, axis=-1, keepdims=True)) + epsilon) * gain_row

def rotary_tables(sequence_length, head_width):
    half_width = head_width // 2
    freqs = theta ** (-(jnp.arange(half_width).astype(jnp.float32) * 2.0 / head_width))
    angles = jnp.arange(sequence_length).astype(jnp.float32)[:, None] * freqs[None, :]
    return (jnp.cos(angles), jnp.sin(angles))

def apply_rotary(values, cosine_table, sine_table):
    half_width = values.shape[-1] // 2
    first_half = values[..., :half_width]
    second_half = values[..., half_width:]
    cos_rows = cosine_table[:, None, :]
    sin_rows = sine_table[:, None, :]
    return jnp.concatenate([first_half * cos_rows - second_half * sin_rows, second_half * cos_rows + first_half * sin_rows], axis=-1)

def attend_sequence(normed, query_matrix, key_value_weight, output_weight):
    sequence_length = normed.shape[0]
    cosine_table, sine_table = rotary_tables(sequence_length, HEAD_DIM)
    merged_heads = jnp.concatenate([query_matrix, key_value_weight.reshape(MODEL_DIM, 2 * KEY_VALUE_HEADS * HEAD_DIM)], axis=1)
    projected_rows = low_back(jnp.dot(normed, merged_heads, precision=highest))
    query_rows = reduced_precision(apply_rotary(projected_rows[:, :QUERY_HEADS * HEAD_DIM].reshape(sequence_length, QUERY_HEADS, HEAD_DIM), cosine_table, sine_table))
    every_key = reduced_precision(apply_rotary(projected_rows[:, QUERY_HEADS * HEAD_DIM:(QUERY_HEADS + KEY_VALUE_HEADS) * HEAD_DIM].reshape(sequence_length, KEY_VALUE_HEADS, HEAD_DIM), cosine_table, sine_table))
    every_value = reduced_precision(projected_rows[:, (QUERY_HEADS + KEY_VALUE_HEADS) * HEAD_DIM:].reshape(sequence_length, KEY_VALUE_HEADS, HEAD_DIM))
    rows_per_block = min(512, sequence_length)
    block_count = sequence_length // rows_per_block
    query_block_list = query_rows.reshape(block_count, rows_per_block, KEY_VALUE_HEADS, QUERY_HEADS // KEY_VALUE_HEADS, HEAD_DIM)
    block_starts = (jnp.arange(block_count) * rows_per_block).astype(jnp.int32)
    key_index = jnp.arange(sequence_length).astype(jnp.int32)

    def one_block(operands):
        query_piece, row_start = operands
        scores = low_back(jnp.einsum('qhgd,shd->hgqs', query_piece, every_key, precision=highest) * HEAD_DIM ** (-0.5))
        row_index = row_start + jnp.arange(rows_per_block).astype(jnp.int32)
        scores = jnp.where(row_index[:, None] >= key_index[None, :], scores, -1e+30)
        row_max = lax.optimization_barrier(jnp.max(scores, axis=-1, keepdims=True))
        exp_scores = jnp.exp(scores - row_max)
        attn_probs = reduced_precision(exp_scores / lax.optimization_barrier(jnp.sum(exp_scores, axis=-1, keepdims=True)))
        attended = jnp.einsum('hgqs,shd->qhgd', attn_probs, every_value, precision=highest)
        return low_back(reduced_precision(attended)).reshape(rows_per_block, QUERY_HEADS * HEAD_DIM)
    attended = lax.map(jax.checkpoint(one_block), (query_block_list, block_starts)).reshape(sequence_length, QUERY_HEADS * HEAD_DIM)
    return jnp.dot(attended, output_weight, precision=highest)

def layer_forward(tokens, norm_gains, query_matrix, key_value_weight, output_weight, router, expert_up, expert_down, routes, slot_token, slot_live, slot_rank):
    normed = reduced_precision(rms_normed(tokens, norm_gains[0]))

    def one_sequence(seq_rows):
        return attend_sequence(seq_rows, query_matrix, key_value_weight, output_weight)
    attn_sum = lax.map(one_sequence, normed.reshape(N_DP, SEQ_LEN, MODEL_DIM)).reshape(TOKENS, MODEL_DIM)
    middle = tokens + low_back(attn_sum)
    mixed_norm = reduced_precision(rms_normed(middle, norm_gains[1]))
    logits = jnp.dot(mixed_norm, router.T, precision=highest)
    chosen = jnp.take_along_axis(logits, routes, axis=1)
    chosen_exp = jnp.exp(chosen - lax.optimization_barrier(jnp.max(chosen, axis=1, keepdims=True)))
    gate_weights = chosen_exp / lax.optimization_barrier(jnp.sum(chosen_exp, axis=1, keepdims=True))

    def one_expert(operands):
        up_matrix, down_matrix, token_ids, live_rows = operands
        expert_rows = low_back(mixed_norm[token_ids]) * live_rows[:, None]
        gate_up = low_back(jnp.dot(expert_rows, up_matrix, precision=highest))
        gate_part = gate_up[:, :FF]
        up_part = gate_up[:, FF:]
        hidden = reduced_precision(gate_part * jax.nn.sigmoid(gate_part) * up_part)
        return low_back(reduced_precision(jnp.dot(hidden, down_matrix, precision=highest)))
    expert_outs = lax.map(jax.checkpoint(one_expert), (expert_up, expert_down, slot_token, slot_live))
    moe_sum = jnp.zeros((TOKENS, MODEL_DIM), jnp.float32)
    for route_rank in range(TOPK):
        picked = expert_outs[routes[:, route_rank], slot_rank[:, route_rank]]
        moe_sum = moe_sum + gate_weights[:, route_rank:route_rank + 1] * picked
    return middle + moe_sum

def reference(tokens, norm_gains, query_matrix, key_value_weight, output_weight, router, expert_up, expert_down, routes, cotangent):
    flat_routes = routes.reshape(-1).astype(jnp.int32)
    pair_count = flat_routes.shape[0]
    expert_ids = jnp.arange(EXPERTS).astype(jnp.int32)
    counts = lax.optimization_barrier(jnp.sum((flat_routes[:, None] == expert_ids[None, :]).astype(jnp.int32), axis=0))
    offsets = (jnp.cumsum(counts) - counts).astype(jnp.int32)
    order = jnp.argsort(flat_routes, stable=True).astype(jnp.int32)
    inverse = jnp.zeros((pair_count,), jnp.int32).at[order].set(jnp.arange(pair_count).astype(jnp.int32))
    slot_rank = (inverse - offsets[flat_routes]).astype(jnp.int32).reshape(TOKENS, TOPK)
    most_rows = CAP * N_DP * N_TENSOR
    spots = jnp.arange(most_rows).astype(jnp.int32)
    where_sorted = jnp.minimum(offsets[:, None] + spots[None, :], pair_count - 1).astype(jnp.int32)
    slot_token = (order[where_sorted] // TOPK).astype(jnp.int32)
    slot_live = (spots[None, :] < counts[:, None]).astype(jnp.float32)

    def forward(tokens_float, gains_float, query_float, keyval_float, output_float, router_float, up_float, down_float):
        return layer_forward(tokens_float, gains_float, query_float, keyval_float, output_float, router_float, up_float, down_float, routes, slot_token, slot_live, slot_rank)
    layer_out, pullback = jax.vjp(forward, tokens.astype(jnp.float32), norm_gains.astype(jnp.float32), query_matrix.astype(jnp.float32), key_value_weight.astype(jnp.float32), output_weight.astype(jnp.float32), router.astype(jnp.float32), expert_up.astype(jnp.float32), expert_down.astype(jnp.float32))
    grads = pullback(cotangent.astype(jnp.float32))
    return (layer_out.astype(jnp.bfloat16), grads[0], grads[1], grads[2], grads[3], grads[4], grads[5], grads[6], grads[7])
```

```python
import jax
import jax.numpy as jnp
from jax import lax
from jax.sharding import PartitionSpec as P

QUERY_HEADS = 24
KEY_VALUE_HEADS = 8
HEAD_DIM = 64
FF = 512
CAP = 68
ROWS = 72


epsilon = 1e-06
theta = 10000.0
highest = lax.Precision.HIGHEST
f32 = jnp.float32
bf16 = jnp.bfloat16


def dot(a, b, ca, cb, precision=None):
    return lax.dot_general(
        a, b, (((ca,), (cb,)), ((), ())), preferred_element_type=f32, precision=precision
    )


def norm_rows(values, gain_row):
    inv_rms = lax.rsqrt(jnp.mean(values * values, axis=-1, keepdims=True) + epsilon)
    return (values * inv_rms * gain_row, inv_rms)


def norm_back(values, inv_rms, gain_row, upstream):
    scaled = upstream * gain_row
    inner_sum = jnp.mean(scaled * values, axis=-1, keepdims=True)
    return inv_rms * scaled - values * (inv_rms * inv_rms * inv_rms) * inner_sum


def rotary_tables(sequence_length, head_width):
    half_width = head_width // 2
    freqs = theta ** (-(jnp.arange(half_width).astype(jnp.float32) * 2.0 / head_width))
    angles = jnp.arange(sequence_length).astype(jnp.float32)[:, None] * freqs[None, :]
    return (jnp.cos(angles), jnp.sin(angles))


def apply_rotary(values, cosine_table, sine_table, direction):
    half_width = values.shape[-1] // 2
    first_half = values[..., :half_width]
    second_half = values[..., half_width:]
    cos_rows = cosine_table[:, None, :]
    sin_rows = sine_table[:, None, :] * direction
    return jnp.concatenate(
        [
            first_half * cos_rows - second_half * sin_rows,
            second_half * cos_rows + first_half * sin_rows,
        ],
        axis=-1,
    )


def split_two(values):
    high = lax.reduce_precision(values, 8, 7)
    return high, values - high


def shift_tensor(values, step):
    return lax.ppermute(values, "tensor", [(i, (i + step) % 4) for i in range(4)])


def gather_tensor(mine, place):
    rows, width = mine.shape
    half = rows // 2
    left = shift_tensor(mine, 1)
    right = shift_tensor(mine, -1)
    far_top = shift_tensor(left[:half], 1)
    far_low = shift_tensor(right[half:], -1)
    whole = jnp.zeros((4 * rows, width), mine.dtype)
    for piece, owner, offset in (
        (mine, 0, 0),
        (left, 3, 0),
        (right, 1, 0),
        (far_top, 2, 0),
        (far_low, 2, half),
    ):
        start = lax.rem(place + owner, 4) * rows + offset
        whole = lax.dynamic_update_slice(whole, piece, (start, jnp.int32(0)))
    return whole


def scatter_tensor(chunk):
    far = chunk(2).astype(bf16)
    half = far.shape[0] // 2
    from_left = shift_tensor(far[:half], 1)
    from_right = shift_tensor(far[half:], -1)
    near_right = chunk(1)
    near_left = chunk(3)
    near_right = jnp.concatenate([near_right[:half] + from_left, near_right[half:]], axis=0)
    near_left = jnp.concatenate([near_left[:half], near_left[half:] + from_right], axis=0)
    one = shift_tensor(near_right.astype(bf16), 1)
    two = shift_tensor(near_left.astype(bf16), -1)
    return chunk(0) + one + two


def exchange(values):
    return lax.all_to_all(values, "dp", split_axis=0, concat_axis=0, tiled=True)


def per_device(
    tokens,
    norm_gains,
    query_matrix,
    key_value_weight,
    output_weight,
    router,
    expert_up,
    expert_down,
    routes,
    cotangent,
):
    local_rows, model_width = tokens.shape
    query_width = query_matrix.shape[1]
    keyval_width = key_value_weight.shape[2]
    head_width = HEAD_DIM
    group_width = QUERY_HEADS // KEY_VALUE_HEADS
    kv_heads = keyval_width // head_width
    local_heads = query_width // head_width
    experts_all = router.shape[0]
    place = lax.axis_index("tensor")
    group = lax.axis_index("dp")

    expert_index = jnp.arange(experts_all, dtype=jnp.int32)
    picked = jnp.any(routes[:, :, None] == expert_index[None, None, :], axis=1)
    token_index = jnp.arange(local_rows, dtype=jnp.int32)
    before = (token_index[:, None] > token_index[None, :]).astype(bf16)
    rank = dot(before, picked.astype(bf16), 1, 0)
    slot = jnp.where(picked, rank, -1.0)
    slot_turned = slot.T
    slot_index = jnp.arange(ROWS, dtype=jnp.int32).astype(f32)
    sending = slot_turned[:, None, :] == slot_index[None, :, None]
    send_matrix = sending.astype(bf16).reshape(experts_all * ROWS, local_rows)

    cot_send = dot(send_matrix, cotangent, 1, 0).astype(bf16)
    cot_rows = exchange(cot_send.reshape(experts_all, ROWS, model_width))
    cot_rows = cot_rows.reshape(experts_all * ROWS, model_width)

    inputs = tokens.astype(jnp.float32)
    normed, inv_rms_one = norm_rows(inputs, norm_gains[0])
    sequence = gather_tensor(normed.astype(jnp.bfloat16), place)
    sequence_length = sequence.shape[0]
    joined_weight = jnp.concatenate(
        [query_matrix, key_value_weight.reshape(model_width, 2 * keyval_width)], axis=1
    )
    projected_rows = jnp.dot(sequence, joined_weight, preferred_element_type=jnp.float32)
    cosine_table, sine_table = rotary_tables(sequence_length, head_width)
    query_rows = apply_rotary(
        projected_rows[:, :query_width].reshape(sequence_length, local_heads, head_width),
        cosine_table,
        sine_table,
        1.0,
    ).astype(jnp.bfloat16)
    keys_low = apply_rotary(
        projected_rows[:, query_width : query_width + keyval_width].reshape(
            sequence_length, kv_heads, head_width
        ),
        cosine_table,
        sine_table,
        1.0,
    ).astype(jnp.bfloat16)
    values_low = (
        projected_rows[:, query_width + keyval_width :]
        .reshape(sequence_length, kv_heads, head_width)
        .astype(jnp.bfloat16)
    )
    rows_per_block = min(512, sequence_length)
    block_count = sequence_length // rows_per_block
    query_block_list = query_rows.reshape(
        block_count, rows_per_block, kv_heads, group_width, head_width
    )
    block_starts = jnp.arange(block_count, dtype=jnp.int32) * rows_per_block
    key_index = jnp.arange(sequence_length, dtype=jnp.int32)
    factor = head_width ** (-0.5)

    def masked_scores(query_piece, row_start):
        raw_scores = (
            jnp.einsum("qhgd,shd->hgqs", query_piece, keys_low, preferred_element_type=jnp.float32)
            * factor
        )
        row_index = row_start + jnp.arange(rows_per_block, dtype=jnp.int32)
        return jnp.where(row_index[:, None] >= key_index[None, :], raw_scores, -1e30)

    def forward_block(operands):
        query_piece, row_start = operands
        scores = masked_scores(query_piece, row_start)
        row_max = jnp.max(scores, axis=-1, keepdims=True)
        exp_scores = jnp.exp(scores - row_max)
        row_total = jnp.sum(exp_scores, axis=-1, keepdims=True)
        attn_probs = (exp_scores / row_total).astype(jnp.bfloat16)
        attended_piece = jnp.einsum(
            "hgqs,shd->qhgd", attn_probs, values_low, preferred_element_type=jnp.float32
        )
        return (attended_piece.astype(jnp.bfloat16), row_max + jnp.log(row_total))

    attended_blocks, log_totals = lax.map(forward_block, (query_block_list, block_starts))
    attended = attended_blocks.reshape(sequence_length, query_width)

    def output_chunk(k):
        start = lax.rem(place + k, 4) * local_rows
        return dot(lax.dynamic_slice_in_dim(attended, start, local_rows, 0), output_weight, 1, 0)

    middle = inputs + scatter_tensor(output_chunk)
    mixed_norm, inv_rms_two = norm_rows(middle, norm_gains[1])
    mixed_low = mixed_norm.astype(jnp.bfloat16)
    logits = dot(mixed_low, router, 1, 1)
    chosen = jnp.where(picked, logits, -jnp.inf)
    chosen_exp = jnp.exp(chosen - jnp.max(chosen, axis=1, keepdims=True))
    gates = chosen_exp / jnp.sum(chosen_exp, axis=1, keepdims=True)

    spare = jnp.arange(ROWS, dtype=jnp.int32)[None, :, None]

    def with_spare(rows, slot_values):
        high, low = split_two(slot_values)
        wide = ((0, 0), (0, model_width - ROWS))
        high = jnp.pad(high, wide)[:, None, :]
        low = jnp.pad(low, wide)[:, None, :]
        rows = jnp.where(spare == CAP, high, rows)
        return jnp.where(spare == CAP + 1, low, rows).astype(bf16)

    def from_spare(rows):
        return rows[:, CAP, :ROWS].astype(f32) + rows[:, CAP + 1, :ROWS].astype(f32)

    gates_slot = jnp.sum(jnp.where(sending, gates.T[:, None, :], 0.0), axis=2)
    mixed_send = dot(send_matrix, mixed_low, 1, 0).reshape(experts_all, ROWS, model_width)
    received = exchange(with_spare(mixed_send, gates_slot))
    gate_column = from_spare(received).reshape(experts_all * ROWS, 1)
    rows_in = received.reshape(experts_all * ROWS, model_width)

    up_matrix, down_matrix = expert_up[0], expert_down[0]
    grad_hidden_one = dot(cot_rows, down_matrix, 1, 1)
    gate_up = dot(rows_in, up_matrix, 1, 0)
    gate_part = gate_up[:, :FF]
    up_part = gate_up[:, FF:]
    sigmoid_gate = jax.nn.sigmoid(gate_part)
    hidden = gate_part * sigmoid_gate * up_part
    hidden_gated = (gate_column * hidden).astype(bf16)
    grad_gate_slot = jnp.sum(hidden * grad_hidden_one, axis=1).reshape(experts_all, ROWS)
    grad_hidden = grad_hidden_one * gate_column
    grad_gate_part = grad_hidden * up_part * sigmoid_gate * (1.0 + gate_part * (1.0 - sigmoid_gate))
    grad_up_part = grad_hidden * gate_part * sigmoid_gate
    grad_gate_up = jnp.concatenate([grad_gate_part, grad_up_part], axis=-1).astype(jnp.bfloat16)
    grad_rows = dot(grad_gate_up, up_matrix, 1, 1).reshape(experts_all, ROWS, model_width)
    grad_back = exchange(with_spare(grad_rows, grad_gate_slot))

    expert_result = dot(hidden_gated, down_matrix, 1, 0).astype(bf16)
    result_back = exchange(expert_result.reshape(experts_all, ROWS, model_width))
    up_grad = dot(rows_in, grad_gate_up, 0, 0).astype(bf16)
    down_grad = dot(cot_rows, hidden_gated, 0, 0).astype(bf16)
    expert_up_grad = lax.psum_scatter(up_grad, "tensor", scatter_dimension=0, tiled=True)
    expert_down_grad = lax.psum_scatter(down_grad, "tensor", scatter_dimension=0, tiled=True)
    expert_up_grad = expert_up_grad.astype(f32)[None]
    expert_down_grad = expert_down_grad.astype(f32).T[None]

    grad_gate = jnp.sum(jnp.where(sending, from_spare(grad_back)[:, :, None], 0.0), axis=1).T
    grad_logits = gates * (grad_gate - jnp.sum(gates * grad_gate, axis=1, keepdims=True))
    grad_mixed = dot(send_matrix, grad_back.reshape(experts_all * ROWS, model_width), 0, 0)
    grad_mixed = grad_mixed + dot(grad_logits, router.astype(f32), 1, 0, highest)
    router_part = dot(mixed_low.astype(f32), grad_logits, 0, 0, highest)
    grad_out = cotangent.astype(jnp.float32)
    grad_middle = grad_out + norm_back(middle, inv_rms_two, norm_gains[1], grad_mixed)
    gain_two_part = jnp.sum(grad_mixed * middle * inv_rms_two, axis=0)

    grad_attn_seq = gather_tensor(grad_middle.astype(jnp.bfloat16), place)
    output_grad_turned = dot(grad_attn_seq, attended, 0, 0)
    router_high, router_low = split_two(router_part)
    gain_high, gain_low = split_two(gain_two_part)
    output_joined = jnp.concatenate(
        [
            output_grad_turned.astype(bf16),
            router_high.astype(bf16),
            router_low.astype(bf16),
            gain_high.astype(bf16)[:, None],
            gain_low.astype(bf16)[:, None],
            jnp.zeros((model_width, 62), bf16),
        ],
        axis=1,
    )
    dp_size = 32
    dp_rows = model_width // dp_size
    output_all = jnp.sum(
        exchange(output_joined.reshape(dp_size, dp_rows, query_width + 128)).astype(f32), axis=0
    )
    output_weight_grad = output_all[:, :query_width].T

    grad_attended = dot(grad_attn_seq, output_weight, 1, 1).astype(jnp.bfloat16)
    grad_blocks = grad_attended.reshape(
        block_count, rows_per_block, kv_heads, group_width, head_width
    )

    def backward_block(totals, operands):
        key_total, value_total = totals
        query_piece, grad_piece, row_start, log_total = operands
        attn_probs = jnp.exp(masked_scores(query_piece, row_start) - log_total)
        value_total = value_total + jnp.einsum(
            "hgqs,qhgd->shd",
            attn_probs.astype(jnp.bfloat16),
            grad_piece,
            preferred_element_type=jnp.float32,
        )
        grad_probs = jnp.einsum(
            "qhgd,shd->hgqs", grad_piece, values_low, preferred_element_type=jnp.float32
        )
        row_inner = jnp.sum(attn_probs * grad_probs, axis=-1, keepdims=True)
        grad_scores = (attn_probs * (grad_probs - row_inner)).astype(jnp.bfloat16)
        query_grad = (
            jnp.einsum("hgqs,shd->qhgd", grad_scores, keys_low, preferred_element_type=jnp.float32)
            * factor
        )
        key_total = (
            key_total
            + jnp.einsum(
                "hgqs,qhgd->shd", grad_scores, query_piece, preferred_element_type=jnp.float32
            )
            * factor
        )
        return ((key_total, value_total), query_grad)

    zero_keys = jnp.zeros((sequence_length, kv_heads, head_width), jnp.float32)
    (key_grad, value_grad), query_grads = lax.scan(
        backward_block,
        (zero_keys, zero_keys),
        (query_block_list, grad_blocks, block_starts, log_totals),
    )
    query_grad_back = apply_rotary(
        query_grads.reshape(sequence_length, local_heads, head_width),
        cosine_table,
        sine_table,
        -1.0,
    )
    key_grad_back = apply_rotary(key_grad, cosine_table, sine_table, -1.0)
    grad_projected = jnp.concatenate(
        [
            query_grad_back.reshape(sequence_length, query_width),
            key_grad_back.reshape(sequence_length, keyval_width),
            value_grad.reshape(sequence_length, keyval_width),
        ],
        axis=1,
    ).astype(jnp.bfloat16)
    joined_grad = dot(sequence, grad_projected, 0, 0).astype(bf16)
    joined_all = jnp.sum(
        exchange(joined_grad.reshape(dp_size, dp_rows, query_width + 2 * keyval_width)).astype(f32),
        axis=0,
    )
    query_weight_grad = joined_all[:, :query_width]
    keyval_weight_grad = joined_all[:, query_width:].reshape(dp_rows, 2, keyval_width)

    def normed_chunk(k):
        start = lax.rem(place + k, 4) * local_rows
        piece = lax.dynamic_slice_in_dim(grad_projected, start, local_rows, 0)
        return dot(piece, joined_weight, 1, 1)

    grad_normed = scatter_tensor(normed_chunk)
    tokens_grad = grad_middle + norm_back(inputs, inv_rms_one, norm_gains[0], grad_normed)

    weight_rows = lax.dynamic_slice_in_dim(joined_weight, group * dp_rows, dp_rows, 0)
    gain_rows = lax.dynamic_slice_in_dim(norm_gains[0], group * dp_rows, dp_rows, 0)
    gain_one_part = jnp.sum(weight_rows.astype(f32) * joined_all, axis=1) / gain_rows
    base = query_width
    small = jnp.concatenate(
        [
            output_all[:, base : base + 32] + output_all[:, base + 32 : base + 64],
            gain_one_part[:, None],
            (output_all[:, base + 64] + output_all[:, base + 65])[:, None],
            jnp.zeros((dp_rows, 94), f32),
        ],
        axis=1,
    ).reshape(4, dp_rows // 4, 128)
    small = jnp.pad(small, ((0, 0), (0, 4), (0, 0)))
    small = lax.all_to_all(small, "tensor", split_axis=0, concat_axis=0, tiled=True)
    small = jnp.sum(small, axis=0)[: dp_rows // 4].T
    router_grad = small[:experts_all]
    gains_grad = small[experts_all : experts_all + 2]

    moe_sum = dot(send_matrix, result_back.reshape(experts_all * ROWS, model_width), 0, 0)
    layer_out = (middle + moe_sum).astype(jnp.bfloat16)
    return (
        layer_out,
        tokens_grad,
        gains_grad,
        query_weight_grad,
        keyval_weight_grad,
        output_weight_grad,
        router_grad,
        expert_up_grad,
        expert_down_grad,
    )


def solution(mesh):
    placed = (
        P(("dp", "tensor"), None),
        P(),
        P(None, "tensor"),
        P(None, None, "tensor"),
        P("tensor", None),
        P(),
        P("dp", None, None),
        P("dp", None, None),
        P(("dp", "tensor"), None),
        P(("dp", "tensor"), None),
    )
    return jax.shard_map(
        per_device,
        mesh=mesh,
        in_specs=placed,
        out_specs=(
            P(("dp", "tensor"), None),
            P(("dp", "tensor"), None),
            P(None, ("dp", "tensor")),
            P("dp", "tensor"),
            P("dp", None, "tensor"),
            P("tensor", "dp"),
            P(None, ("dp", "tensor")),
            P("dp", "tensor", None),
            P("dp", None, "tensor"),
        ),
        check_vma=False,
    )
```

```python
import jax
import jax.numpy as jnp
from jax import lax
from jax.experimental import pallas as pl
from jax.experimental.pallas import tpu as pltpu
from jax.sharding import PartitionSpec as P

QUERY_HEADS = 24
KEY_VALUE_HEADS = 8
HEAD_DIM = 64
FF = 512
CAP = 68
ROWS = 72


epsilon = 1e-06
theta = 10000.0
BLOCK = 256
GROUP = QUERY_HEADS // KEY_VALUE_HEADS
QUERY_LOCAL = QUERY_HEADS // 4
KEY_LOCAL = KEY_VALUE_HEADS // 4
FACTOR = HEAD_DIM**-0.5
SCALE = FACTOR * 1.4426950408889634
highest = lax.Precision.HIGHEST
f32 = jnp.float32
bf16 = jnp.bfloat16


def dot(a, b, ca, cb, precision=None):
    return lax.dot_general(
        a, b, (((ca,), (cb,)), ((), ())), preferred_element_type=f32, precision=precision
    )


def norm_rows(values, gain_row):
    inv_rms = lax.rsqrt(jnp.mean(values * values, axis=-1, keepdims=True) + epsilon)
    return (values * inv_rms * gain_row, inv_rms)


def norm_back(values, inv_rms, gain_row, upstream):
    scaled = upstream * gain_row
    inner_sum = jnp.mean(scaled * values, axis=-1, keepdims=True)
    return inv_rms * scaled - values * (inv_rms * inv_rms * inv_rms) * inner_sum


def rotary_tables(sequence_length, head_width):
    half_width = head_width // 2
    freqs = theta ** (-(jnp.arange(half_width).astype(jnp.float32) * 2.0 / head_width))
    angles = freqs[:, None] * jnp.arange(sequence_length).astype(jnp.float32)[None, :]
    return (jnp.cos(angles), jnp.sin(angles))


def split_two(values):
    high = lax.reduce_precision(values, 8, 7)
    return high, values - high


def shift_tensor(values, step):
    return lax.ppermute(values, "tensor", [(i, (i + step) % 4) for i in range(4)])


def gather_tensor(mine, place):
    rows, width = mine.shape
    half = rows // 2
    left = shift_tensor(mine, 1)
    right = shift_tensor(mine, -1)
    far_top = shift_tensor(left[:half], 1)
    far_low = shift_tensor(right[half:], -1)
    whole = jnp.zeros((4 * rows, width), mine.dtype)
    for piece, owner, offset in (
        (mine, 0, 0),
        (left, 3, 0),
        (right, 1, 0),
        (far_top, 2, 0),
        (far_low, 2, half),
    ):
        start = lax.rem(place + owner, 4) * rows + offset
        whole = lax.dynamic_update_slice(whole, piece, (start, jnp.int32(0)))
    return whole


def scatter_tensor(chunk):
    far = chunk(2).astype(bf16)
    half = far.shape[0] // 2
    from_left = shift_tensor(far[:half], 1)
    from_right = shift_tensor(far[half:], -1)
    near_right = chunk(1)
    near_left = chunk(3)
    near_right = jnp.concatenate([near_right[:half] + from_left, near_right[half:]], axis=0)
    near_left = jnp.concatenate([near_left[:half], near_left[half:] + from_right], axis=0)
    one = shift_tensor(near_right.astype(bf16), 1)
    two = shift_tensor(near_left.astype(bf16), -1)
    return chunk(0) + one + two


def exchange(values):
    return lax.all_to_all(values, "dp", split_axis=0, concat_axis=0, tiled=True)


def turn(values, cos, sin):
    half = values.shape[0] // 2
    low, high = values[:half], values[half:]
    return jnp.concatenate([low * cos - high * sin, high * cos + low * sin], axis=0)


def diagonal_mask():
    key = lax.broadcasted_iota(jnp.int32, (BLOCK, BLOCK), 0)
    query = lax.broadcasted_iota(jnp.int32, (BLOCK, BLOCK), 1)
    return key <= query


def attend_kernel(q_ref, k_ref, v_ref, cos_ref, sin_ref, out_ref, total_ref, turned_ref, key_s):
    group, member = pl.program_id(0), pl.program_id(1)
    cos, sin = cos_ref[...], sin_ref[...]

    @pl.when(member == 0)
    def _():
        keys = turn(k_ref[...], cos, sin)
        key_s[...] = keys.T.astype(bf16)
        first = pl.multiple_of((QUERY_LOCAL + group) * HEAD_DIM, HEAD_DIM)
        turned_ref[pl.ds(first, HEAD_DIM), :] = keys.astype(bf16)
        second = pl.multiple_of((QUERY_LOCAL + KEY_LOCAL + group) * HEAD_DIM, HEAD_DIM)
        turned_ref[pl.ds(second, HEAD_DIM), :] = v_ref[...].astype(bf16)

    queries = turn(q_ref[...], cos, sin).astype(bf16)
    values = v_ref[...].astype(bf16)
    head = pl.multiple_of((group * GROUP + member) * HEAD_DIM, HEAD_DIM)
    turned_ref[pl.ds(head, HEAD_DIM), :] = queries
    causal = diagonal_mask()
    for j in range(queries.shape[1] // BLOCK):
        columns = slice(j * BLOCK, (j + 1) * BLOCK)
        query = queries[:, columns]
        tiles = []
        top = None
        for i in range(j + 1):
            tile = dot(key_s[i * BLOCK : (i + 1) * BLOCK, :], query, 1, 0) * SCALE
            if i == j:
                tile = jnp.where(causal, tile, -1e30)
            tiles.append(tile)
            peak = jnp.max(tile, axis=0, keepdims=True)
            top = peak if top is None else jnp.maximum(top, peak)
        total = jnp.zeros_like(top)
        summed = jnp.zeros((HEAD_DIM, BLOCK), f32)
        for i in range(j + 1):
            tile = jnp.exp2(tiles[i] - top)
            total = total + jnp.sum(tile, axis=0, keepdims=True)
            summed = summed + dot(values[:, i * BLOCK : (i + 1) * BLOCK], tile.astype(bf16), 1, 0)
        out_ref[pl.ds(head, HEAD_DIM), columns] = (summed / total).astype(bf16)
        total_ref[0, :, columns] = top + jnp.log2(total)


def attend_back_kernel(
    q_ref, k_ref, v_ref, out_ref, grad_ref, total_ref, cos_ref, sin_ref, back_ref, key_s, val_s, gk_s, gv_s
):
    group, member = pl.program_id(0), pl.program_id(1)
    cos, sin = cos_ref[...], sin_ref[...]

    @pl.when(member == 0)
    def _():
        key_s[...] = k_ref[...].astype(f32).T.astype(bf16)
        val_s[...] = v_ref[...].astype(f32).T.astype(bf16)
        gk_s[...] = jnp.zeros_like(gk_s)
        gv_s[...] = jnp.zeros_like(gv_s)

    queries, grads, keys = q_ref[...], grad_ref[...], k_ref[...]
    inner = jnp.sum(out_ref[...].astype(f32) * grads.astype(f32), axis=0, keepdims=True)
    totals = total_ref[0]
    causal = diagonal_mask()
    pieces = []
    for j in range(queries.shape[1] // BLOCK):
        columns = slice(j * BLOCK, (j + 1) * BLOCK)
        query, grad = queries[:, columns], grads[:, columns]
        query_grad = jnp.zeros((HEAD_DIM, BLOCK), f32)
        for i in range(j + 1):
            rows = slice(i * BLOCK, (i + 1) * BLOCK)
            probs = jnp.exp2(dot(key_s[rows, :], query, 1, 0) * SCALE - totals[:, columns])
            if i == j:
                probs = jnp.where(causal, probs, 0.0)
            gv_s[rows, :] += dot(probs.astype(bf16), grad, 1, 1)
            grad_probs = dot(val_s[rows, :], grad, 1, 0)
            grad_scores = (probs * (grad_probs - inner[:, columns])).astype(bf16)
            query_grad = query_grad + dot(keys[:, rows], grad_scores, 1, 0)
            gk_s[rows, :] += dot(grad_scores, query, 1, 1)
        pieces.append(query_grad * FACTOR)
    head = pl.multiple_of((group * GROUP + member) * HEAD_DIM, HEAD_DIM)
    query_back = turn(jnp.concatenate(pieces, axis=1), cos, -sin)
    back_ref[pl.ds(head, HEAD_DIM), :] = query_back.astype(bf16)

    @pl.when(member == GROUP - 1)
    def _():
        first = pl.multiple_of((QUERY_LOCAL + group) * HEAD_DIM, HEAD_DIM)
        back_ref[pl.ds(first, HEAD_DIM), :] = turn(gk_s[...].T * FACTOR, cos, -sin).astype(bf16)
        second = pl.multiple_of((QUERY_LOCAL + KEY_LOCAL + group) * HEAD_DIM, HEAD_DIM)
        back_ref[pl.ds(second, HEAD_DIM), :] = gv_s[...].T.astype(bf16)


def head_block(first, per_group, tokens):
    if per_group:
        return pl.BlockSpec((HEAD_DIM, tokens), lambda g, m: (first + g * per_group + m, 0))
    return pl.BlockSpec((HEAD_DIM, tokens), lambda g, m: (first + g, 0))


def whole_block(shape):
    return pl.BlockSpec(shape, lambda g, m: (0,) * len(shape))


def attend(projected, cos, sin):
    width, tokens = projected.shape
    total_block = pl.BlockSpec((1, 1, tokens), lambda g, m: (g * GROUP + m, 0, 0))
    return pl.pallas_call(
        attend_kernel,
        grid=(KEY_LOCAL, GROUP),
        in_specs=[
            head_block(0, GROUP, tokens),
            head_block(QUERY_LOCAL, 0, tokens),
            head_block(QUERY_LOCAL + KEY_LOCAL, 0, tokens),
            whole_block(cos.shape),
            whole_block(sin.shape),
        ],
        out_specs=(
            whole_block((QUERY_LOCAL * HEAD_DIM, tokens)),
            total_block,
            whole_block((width, tokens)),
        ),
        out_shape=(
            jax.ShapeDtypeStruct((QUERY_LOCAL * HEAD_DIM, tokens), bf16),
            jax.ShapeDtypeStruct((QUERY_LOCAL, 1, tokens), f32),
            jax.ShapeDtypeStruct((width, tokens), bf16),
        ),
        scratch_shapes=[pltpu.VMEM((tokens, HEAD_DIM), bf16)],
        compiler_params=pltpu.CompilerParams(vmem_limit_bytes=40 * 2**20),
        cost_estimate=pl.CostEstimate(
            flops=QUERY_LOCAL * tokens * tokens * HEAD_DIM * 3,
            bytes_accessed=6 * width * tokens,
            transcendentals=QUERY_LOCAL * tokens * tokens,
        ),
        name="attend",
    )(projected, projected, projected, cos, sin)


def attend_back(turned, out, grad, totals, cos, sin):
    width, tokens = turned.shape
    total_block = pl.BlockSpec((1, 1, tokens), lambda g, m: (g * GROUP + m, 0, 0))
    return pl.pallas_call(
        attend_back_kernel,
        grid=(KEY_LOCAL, GROUP),
        in_specs=[
            head_block(0, GROUP, tokens),
            head_block(QUERY_LOCAL, 0, tokens),
            head_block(QUERY_LOCAL + KEY_LOCAL, 0, tokens),
            head_block(0, GROUP, tokens),
            head_block(0, GROUP, tokens),
            total_block,
            whole_block(cos.shape),
            whole_block(sin.shape),
        ],
        out_specs=whole_block((width, tokens)),
        out_shape=jax.ShapeDtypeStruct((width, tokens), bf16),
        scratch_shapes=[
            pltpu.VMEM((tokens, HEAD_DIM), bf16),
            pltpu.VMEM((tokens, HEAD_DIM), bf16),
            pltpu.VMEM((tokens, HEAD_DIM), f32),
            pltpu.VMEM((tokens, HEAD_DIM), f32),
        ],
        compiler_params=pltpu.CompilerParams(vmem_limit_bytes=40 * 2**20),
        cost_estimate=pl.CostEstimate(
            flops=QUERY_LOCAL * tokens * tokens * HEAD_DIM * 7,
            bytes_accessed=6 * width * tokens,
            transcendentals=QUERY_LOCAL * tokens * tokens,
        ),
        name="attend_back",
    )(turned, turned, turned, out, grad, totals, cos, sin)


def per_device(
    tokens,
    norm_gains,
    query_matrix,
    key_value_weight,
    output_weight,
    router,
    expert_up,
    expert_down,
    routes,
    cotangent,
):
    local_rows, model_width = tokens.shape
    query_width = query_matrix.shape[1]
    keyval_width = key_value_weight.shape[2]
    experts_all = router.shape[0]
    place = lax.axis_index("tensor")
    group = lax.axis_index("dp")

    expert_index = jnp.arange(experts_all, dtype=jnp.int32)
    picked = jnp.any(routes[:, :, None] == expert_index[None, None, :], axis=1)
    token_index = jnp.arange(local_rows, dtype=jnp.int32)
    before = (token_index[:, None] > token_index[None, :]).astype(bf16)
    rank = dot(before, picked.astype(bf16), 1, 0)
    slot = jnp.where(picked, rank, -1.0)
    slot_turned = slot.T
    slot_index = jnp.arange(ROWS, dtype=jnp.int32).astype(f32)
    sending = slot_turned[:, None, :] == slot_index[None, :, None]
    send_matrix = sending.astype(bf16).reshape(experts_all * ROWS, local_rows)

    cot_send = dot(send_matrix, cotangent, 1, 0).astype(bf16)
    cot_rows = exchange(cot_send.reshape(experts_all, ROWS, model_width))
    cot_rows = cot_rows.reshape(experts_all * ROWS, model_width)

    inputs = tokens.astype(jnp.float32)
    normed, inv_rms_one = norm_rows(inputs, norm_gains[0])
    sequence = gather_tensor(normed.astype(jnp.bfloat16), place)
    sequence_length = sequence.shape[0]
    joined_weight = jnp.concatenate(
        [query_matrix, key_value_weight.reshape(model_width, 2 * keyval_width)], axis=1
    )
    weight_turned = joined_weight.T
    cos, sin = rotary_tables(sequence_length, HEAD_DIM)
    projected = dot(weight_turned, sequence, 1, 1)
    attended, log_totals, turned = attend(projected, cos, sin)

    def output_chunk(k):
        start = lax.rem(place + k, 4) * local_rows
        return dot(lax.dynamic_slice_in_dim(attended, start, local_rows, 1), output_weight, 0, 0)

    middle = inputs + scatter_tensor(output_chunk)
    mixed_norm, inv_rms_two = norm_rows(middle, norm_gains[1])
    mixed_low = mixed_norm.astype(jnp.bfloat16)
    logits = dot(mixed_low, router, 1, 1)
    chosen = jnp.where(picked, logits, -jnp.inf)
    chosen_exp = jnp.exp(chosen - jnp.max(chosen, axis=1, keepdims=True))
    gates = chosen_exp / jnp.sum(chosen_exp, axis=1, keepdims=True)

    spare = jnp.arange(ROWS, dtype=jnp.int32)[None, :, None]

    def with_spare(rows, slot_values):
        high, low = split_two(slot_values)
        wide = ((0, 0), (0, model_width - ROWS))
        high = jnp.pad(high, wide)[:, None, :]
        low = jnp.pad(low, wide)[:, None, :]
        rows = jnp.where(spare == CAP, high, rows)
        return jnp.where(spare == CAP + 1, low, rows).astype(bf16)

    def from_spare(rows):
        return rows[:, CAP, :ROWS].astype(f32) + rows[:, CAP + 1, :ROWS].astype(f32)

    gates_slot = jnp.sum(jnp.where(sending, gates.T[:, None, :], 0.0), axis=2)
    mixed_send = dot(send_matrix, mixed_low, 1, 0).reshape(experts_all, ROWS, model_width)
    mixed_send, cot_rows = lax.optimization_barrier(
        (with_spare(mixed_send, gates_slot), cot_rows)
    )
    received = exchange(mixed_send)
    gate_column = from_spare(received).reshape(experts_all * ROWS, 1)
    rows_in = received.reshape(experts_all * ROWS, model_width)

    up_matrix, down_matrix = expert_up[0], expert_down[0]
    grad_hidden_one = dot(cot_rows, down_matrix, 1, 1)
    gate_up = dot(rows_in, up_matrix, 1, 0)
    gate_part = gate_up[:, :FF]
    up_part = gate_up[:, FF:]
    sigmoid_gate = jax.nn.sigmoid(gate_part)
    hidden = gate_part * sigmoid_gate * up_part
    hidden_gated = (gate_column * hidden).astype(bf16)
    grad_gate_slot = jnp.sum(hidden * grad_hidden_one, axis=1).reshape(experts_all, ROWS)
    grad_hidden = grad_hidden_one * gate_column
    grad_gate_part = grad_hidden * up_part * sigmoid_gate * (1.0 + gate_part * (1.0 - sigmoid_gate))
    grad_up_part = grad_hidden * gate_part * sigmoid_gate
    grad_gate_up = jnp.concatenate([grad_gate_part, grad_up_part], axis=-1).astype(jnp.bfloat16)
    grad_rows = dot(grad_gate_up, up_matrix, 1, 1).reshape(experts_all, ROWS, model_width)
    grad_back = exchange(with_spare(grad_rows, grad_gate_slot))

    expert_result = dot(hidden_gated, down_matrix, 1, 0).astype(bf16)
    result_back = exchange(expert_result.reshape(experts_all, ROWS, model_width))
    up_grad = dot(rows_in, grad_gate_up, 0, 0).astype(bf16)
    down_grad = dot(cot_rows, hidden_gated, 0, 0).astype(bf16)
    expert_up_grad = lax.psum_scatter(up_grad, "tensor", scatter_dimension=0, tiled=True)
    expert_down_grad = lax.psum_scatter(down_grad, "tensor", scatter_dimension=0, tiled=True)
    expert_up_grad = expert_up_grad.astype(f32)[None]
    expert_down_grad = expert_down_grad.astype(f32).T[None]

    grad_gate = jnp.sum(jnp.where(sending, from_spare(grad_back)[:, :, None], 0.0), axis=1).T
    grad_logits = gates * (grad_gate - jnp.sum(gates * grad_gate, axis=1, keepdims=True))
    grad_mixed = dot(send_matrix, grad_back.reshape(experts_all * ROWS, model_width), 0, 0)
    grad_mixed = grad_mixed + dot(grad_logits, router.astype(f32), 1, 0, highest)
    router_part = dot(mixed_low.astype(f32), grad_logits, 0, 0, highest)
    grad_out = cotangent.astype(jnp.float32)
    grad_middle = grad_out + norm_back(middle, inv_rms_two, norm_gains[1], grad_mixed)
    gain_two_part = jnp.sum(grad_mixed * middle * inv_rms_two, axis=0)

    grad_attn_seq = gather_tensor(grad_middle.astype(jnp.bfloat16), place)
    output_grad_turned = dot(grad_attn_seq, attended, 0, 1)
    router_high, router_low = split_two(router_part)
    gain_high, gain_low = split_two(gain_two_part)
    output_joined = jnp.concatenate(
        [
            output_grad_turned.astype(bf16),
            router_high.astype(bf16),
            router_low.astype(bf16),
            gain_high.astype(bf16)[:, None],
            gain_low.astype(bf16)[:, None],
            jnp.zeros((model_width, 62), bf16),
        ],
        axis=1,
    )
    dp_size = 32
    dp_rows = model_width // dp_size
    output_all = jnp.sum(
        exchange(output_joined.reshape(dp_size, dp_rows, query_width + 128)).astype(f32), axis=0
    )
    output_weight_grad = output_all[:, :query_width].T

    grad_attended = dot(output_weight, grad_attn_seq, 1, 1).astype(bf16)
    grad_projected = attend_back(turned, attended, grad_attended, log_totals, cos, sin)
    joined_grad = dot(sequence, grad_projected, 0, 1).astype(bf16)
    joined_all = jnp.sum(
        exchange(joined_grad.reshape(dp_size, dp_rows, query_width + 2 * keyval_width)).astype(f32),
        axis=0,
    )
    query_weight_grad = joined_all[:, :query_width]
    keyval_weight_grad = joined_all[:, query_width:].reshape(dp_rows, 2, keyval_width)

    def normed_chunk(k):
        start = lax.rem(place + k, 4) * local_rows
        piece = lax.dynamic_slice_in_dim(grad_projected, start, local_rows, 1)
        return dot(piece, weight_turned, 0, 0)

    grad_normed = scatter_tensor(normed_chunk)
    tokens_grad = grad_middle + norm_back(inputs, inv_rms_one, norm_gains[0], grad_normed)

    weight_rows = lax.dynamic_slice_in_dim(joined_weight, group * dp_rows, dp_rows, 0)
    gain_rows = lax.dynamic_slice_in_dim(norm_gains[0], group * dp_rows, dp_rows, 0)
    gain_one_part = jnp.sum(weight_rows.astype(f32) * joined_all, axis=1) / gain_rows
    base = query_width
    small = jnp.concatenate(
        [
            output_all[:, base : base + 32] + output_all[:, base + 32 : base + 64],
            gain_one_part[:, None],
            (output_all[:, base + 64] + output_all[:, base + 65])[:, None],
            jnp.zeros((dp_rows, 94), f32),
        ],
        axis=1,
    ).reshape(4, dp_rows // 4, 128)
    small = jnp.pad(small, ((0, 0), (0, 4), (0, 0)))
    small = lax.all_to_all(small, "tensor", split_axis=0, concat_axis=0, tiled=True)
    small = jnp.sum(small, axis=0)[: dp_rows // 4].T
    router_grad = small[:experts_all]
    gains_grad = small[experts_all : experts_all + 2]

    moe_sum = dot(send_matrix, result_back.reshape(experts_all * ROWS, model_width), 0, 0)
    layer_out = (middle + moe_sum).astype(jnp.bfloat16)
    return (
        layer_out,
        tokens_grad,
        gains_grad,
        query_weight_grad,
        keyval_weight_grad,
        output_weight_grad,
        router_grad,
        expert_up_grad,
        expert_down_grad,
    )


def solution(mesh):
    placed = (
        P(("dp", "tensor"), None),
        P(),
        P(None, "tensor"),
        P(None, None, "tensor"),
        P("tensor", None),
        P(),
        P("dp", None, None),
        P("dp", None, None),
        P(("dp", "tensor"), None),
        P(("dp", "tensor"), None),
    )
    return jax.shard_map(
        per_device,
        mesh=mesh,
        in_specs=placed,
        out_specs=(
            P(("dp", "tensor"), None),
            P(("dp", "tensor"), None),
            P(None, ("dp", "tensor")),
            P("dp", "tensor"),
            P("dp", None, "tensor"),
            P("tensor", "dp"),
            P(None, ("dp", "tensor")),
            P("dp", "tensor", None),
            P("dp", None, "tensor"),
        ),
        check_vma=False,
    )
```

```python
import jax
import jax.numpy as jnp
from jax import lax
from jax.experimental import pallas as pl
from jax.experimental.pallas import tpu as pltpu
from jax.sharding import PartitionSpec as P

QUERY_HEADS = 24
KEY_VALUE_HEADS = 8
HEAD_DIM = 64
FF = 512
CAP = 68
ROWS = 72
PAIR = 2 * ROWS
LINE = 4 * PAIR
HALF = 768
EXTRA = 128


epsilon = 1e-06
theta = 10000.0
BLOCK = 256
GROUP = QUERY_HEADS // KEY_VALUE_HEADS
QUERY_LOCAL = QUERY_HEADS // 4
KEY_LOCAL = KEY_VALUE_HEADS // 4
FACTOR = HEAD_DIM**-0.5
SCALE = FACTOR * 1.4426950408889634
highest = lax.Precision.HIGHEST
BRIEF = pl.CostEstimate(flops=1, bytes_accessed=1, transcendentals=0)
LONG = pl.CostEstimate(flops=10**11, bytes_accessed=1, transcendentals=0)
VMEM_LIMIT = 56 * 2**20
f32 = jnp.float32
bf16 = jnp.bfloat16


def dot(a, b, ca, cb, precision=None):
    return lax.dot_general(
        a, b, (((ca,), (cb,)), ((), ())), preferred_element_type=f32, precision=precision
    )


def inverse_rms(values):
    return lax.rsqrt(jnp.mean(values * values, axis=-1, keepdims=True) + epsilon)


def norm_rows(values, gain_row):
    inv_rms = inverse_rms(values)
    return (values * inv_rms * gain_row, inv_rms)


def norm_back(values, inv_rms, gain_row, upstream):
    scaled = upstream * gain_row
    inner_sum = jnp.mean(scaled * values, axis=-1, keepdims=True)
    return inv_rms * scaled - values * (inv_rms * inv_rms * inv_rms) * inner_sum


def rotary_tables(sequence_length, head_width):
    half_width = head_width // 2
    freqs = theta ** (-(jnp.arange(half_width).astype(jnp.float32) * 2.0 / head_width))
    angles = freqs[:, None] * jnp.arange(sequence_length).astype(jnp.float32)[None, :]
    return (jnp.cos(angles), jnp.sin(angles))


def split_two(values):
    high = lax.reduce_precision(values, 8, 7)
    return high, values - high


def shift_tensor(values, step):
    return lax.ppermute(values, "tensor", [(i, (i + step) % 4) for i in range(4)])


def gather_near(mine, halves):
    if not halves:
        return shift_tensor(mine, 1), shift_tensor(mine, -1)
    half = mine.shape[0] // 2
    top, low = mine[:half], mine[half:]
    left_top, right_low = shift_tensor(top, 1), shift_tensor(low, -1)
    return left_top, right_low, shift_tensor(low, 1), shift_tensor(top, -1)


def gather_far(mine, near, place):
    rows = mine.shape[0]
    half = rows // 2
    if len(near) == 2:
        left, right = near
        far = shift_tensor(left[:half], 1), shift_tensor(right[half:], -1)
        pieces = [(mine, 0, 0), (left, 3, 0), (right, 1, 0)]
    else:
        far = shift_tensor(near[0], 1), shift_tensor(near[1], -1)
        pieces = [(mine, 0, 0), (near[0], 3, 0), (near[2], 3, half)]
        pieces += [(near[3], 1, 0), (near[1], 1, half)]
    pieces += [(far[0], 2, 0), (far[1], 2, half)]
    return [
        (piece, lax.rem(place + owner, 4) * rows + offset) for piece, owner, offset in pieces
    ]


def scatter_far(chunk):
    far = chunk(2).astype(bf16)
    half = far.shape[0] // 2
    return shift_tensor(far[:half], 1), shift_tensor(far[half:], -1)


def scatter_plain(chunk):
    right, left = chunk(1), chunk(3)
    half = right.shape[0] // 2
    return shift_tensor(right[half:].astype(bf16), 1), shift_tensor(left[:half].astype(bf16), -1)


def scatter_summed(chunk, from_left, from_right):
    right, left = chunk(1), chunk(3)
    half = right.shape[0] // 2
    return (
        shift_tensor((right[:half] + from_left.astype(f32)).astype(bf16), 1),
        shift_tensor((left[half:] + from_right.astype(f32)).astype(bf16), -1),
    )


def scatter_near(chunk, from_left, from_right):
    left_low, right_top = scatter_plain(chunk)
    left_top, right_low = scatter_summed(chunk, from_left, from_right)
    return left_top, left_low, right_top, right_low


def scatter_whole(chunk, from_left, from_right):
    right, left = chunk(1), chunk(3)
    half = right.shape[0] // 2
    right = jnp.concatenate([right[:half] + from_left, right[half:]], axis=0).astype(bf16)
    left = jnp.concatenate([left[:half], left[half:] + from_right], axis=0).astype(bf16)
    return shift_tensor(right, 1), shift_tensor(left, -1)


def add_near(mine, near):
    left_top, left_low, right_top, right_low = near
    return mine + jnp.concatenate(
        [left_top.astype(f32) + right_top, left_low.astype(f32) + right_low], axis=0
    )


def exchange_tensor(values):
    parts = values.reshape(4, values.shape[0] // 4, values.shape[1])
    return lax.all_to_all(parts, "tensor", split_axis=0, concat_axis=0, tiled=True)


def add_terms(terms):
    return jnp.sum(terms.astype(f32), axis=0)


def sync(*values):
    return lax.optimization_barrier(values)


def dp_index(y, z, core):
    return (y % 4) * 8 + (z % 4) * 2 + core


def move(values, axes, step, cross):
    pairs = []
    for y in range(4):
        for z in range(4):
            for core in range(2):
                there = (y + step, z) if axes[core] == 0 else (y, z + step)
                pairs.append((dp_index(y, z, core), dp_index(*there, core ^ cross)))
    return lax.ppermute(values, "dp", pairs)


ALONG, ACROSS = (0, 1), (1, 0)


def swap_core(values):
    return move(values, ALONG, 0, 1)


def spread_near(values, extra, core):
    mine = lax.dynamic_slice_in_dim(values, core * HALF, HALF, 1)
    other = lax.dynamic_slice_in_dim(values, (1 - core) * HALF, HALF, 1)
    mine = jnp.concatenate([mine, extra], axis=1)
    other = jnp.concatenate([other, extra], axis=1)
    return mine, other, move(mine, ALONG, 1, 0), move(other, ACROSS, -1, 1), swap_core(other)


def spread_far(mine, other, back_mine, ahead_other, swapped):
    ahead_mine = move(mine, ALONG, -1, 0)
    back_other = move(other, ACROSS, 1, 1)
    far_mine = move(back_mine, ALONG, 1, 0)
    far_other = move(ahead_other, ALONG, -1, 0)
    return [mine, swapped, back_mine, back_other, far_mine, far_other, ahead_mine, ahead_other]


def send_first(chunks):
    middle = [move(chunks[2][0], ACROSS, 1, 0), move(chunks[2][1], ACROSS, -1, 0)]
    return middle, move(chunks[1][0], ACROSS, 1, 0), move(chunks[3][0], ACROSS, -1, 0)


def send_cross(chunks):
    return (
        swap_core(chunks[0][1]),
        move(chunks[1][1], ACROSS, 1, 1),
        move(chunks[3][1], ACROSS, -1, 1),
    )


def send_far(middle):
    return move(middle[0], ACROSS, 1, 0), move(middle[1], ACROSS, -1, 1)


def gather_rows(chunks, first, cross, far):
    _, near, wide = first
    swapped, other_near, other_wide = cross
    return [chunks[0][0], near, far[0], wide], [swapped, other_near, far[1], other_wide]


def send_rest(chunks, middle, near, wide):
    return gather_rows(chunks, (middle, near, wide), send_cross(chunks), send_far(middle))


def return_first(mine, other):
    middle = [move(mine[2], ACROSS, 1, 0), move(other[2], ALONG, -1, 1)]
    return middle, move(mine[1], ACROSS, -1, 0), move(mine[3], ACROSS, 1, 0)


def return_rest(mine, other, middle, near, wide):
    other_near = move(other[1], ALONG, -1, 1)
    other_wide = move(other[3], ALONG, 1, 1)
    far = [move(middle[0], ACROSS, 1, 0), move(middle[1], ACROSS, -1, 0)]
    return [[mine[0], swap_core(other[0])], [near, other_near], far, [wide, other_wide]]


def sum_far(blocks):
    return move(blocks[4], ALONG, 1, 0), move(blocks[5], ALONG, -1, 0)


def sum_near(blocks, passing, core):
    here, back, ahead = blocks[0:2], blocks[2:4], blocks[6:8]
    add = lambda a, b: (a.astype(f32) + b.astype(f32)).astype(bf16)
    far_one, far_two = passing
    mine_two = move(back[0], ALONG, -1, 0)
    other_one = move(ahead[1], ALONG, 1, 1)
    other_here = swap_core(here[1])
    mine_one = move(add(ahead[0], far_one), ALONG, 1, 0)
    other_two = move(add(back[1], far_two), ALONG, -1, 1)
    mine = here[0].astype(f32) + mine_one.astype(f32) + mine_two.astype(f32)
    other = other_here.astype(f32) + other_one.astype(f32) + other_two.astype(f32)
    first = core == 0
    left = jnp.where(first, mine[:, :HALF], other[:, :HALF])
    right = jnp.where(first, other[:, :HALF], mine[:, :HALF])
    return jnp.concatenate([left, right], axis=1), mine[:, HALF:] + other[:, HALF:]


def exchange(values):
    return lax.all_to_all(values, "dp", split_axis=0, concat_axis=0, tiled=True)


def turn(values, cos, sin):
    half = values.shape[0] // 2
    low, high = values[:half], values[half:]
    return jnp.concatenate([low * cos - high * sin, high * cos + low * sin], axis=0)


def diagonal_mask():
    key = lax.broadcasted_iota(jnp.int32, (BLOCK, BLOCK), 0)
    query = lax.broadcasted_iota(jnp.int32, (BLOCK, BLOCK), 1)
    return key <= query


def attend_kernel(
    q_ref, k_ref, v_ref, inverse_ref, cos_ref, sin_ref, out_ref, total_ref, turned_ref, key_s
):
    group, member = pl.program_id(0), pl.program_id(1)
    inverse = inverse_ref[...]
    cos, sin = cos_ref[...] * inverse, sin_ref[...] * inverse

    @pl.when(member == 0)
    def _():
        keys = turn(k_ref[...], cos, sin)
        key_s[...] = keys.T.astype(bf16)
        first = pl.multiple_of((QUERY_LOCAL + group) * HEAD_DIM, HEAD_DIM)
        turned_ref[pl.ds(first, HEAD_DIM), :] = keys.astype(bf16)
        second = pl.multiple_of((QUERY_LOCAL + KEY_LOCAL + group) * HEAD_DIM, HEAD_DIM)
        turned_ref[pl.ds(second, HEAD_DIM), :] = (v_ref[...] * inverse).astype(bf16)

    queries = turn(q_ref[...], cos, sin).astype(bf16)
    values = (v_ref[...] * inverse).astype(bf16)
    head = pl.multiple_of((group * GROUP + member) * HEAD_DIM, HEAD_DIM)
    turned_ref[pl.ds(head, HEAD_DIM), :] = queries
    causal = diagonal_mask()
    for j in range(queries.shape[1] // BLOCK):
        columns = slice(j * BLOCK, (j + 1) * BLOCK)
        query = queries[:, columns]
        tiles = []
        top = None
        for i in range(j + 1):
            tile = dot(key_s[i * BLOCK : (i + 1) * BLOCK, :], query, 1, 0) * SCALE
            if i == j:
                tile = jnp.where(causal, tile, -1e30)
            tiles.append(tile)
            peak = jnp.max(tile, axis=0, keepdims=True)
            top = peak if top is None else jnp.maximum(top, peak)
        total = jnp.zeros_like(top)
        summed = jnp.zeros((HEAD_DIM, BLOCK), f32)
        for i in range(j + 1):
            tile = jnp.exp2(tiles[i] - top)
            total = total + jnp.sum(tile, axis=0, keepdims=True)
            summed = summed + dot(values[:, i * BLOCK : (i + 1) * BLOCK], tile.astype(bf16), 1, 0)
        out_ref[pl.ds(head, HEAD_DIM), columns] = (summed / total).astype(bf16)
        total_ref[0, :, columns] = top + jnp.log2(total)


def attend_back_kernel(*refs):
    q_ref, k_ref, v_ref, out_ref, grad_ref, total_ref, inverse_ref, cos_ref, sin_ref = refs[:9]
    back_ref, scaled_ref, key_s, val_s, gk_s, gv_s = refs[9:]
    inverse = inverse_ref[...]

    def put(row, values):
        row = pl.multiple_of(row * HEAD_DIM, HEAD_DIM)
        back_ref[pl.ds(row, HEAD_DIM), :] = values.astype(bf16)
        scaled_ref[pl.ds(row, HEAD_DIM), :] = (values * inverse).astype(bf16)

    group, member = pl.program_id(0), pl.program_id(1)
    cos, sin = cos_ref[...], sin_ref[...]

    @pl.when(member == 0)
    def _():
        key_s[...] = k_ref[...].astype(f32).T.astype(bf16)
        val_s[...] = v_ref[...].astype(f32).T.astype(bf16)
        gk_s[...] = jnp.zeros_like(gk_s)
        gv_s[...] = jnp.zeros_like(gv_s)

    queries, grads, keys = q_ref[...], grad_ref[...], k_ref[...]
    inner = jnp.sum(out_ref[...].astype(f32) * grads.astype(f32), axis=0, keepdims=True)
    totals = total_ref[0]
    causal = diagonal_mask()
    pieces = []
    for j in range(queries.shape[1] // BLOCK):
        columns = slice(j * BLOCK, (j + 1) * BLOCK)
        query, grad = queries[:, columns], grads[:, columns]
        query_grad = jnp.zeros((HEAD_DIM, BLOCK), f32)
        for i in range(j + 1):
            rows = slice(i * BLOCK, (i + 1) * BLOCK)
            probs = jnp.exp2(dot(key_s[rows, :], query, 1, 0) * SCALE - totals[:, columns])
            if i == j:
                probs = jnp.where(causal, probs, 0.0)
            gv_s[rows, :] += dot(probs.astype(bf16), grad, 1, 1)
            grad_probs = dot(val_s[rows, :], grad, 1, 0)
            grad_scores = (probs * (grad_probs - inner[:, columns])).astype(bf16)
            query_grad = query_grad + dot(keys[:, rows], grad_scores, 1, 0)
            gk_s[rows, :] += dot(grad_scores, query, 1, 1)
        pieces.append(query_grad * FACTOR)
    put(group * GROUP + member, turn(jnp.concatenate(pieces, axis=1), cos, -sin))

    @pl.when(member == GROUP - 1)
    def _():
        put(QUERY_LOCAL + group, turn(gk_s[...].T * FACTOR, cos, -sin))
        put(QUERY_LOCAL + KEY_LOCAL + group, gv_s[...].T)


def head_block(first, per_group, tokens):
    if per_group:
        return pl.BlockSpec((HEAD_DIM, tokens), lambda g, m: (first + g * per_group + m, 0))
    return pl.BlockSpec((HEAD_DIM, tokens), lambda g, m: (first + g, 0))


def whole_block(shape):
    return pl.BlockSpec(shape, lambda g, m: (0,) * len(shape))


def project_kernel(start_ref, *refs):
    pieces, weight_ref = refs[:-4], refs[-4]
    out_ref, sequence_ref, inverse_ref = refs[-3:]
    ones = jnp.ones((8, weight_ref.shape[1]), bf16)
    for i, piece in enumerate(pieces):
        count = piece.shape[0]
        start = pl.multiple_of(start_ref[i], 128)
        rows = piece[...]
        sequence_ref[pl.ds(start, count), :] = rows
        out_ref[:, pl.ds(start, count)] = dot(weight_ref[...], rows, 1, 1)
        wide = rows.astype(f32)
        squares = dot(ones, (wide * wide).astype(bf16), 1, 1)[0:1]
        inverse_ref[:, pl.ds(start, count)] = lax.rsqrt(squares * (1.0 / rows.shape[1]) + epsilon)


def project_back_kernel(start_ref, *refs):
    pieces, weight_ref = refs[:-3], refs[-3]
    out_ref, sequence_ref = refs[-2:]
    for i, piece in enumerate(pieces):
        count = piece.shape[0]
        start = pl.multiple_of(start_ref[i], 128)
        rows = piece[...]
        sequence_ref[pl.ds(start, count), :] = rows
        out_ref[:, pl.ds(start, count)] = dot(weight_ref[...], rows, 1, 1).astype(bf16)


def project(pieces, weight, back):
    tokens = sum(piece.shape[0] for piece, _ in pieces)
    width, depth = weight.shape
    outs = [
        jax.ShapeDtypeStruct((width, tokens), bf16 if back else f32),
        jax.ShapeDtypeStruct((tokens, depth), bf16),
    ]
    if not back:
        outs.append(jax.ShapeDtypeStruct((1, tokens), f32))
    spec = pl.BlockSpec(memory_space=pltpu.VMEM)
    return pl.pallas_call(
        project_back_kernel if back else project_kernel,
        in_specs=[pl.BlockSpec(memory_space=pltpu.SMEM)] + [spec] * (len(pieces) + 1),
        out_specs=[spec] * len(outs),
        out_shape=outs,
        compiler_params=pltpu.CompilerParams(vmem_limit_bytes=20 * 2**20),
        cost_estimate=BRIEF,
        name="project_back" if back else "project",
    )(jnp.stack([start for _, start in pieces]), *[piece for piece, _ in pieces], weight)


def weight_grads_kernel(one_ref, rows_ref, scale_ref, two_ref, other_ref, extra_ref, out_ref):
    one, two = one_ref.shape[0], two_ref.shape[0]
    total = dot(one_ref[...], rows_ref[...], 1, 0) * scale_ref[...]
    out_ref[:, :one] = total.T.astype(bf16)
    total = dot(two_ref[...], other_ref[...], 1, 0)
    out_ref[:, one : one + two] = total.T.astype(bf16)
    out_ref[:, one + two :] = extra_ref[...].T.astype(bf16)


def weight_grads(one, rows, scale, two, other, extra):
    tokens, depth = rows.shape
    block = 256
    width = one.shape[0] + two.shape[0] + extra.shape[0]
    whole = lambda shape: pl.BlockSpec(shape, lambda d: (0, 0))
    return pl.pallas_call(
        weight_grads_kernel,
        grid=(depth // block,),
        in_specs=[
            whole(one.shape),
            pl.BlockSpec((tokens, block), lambda d: (0, d)),
            pl.BlockSpec((1, block), lambda d: (0, d)),
            whole(two.shape),
            pl.BlockSpec((tokens, block), lambda d: (0, d)),
            pl.BlockSpec((extra.shape[0], block), lambda d: (0, d)),
        ],
        out_specs=pl.BlockSpec((block, width), lambda d: (d, 0)),
        out_shape=jax.ShapeDtypeStruct((depth, width), bf16),
        compiler_params=pltpu.CompilerParams(vmem_limit_bytes=30 * 2**20),
        cost_estimate=BRIEF,
        name="weight_grads",
    )(one, rows, scale, two, other, extra)


def expert_sums_kernel(place_ref, mine_ref, left_ref, right_ref, up_ref, down_ref):
    total = mine_ref[...].astype(f32) + left_ref[...].astype(f32) + right_ref[...].astype(f32)
    up_ref[...] = total[:, : 2 * FF]
    down_ref[...] = total[:, 2 * FF :].T


def expert_sums(place, grads, left, right):
    rows, width = left.shape
    whole = lambda shape: pl.BlockSpec(shape, lambda i, at: (0, 0))
    return pl.pallas_call(
        expert_sums_kernel,
        grid_spec=pltpu.PrefetchScalarGridSpec(
            num_scalar_prefetch=1,
            grid=(1,),
            in_specs=[pl.BlockSpec((rows, width), lambda i, at: (at[0], 0))] + [whole((rows, width))] * 2,
            out_specs=[whole((rows, 2 * FF)), whole((FF, rows))],
        ),
        out_shape=[
            jax.ShapeDtypeStruct((rows, 2 * FF), f32),
            jax.ShapeDtypeStruct((FF, rows), f32),
        ],
        compiler_params=pltpu.CompilerParams(vmem_limit_bytes=24 * 2**20),
        cost_estimate=BRIEF,
        name="expert_sums",
    )(place, grads, left, right)


def attend(projected, inverse, cos, sin):
    width, tokens = projected.shape
    total_block = pl.BlockSpec((1, 1, tokens), lambda g, m: (g * GROUP + m, 0, 0))
    return pl.pallas_call(
        attend_kernel,
        grid=(KEY_LOCAL, GROUP),
        in_specs=[
            head_block(0, GROUP, tokens),
            head_block(QUERY_LOCAL, 0, tokens),
            head_block(QUERY_LOCAL + KEY_LOCAL, 0, tokens),
            whole_block(inverse.shape),
            whole_block(cos.shape),
            whole_block(sin.shape),
        ],
        out_specs=(
            whole_block((QUERY_LOCAL * HEAD_DIM, tokens)),
            total_block,
            whole_block((width, tokens)),
        ),
        out_shape=(
            jax.ShapeDtypeStruct((QUERY_LOCAL * HEAD_DIM, tokens), bf16),
            jax.ShapeDtypeStruct((QUERY_LOCAL, 1, tokens), f32),
            jax.ShapeDtypeStruct((width, tokens), bf16),
        ),
        scratch_shapes=[pltpu.VMEM((tokens, HEAD_DIM), bf16)],
        compiler_params=pltpu.CompilerParams(vmem_limit_bytes=20 * 2**20),
        cost_estimate=BRIEF,
        name="attend",
    )(projected, projected, projected, inverse, cos, sin)


def attend_back(turned, out, grad, totals, inverse, cos, sin):
    width, tokens = turned.shape
    total_block = pl.BlockSpec((1, 1, tokens), lambda g, m: (g * GROUP + m, 0, 0))
    return pl.pallas_call(
        attend_back_kernel,
        grid=(KEY_LOCAL, GROUP),
        in_specs=[
            head_block(0, GROUP, tokens),
            head_block(QUERY_LOCAL, 0, tokens),
            head_block(QUERY_LOCAL + KEY_LOCAL, 0, tokens),
            head_block(0, GROUP, tokens),
            head_block(0, GROUP, tokens),
            total_block,
            whole_block(inverse.shape),
            whole_block(cos.shape),
            whole_block(sin.shape),
        ],
        out_specs=[whole_block((width, tokens))] * 2,
        out_shape=[jax.ShapeDtypeStruct((width, tokens), bf16)] * 2,
        scratch_shapes=[
            pltpu.VMEM((tokens, HEAD_DIM), bf16),
            pltpu.VMEM((tokens, HEAD_DIM), bf16),
            pltpu.VMEM((tokens, HEAD_DIM), f32),
            pltpu.VMEM((tokens, HEAD_DIM), f32),
        ],
        compiler_params=pltpu.CompilerParams(vmem_limit_bytes=20 * 2**20),
        cost_estimate=LONG,
        name="attend_back",
    )(turned, turned, turned, out, grad, totals, inverse, cos, sin)


def build_kernel(*refs):
    tokens, (expand_ref, pick_ref, core_ref) = refs[:8], refs[8:11]
    outs, token_s = refs[11:19], refs[19]
    step = pl.program_id(0)
    for r in range(4):

        @pl.when(step == r)
        def _(r=r):
            token_s[0] = tokens[2 * r][...]
            token_s[1] = tokens[2 * r + 1][...]

    count = tokens[0].shape[0]
    index = lax.broadcasted_iota(jnp.int32, (ROWS, count), 0).astype(f32)
    below = lax.broadcasted_iota(jnp.int32, (8, 128), 0)
    across = lax.broadcasted_iota(jnp.int32, (8, 128), 1)
    pieces = []
    for s in (core_ref[0], 1 - core_ref[0]):
        slots = dot(expand_ref[...], token_s[s, :, HALF:], 1, 1)
        hot = jnp.concatenate(
            [
                jnp.where(slots[k * ROWS : (k + 1) * ROWS] == index, 1.0, 0.0)
                for k in range(8)
            ],
            axis=0,
        ).astype(bf16)
        rows = dot(hot, token_s[s, :, :HALF], 1, 0)
        parts = [rows[k * ROWS : (k + 1) * ROWS] for k in range(8)]
        gates = dot(pick_ref[...], token_s[s, :, HALF:], 1, 1).astype(bf16)
        for d in range(4):
            values = dot(gates, hot[d * PAIR : d * PAIR + 128], 1, 1)
            high, low = values[2 * d : 2 * d + 1], values[2 * d + 1 : 2 * d + 2]
            spare = jnp.where(below == 4, high, jnp.where(below == 5, low, 0.0))
            spare = jnp.where(across < ROWS, spare, 0.0)
            part = parts[2 * d]
            last = jnp.concatenate([part[64:, :128] + spare, part[64:, 128:]], axis=1)
            parts[2 * d] = jnp.concatenate([part[:64], last], axis=0)
        pieces.append(parts)
    for k in range(8):
        outs[k][0] = jnp.concatenate([pieces[0][k], pieces[1][k]], axis=0).astype(bf16)


def build(core, blocks, expand, pick, cost):
    count, width = blocks[0].shape
    whole = lambda shape: pl.BlockSpec(shape, lambda r: (0,) * len(shape))
    outs = pl.pallas_call(
        build_kernel,
        grid=(4,),
        in_specs=[whole((count, width))] * 8
        + [whole(expand.shape), whole(pick.shape), pl.BlockSpec(memory_space=pltpu.SMEM)],
        out_specs=[pl.BlockSpec((1, PAIR, HALF), lambda r: (r, 0, 0))] * 8,
        out_shape=[jax.ShapeDtypeStruct((4, PAIR, HALF), bf16)] * 8,
        scratch_shapes=[pltpu.VMEM((2, count, width), bf16)],
        compiler_params=pltpu.CompilerParams(vmem_limit_bytes=VMEM_LIMIT),
        cost_estimate=cost,
        name="build_rows",
    )(*blocks, expand, pick, core)
    return [[outs[2 * d], outs[2 * d + 1]] for d in range(4)]


def combine_kernel(gated, refs):
    given, slots, (expand_ref, aim_ref, pick_ref, core_ref) = refs[:8], refs[8:16], refs[16:20]
    outs, total_s, slot_s = refs[20:28], refs[28], refs[29]
    core = core_ref[0]
    step = pl.program_id(0)
    for r in range(4):

        @pl.when(step == r)
        def _(r=r):
            slot_s[0] = slots[2 * r][...]
            slot_s[1] = slots[2 * r + 1][...]

    rows = jnp.concatenate([ref[0] for ref in given], axis=0)
    if gated:
        own = lax.broadcasted_iota(jnp.int32, (ROWS, 128), 0)
        own = own == lax.broadcasted_iota(jnp.int32, (ROWS, 128), 1)
        columns = []
        for d in range(4):
            head = given[2 * d][0, :, :128].astype(f32)
            for s in range(2):
                at = s * ROWS + CAP
                high = jnp.sum(jnp.where(own, head[at : at + 1], 0.0), axis=1, keepdims=True)
                low = jnp.sum(jnp.where(own, head[at + 1 : at + 2], 0.0), axis=1, keepdims=True)
                columns.append(
                    high * pick_ref[2 * d : 2 * d + 1] + low * pick_ref[2 * d + 1 : 2 * d + 2]
                )
            columns.append(jnp.zeros((PAIR, EXTRA), f32))
        rows = jnp.concatenate([rows, jnp.concatenate(columns, axis=0).astype(bf16)], axis=1)
    hots = []
    for s in range(2):
        hot = dot(slot_s[core if s == 0 else 1 - core], expand_ref[...], 1, 0)
        hot = hot == aim_ref[s : s + 1]
        hots.append(jnp.where(hot, 1.0, 0.0).astype(bf16))
    total = dot(jnp.concatenate(hots, axis=0), rows, 1, 0).astype(bf16)
    count = slot_s.shape[1]
    total_s[0] = total[:count]
    total_s[1] = total[count:]
    for r in range(4):

        @pl.when(step == r)
        def _(r=r):
            outs[2 * r][...] = total_s[core]
            outs[2 * r + 1][...] = total_s[1 - core]


def combine(core, chunks, blocks, expand, aim, pick, gated):
    count = blocks[0].shape[0]
    width = HALF + (EXTRA if gated else 0)
    whole = lambda shape: pl.BlockSpec(shape, lambda r: (0,) * len(shape))
    return pl.pallas_call(
        lambda *refs: combine_kernel(gated, refs),
        grid=(4,),
        in_specs=[pl.BlockSpec((1, PAIR, HALF), lambda r: (r, 0, 0))] * 8
        + [pl.BlockSpec((count, EXTRA), lambda r: (0, HALF // EXTRA))] * 8
        + [
            whole(expand.shape),
            whole(aim.shape),
            whole(pick.shape),
            pl.BlockSpec(memory_space=pltpu.SMEM),
        ],
        out_specs=[whole((count, width))] * 8,
        out_shape=[jax.ShapeDtypeStruct((count, width), bf16)] * 8,
        scratch_shapes=[
            pltpu.VMEM((2, count, width), bf16),
            pltpu.VMEM((2, count, EXTRA), bf16),
        ],
        compiler_params=pltpu.CompilerParams(vmem_limit_bytes=VMEM_LIMIT),
        cost_estimate=LONG if gated else BRIEF,
        name="combine_rows",
    )(*[piece for chunk in chunks for piece in chunk], *blocks, expand, aim, pick, core)


def whole_rows(core_ref, mine, other, mine_s):
    step = pl.program_id(0)
    for d in range(4):

        @pl.when(step == d)
        def _(d=d):
            for r in range(4):
                mine_s[r * PAIR : (r + 1) * PAIR, :] = mine[d][r]

    one = mine_s[...]
    two = jnp.concatenate([ref[0] for ref in other], axis=0)
    first = core_ref[0] == 0
    return one, jnp.concatenate([jnp.where(first, one, two), jnp.where(first, two, one)], axis=1)


def store_halves(core_ref, values, spare, mine, other):
    step = pl.program_id(0)
    first = core_ref[0] == 0
    one = jnp.where(first, values[:, :HALF], values[:, HALF:])
    two = jnp.where(first, values[:, HALF:], values[:, :HALF]).astype(bf16)
    if spare is not None:
        one = jnp.concatenate([one[:, :128] + spare, one[:, 128:]], axis=1)
    one = one.astype(bf16)
    for d in range(4):

        @pl.when(step == d)
        def _(d=d):
            for r in range(4):
                mine[d][r] = one[r * PAIR : (r + 1) * PAIR]

    for r in range(4):
        other[r][0] = two[r * PAIR : (r + 1) * PAIR]


def cotangent_kernel(*refs):
    core_ref, mine, other = refs[0], refs[1:5], refs[5:9]
    down_ref, rows_ref, hidden_ref, mine_s = refs[9:]
    _, rows = whole_rows(core_ref, mine, other, mine_s)
    rows_ref[0] = rows
    hidden_ref[0] = dot(rows, down_ref[...], 1, 1)


def expert_kernel(*refs):
    core_ref, mine, other, up_ref, back_ref = refs[0], refs[1:5], refs[5:9], refs[9], refs[10]
    rows_ref, grad_ref, hidden_ref = refs[11:14]
    mine_out, other_out, mine_s = refs[14:18], refs[18:22], refs[22]
    one, rows = whole_rows(core_ref, mine, other, mine_s)
    rows_ref[0] = rows
    own = lax.broadcasted_iota(jnp.int32, (ROWS, 128), 0)
    own = own == lax.broadcasted_iota(jnp.int32, (ROWS, 128), 1)
    head = one[:, :128].astype(f32)
    gates = []
    for i in range(LINE // ROWS):
        at = i * ROWS + CAP
        line = head[at : at + 1] + head[at + 1 : at + 2]
        gates.append(jnp.sum(jnp.where(own, line, 0.0), axis=1, keepdims=True))
    gate = jnp.concatenate(gates, axis=0)
    inner, total = 0.0, 0.0
    width = FF // 2
    for c in range(2):
        low, high = slice(c * width, (c + 1) * width), slice(FF + c * width, FF + (c + 1) * width)
        gate_part = dot(rows, up_ref[:, low], 1, 0)
        up_part = dot(rows, up_ref[:, high], 1, 0)
        sigmoid = 1.0 / (1.0 + jnp.exp(-gate_part))
        silu = gate_part * sigmoid
        hidden = silu * up_part
        back = back_ref[0, :, low]
        inner = inner + jnp.sum(hidden * back, axis=1, keepdims=True)
        hidden_ref[0, :, low] = (gate * hidden).astype(bf16)
        back = gate * back
        grad_one = (back * up_part * (sigmoid + silu * (1.0 - sigmoid))).astype(bf16)
        grad_two = (back * silu).astype(bf16)
        grad_ref[0, :, low] = grad_one
        grad_ref[0, :, high] = grad_two
        total = total + dot(grad_one, up_ref[:, low], 1, 1) + dot(grad_two, up_ref[:, high], 1, 1)
    below = lax.broadcasted_iota(jnp.int32, (8, 128), 0)
    spares = []
    for i in range(LINE // ROWS):
        line = jnp.where(own, inner[i * ROWS : (i + 1) * ROWS], 0.0)
        line = jnp.sum(line, axis=0, keepdims=True)
        high = line.astype(bf16).astype(f32)
        spare = jnp.where(below == 4, high, jnp.where(below == 5, line - high, 0.0))
        spares += [jnp.zeros((ROWS - 8, 128), f32), spare]
    store_halves(
        core_ref, total, jnp.concatenate(spares, axis=0), mine_out, other_out
    )


def result_kernel(*refs):
    core_ref, hidden_ref, down_ref = refs[:3]
    store_halves(core_ref, dot(hidden_ref[0], down_ref[...], 1, 0), None, refs[3:7], refs[7:11])


def whole_spec(shape):
    return pl.BlockSpec(shape, lambda d: (0,) * len(shape))


def line_spec(rows, width):
    return pl.BlockSpec((1, rows, width), lambda d: (d, 0, 0))


CORE_SPEC = pl.BlockSpec(memory_space=pltpu.SMEM)
EXPERT_PARAMS = dict(compiler_params=pltpu.CompilerParams(vmem_limit_bytes=VMEM_LIMIT))


def cotangent_rows(core, mine, other, down):
    return pl.pallas_call(
        cotangent_kernel,
        grid=(4,),
        in_specs=[CORE_SPEC]
        + [whole_spec((4, PAIR, HALF))] * 4
        + [line_spec(PAIR, HALF)] * 4
        + [whole_spec(down.shape)],
        out_specs=(line_spec(LINE, 2 * HALF), line_spec(LINE, FF)),
        out_shape=(
            jax.ShapeDtypeStruct((4, LINE, 2 * HALF), bf16),
            jax.ShapeDtypeStruct((4, LINE, FF), f32),
        ),
        scratch_shapes=[pltpu.VMEM((LINE, HALF), bf16)],
        cost_estimate=BRIEF,
        name="cotangent_rows",
        compiler_params=pltpu.CompilerParams(vmem_limit_bytes=28 * 2**20),
    )(core, *mine, *other, down)


def expert_rows(core, mine, other, up, back):
    outs = pl.pallas_call(
        expert_kernel,
        grid=(4,),
        in_specs=[CORE_SPEC]
        + [whole_spec((4, PAIR, HALF))] * 4
        + [line_spec(PAIR, HALF)] * 4
        + [whole_spec(up.shape), line_spec(LINE, FF)],
        out_specs=[line_spec(LINE, 2 * HALF), line_spec(LINE, 2 * FF), line_spec(LINE, FF)]
        + [whole_spec((4, PAIR, HALF))] * 4
        + [line_spec(PAIR, HALF)] * 4,
        out_shape=[
            jax.ShapeDtypeStruct((4, LINE, 2 * HALF), bf16),
            jax.ShapeDtypeStruct((4, LINE, 2 * FF), bf16),
            jax.ShapeDtypeStruct((4, LINE, FF), bf16),
        ]
        + [jax.ShapeDtypeStruct((4, PAIR, HALF), bf16)] * 8,
        scratch_shapes=[pltpu.VMEM((LINE, HALF), bf16)],
        cost_estimate=BRIEF,
        name="expert_rows",
        **EXPERT_PARAMS,
    )(core, *mine, *other, up, back)
    return outs[0], outs[1], outs[2], outs[3:7], outs[7:11]


def result_rows(core, hidden, down):
    outs = pl.pallas_call(
        result_kernel,
        grid=(4,),
        in_specs=[CORE_SPEC, line_spec(LINE, FF), whole_spec(down.shape)],
        out_specs=[whole_spec((4, PAIR, HALF))] * 4 + [line_spec(PAIR, HALF)] * 4,
        out_shape=[jax.ShapeDtypeStruct((4, PAIR, HALF), bf16)] * 8,
        cost_estimate=LONG,
        name="result_rows",
        **EXPERT_PARAMS,
    )(core, hidden, down)
    return outs[:4], outs[4:]


def per_device(
    tokens,
    norm_gains,
    query_matrix,
    key_value_weight,
    output_weight,
    router,
    expert_up,
    expert_down,
    routes,
    cotangent,
):
    local_rows, model_width = tokens.shape
    query_width = query_matrix.shape[1]
    keyval_width = key_value_weight.shape[2]
    experts_all = router.shape[0]
    place = lax.axis_index("tensor")
    group = lax.axis_index("dp")

    expert_index = jnp.arange(experts_all, dtype=jnp.int32)
    picked = jnp.any(routes[:, :, None] == expert_index[None, None, :], axis=1)
    token_index = jnp.arange(local_rows, dtype=jnp.int32)
    before = (token_index[:, None] > token_index[None, :]).astype(bf16)
    rank = dot(before, picked.astype(bf16), 1, 0)
    slot = jnp.where(picked, rank, -1.0)
    core = lax.rem(group, 2)
    line_y, line_z = group // 8, lax.rem(group // 2, 4)
    core_scalar = jnp.reshape(core, (1,)).astype(jnp.int32)

    distance = jnp.arange(4, dtype=jnp.int32)
    chip = jnp.where(
        core == 0, line_y * 4 + (line_z + distance) % 4, ((line_y + distance) % 4) * 4 + line_z
    )
    partner = jnp.stack([2 * chip + core, 2 * chip + 1 - core], axis=1).reshape(8)
    lane = jnp.arange(EXTRA, dtype=jnp.int32)
    hit = lane[None, :] == partner[:, None] + 64
    expand = jnp.repeat(hit, ROWS, axis=0).astype(bf16)
    expand_turned = jnp.repeat(hit, PAIR, axis=0).T.astype(bf16)
    near = partner.reshape(4, 2)[:, 0]
    pick = jnp.stack([near, near + 32], axis=1).reshape(8)
    pick = jnp.pad((lane[None, :] == pick[:, None]).astype(bf16), ((0, 8), (0, 0)))
    pick_wide = pick.astype(f32)
    spot = jnp.arange(8 * PAIR, dtype=jnp.int32)
    aim = jnp.stack(
        [
            jnp.where((spot // ROWS) % 2 == s, spot % ROWS, -5 if s < 2 else -6).astype(f32)
            for s in range(8)
        ],
        axis=0,
    )

    def wide(values):
        return jnp.pad(values, ((0, 0), (0, EXTRA - values.shape[1])))

    up_matrix, down_matrix = expert_up[0], expert_down[0]

    inputs = tokens.astype(jnp.float32)
    inv_rms_one = inverse_rms(inputs)
    near = gather_near(tokens, False)
    cot_near = spread_near(
        cotangent, wide(jnp.concatenate([jnp.zeros((local_rows, 64), f32), slot], axis=1).astype(bf16)), core
    )
    sequence_length = 4 * local_rows
    joined_weight = jnp.concatenate(
        [query_matrix, key_value_weight.reshape(model_width, 2 * keyval_width)], axis=1
    )
    weight_turned = joined_weight.T
    gained_turned = (norm_gains[0][:, None] * joined_weight.astype(f32)).astype(bf16).T
    cos, sin = rotary_tables(sequence_length, HEAD_DIM)
    near, cot_near, gained_turned, weight_turned, cos, sin, expand_turned, aim, pick_wide = sync(
        near, cot_near, gained_turned, weight_turned, cos, sin, expand_turned, aim, pick_wide
    )
    pieces = gather_far(tokens, near, place)
    cot_chunks = build(core_scalar, spread_far(*cot_near), expand, pick, LONG)
    pieces, cot_chunks = sync(pieces, cot_chunks)
    cot_first = send_first(cot_chunks)
    projected, sequence, inverse = project(pieces, gained_turned, False)
    attended, log_totals, turned = attend(projected, inverse, cos, sin)
    def output_chunk(k):
        start = lax.rem(place + k, 4) * local_rows
        return dot(lax.dynamic_slice_in_dim(attended, start, local_rows, 1), output_weight, 0, 0)

    attended, cot_first = sync(attended, cot_first)
    far = scatter_far(output_chunk)
    cot_swapped = send_cross(cot_chunks)
    far, cot_swapped = sync(far, cot_swapped)
    near = scatter_whole(output_chunk, *far)
    near, cot_far = sync(near, send_far(cot_first[0]))
    cot_got = gather_rows(cot_chunks, cot_first, cot_swapped, cot_far)
    middle = inputs + output_chunk(0) + near[0].astype(f32) + near[1].astype(f32)
    mixed_norm, inv_rms_two = norm_rows(middle, norm_gains[1])
    mixed_low = mixed_norm.astype(jnp.bfloat16)
    logits = dot(mixed_low, router, 1, 1)
    chosen = jnp.where(picked, logits, -jnp.inf)
    chosen_exp = jnp.exp(chosen - jnp.max(chosen, axis=1, keepdims=True))
    gates = chosen_exp / jnp.sum(chosen_exp, axis=1, keepdims=True)

    gates_high, gates_low = split_two(gates)
    mixed_near = spread_near(
        mixed_low, wide(jnp.concatenate([gates_high, gates_low, slot], axis=1).astype(bf16)), core
    )
    mixed_blocks = spread_far(*mixed_near)
    mixed_chunks = build(core_scalar, mixed_blocks, expand, pick, BRIEF)
    cot_rows, grad_hidden_one = cotangent_rows(core_scalar, *cot_got, down_matrix)
    mixed_first, grad_hidden_one = sync(send_first(mixed_chunks), grad_hidden_one)
    mixed_got = send_rest(mixed_chunks, *mixed_first)
    mixed_got, grad_hidden_one = sync(mixed_got, grad_hidden_one)
    rows_in, grad_gate_up, hidden_gated, grad_mine, grad_other = expert_rows(
        core_scalar, *mixed_got, up_matrix, grad_hidden_one
    )

    rows_in = rows_in.reshape(4 * LINE, model_width)
    cot_rows = cot_rows.reshape(4 * LINE, model_width)
    grad_gate_up = grad_gate_up.reshape(4 * LINE, 2 * FF)
    hidden_flat = hidden_gated.reshape(4 * LINE, FF)
    up_grad = dot(rows_in, grad_gate_up, 0, 0).astype(bf16)
    grad_first, up_grad = sync(return_first(grad_mine, grad_other), up_grad)
    down_grad = dot(cot_rows, hidden_flat, 0, 0).astype(bf16)
    grad_chunks = return_rest(grad_mine, grad_other, *grad_first)
    expert_grads = jnp.concatenate([up_grad, down_grad], axis=1)
    grad_chunks, expert_grads, hidden_gated = sync(grad_chunks, expert_grads, hidden_gated)
    expert_rows_out = model_width // 4

    def expert_chunk(k):
        start = lax.rem(place + k, 4) * expert_rows_out
        return lax.dynamic_slice_in_dim(expert_grads, start, expert_rows_out, 0)

    grad_blocks = combine(core_scalar, grad_chunks, mixed_blocks, expand_turned, aim, pick_wide, True)
    grad_blocks, expert_far, hidden_gated = sync(
        grad_blocks, scatter_far(expert_chunk), hidden_gated
    )
    result_mine, result_other = result_rows(core_scalar, hidden_gated, down_matrix)
    grad_mixed, grad_gate = sum_near(grad_blocks, sum_far(grad_blocks), core)
    grad_mixed, grad_gate, result_mine, result_other = sync(
        grad_mixed, grad_gate, result_mine, result_other
    )
    grad_gate = grad_gate[:, :32] + grad_gate[:, 32:64]

    grad_logits = gates * (grad_gate - jnp.sum(gates * grad_gate, axis=1, keepdims=True))
    grad_mixed = grad_mixed + dot(grad_logits, router.astype(f32), 1, 0, highest)
    router_part = dot(grad_logits, mixed_low.astype(f32), 0, 0, highest)
    grad_out = cotangent.astype(jnp.float32)
    grad_middle = grad_out + norm_back(middle, inv_rms_two, norm_gains[1], grad_mixed)
    gain_two_part = jnp.sum(grad_mixed * middle * inv_rms_two, axis=0)

    grad_low = grad_middle.astype(bf16)
    router_part, result_mine, result_other = sync(router_part, result_mine, result_other)
    near = gather_near(grad_low, False)
    middle_rows = [move(result_mine[2], ACROSS, 1, 0), move(result_other[2], ALONG, -1, 1)]
    back_near = move(result_mine[1], ACROSS, -1, 0)
    near, middle_rows, back_near = sync(near, middle_rows, back_near)
    pieces = gather_far(grad_low, near, place)
    back_wide = move(result_mine[3], ACROSS, 1, 0)
    other_near = move(result_other[1], ALONG, -1, 1)
    other_wide = move(result_other[3], ALONG, 1, 1)
    grad_attended, grad_attn_seq = project(pieces, output_weight, True)
    small_high, small_low = split_two(
        jnp.concatenate([router_part, gain_two_part[None], jnp.zeros((31, model_width), f32)], axis=0)
    )
    small_rows = jnp.concatenate([small_high, small_low], axis=0)
    dp_size = 32
    dp_rows = model_width // dp_size
    grad_attended, back_wide, other_near, other_wide, expert_far = sync(
        grad_attended, back_wide, other_near, other_wide, expert_far
    )
    far_rows = [move(middle_rows[0], ACROSS, 1, 0), move(middle_rows[1], ACROSS, -1, 0)]
    swapped = swap_core(result_other[0])
    expert_near = scatter_whole(expert_chunk, *expert_far)
    grad_projected, grad_scaled = attend_back(
        turned, attended, grad_attended, log_totals, inverse, cos, sin
    )
    grad_projected, grad_scaled, far_rows, swapped = sync(
        grad_projected, grad_scaled, far_rows, swapped
    )
    joined_grad = weight_grads(
        grad_scaled, sequence, norm_gains[0:1], attended, grad_attn_seq, small_rows
    )
    grad_projected, joined_grad = sync(grad_projected, joined_grad)

    def normed_chunk(grads, k):
        start = lax.rem(place + k, 4) * local_rows
        piece = lax.dynamic_slice_in_dim(grads, start, local_rows, 1)
        return dot(piece, weight_turned, 0, 0)

    far = scatter_far(lambda k: normed_chunk(grad_projected, k))
    far, expert_near = sync(far, expert_near)
    near = scatter_whole(lambda k: normed_chunk(grad_projected, k), *far)
    result_chunks = [
        [result_mine[0], swapped],
        [back_near, other_near],
        far_rows,
        [back_wide, other_wide],
    ]
    joined_terms = exchange(joined_grad.reshape(dp_size, dp_rows, joined_grad.shape[1]))
    result_blocks = combine(
        core_scalar, result_chunks, mixed_blocks, expand_turned, aim, pick_wide, False
    )
    result_far, joined_terms, near = sync(sum_far(result_blocks), joined_terms, near)
    moe_sum, _ = sum_near(result_blocks, result_far, core)
    grad_normed = normed_chunk(grad_projected, 0) + near[0].astype(f32) + near[1].astype(f32)
    weight_all = add_terms(joined_terms)
    joined_all = weight_all[:, : query_width + 2 * keyval_width]
    output_all = weight_all[:, query_width + 2 * keyval_width :]
    expert_up_grad, expert_down_grad = expert_sums(
        jnp.reshape(place, (1,)), expert_grads, *expert_near
    )
    expert_up_grad, expert_down_grad = expert_up_grad[None], expert_down_grad[None]
    query_weight_grad = joined_all[:, :query_width]
    keyval_weight_grad = joined_all[:, query_width:].reshape(dp_rows, 2, keyval_width)
    output_weight_grad = output_all[:, :query_width].T
    tokens_grad = grad_middle + norm_back(inputs, inv_rms_one, norm_gains[0], grad_normed)

    weight_rows = lax.dynamic_slice_in_dim(joined_weight, group * dp_rows, dp_rows, 0)
    gain_rows = lax.dynamic_slice_in_dim(norm_gains[0], group * dp_rows, dp_rows, 0)
    gain_one_part = jnp.sum(weight_rows.astype(f32) * joined_all, axis=1) / gain_rows
    base = query_width
    small = jnp.concatenate(
        [
            output_all[:, base : base + 33] + output_all[:, base + 64 : base + 97],
            gain_one_part[:, None],
            jnp.zeros((dp_rows, 94), f32),
        ],
        axis=1,
    ).reshape(4, dp_rows // 4, 128)
    small = jnp.pad(small, ((0, 0), (0, 4), (0, 0)))
    small = lax.all_to_all(small, "tensor", split_axis=0, concat_axis=0, tiled=True)
    small = jnp.sum(small, axis=0)[: dp_rows // 4].T
    router_grad = small[:experts_all]
    gains_grad = jnp.stack([small[experts_all + 1], small[experts_all]])

    layer_out = (middle + moe_sum).astype(jnp.bfloat16)
    return (
        layer_out,
        tokens_grad,
        gains_grad,
        query_weight_grad,
        keyval_weight_grad,
        output_weight_grad,
        router_grad,
        expert_up_grad,
        expert_down_grad,
    )


def solution(mesh):
    placed = (
        P(("dp", "tensor"), None),
        P(),
        P(None, "tensor"),
        P(None, None, "tensor"),
        P("tensor", None),
        P(),
        P("dp", None, None),
        P("dp", None, None),
        P(("dp", "tensor"), None),
        P(("dp", "tensor"), None),
    )
    return jax.shard_map(
        per_device,
        mesh=mesh,
        in_specs=placed,
        out_specs=(
            P(("dp", "tensor"), None),
            P(("dp", "tensor"), None),
            P(None, ("dp", "tensor")),
            P("dp", "tensor"),
            P("dp", None, "tensor"),
            P("tensor", "dp"),
            P(None, ("dp", "tensor")),
            P("dp", "tensor", None),
            P("dp", None, "tensor"),
        ),
        check_vma=False,
    )
```

```python
import jax
import jax.numpy as jnp
from jax import lax
from jax.experimental import pallas as pl
from jax.experimental.pallas import tpu as pltpu
from jax.sharding import PartitionSpec as P

QUERY_HEADS = 24
KEY_VALUE_HEADS = 8
HEAD_DIM = 64
FF = 512
CAP = 68
PART = 48
ROWS = 72
PAIR = 2 * ROWS
LINE = 4 * PAIR
HALF = 768
EXTRA = 128


epsilon = 1e-06
theta = 10000.0
FORWARD = 512
BACKWARD = 256
GROUP = QUERY_HEADS // KEY_VALUE_HEADS
QUERY_LOCAL = QUERY_HEADS // 4
KEY_LOCAL = KEY_VALUE_HEADS // 4
FACTOR = HEAD_DIM**-0.5
SCALE = FACTOR * 1.4426950408889634
highest = lax.Precision.HIGHEST
BRIEF = pl.CostEstimate(flops=1, bytes_accessed=1, transcendentals=0)
LONG = pl.CostEstimate(flops=10**11, bytes_accessed=1, transcendentals=0)
VMEM_LIMIT = 56 * 2**20
f32 = jnp.float32
bf16 = jnp.bfloat16


def dot(a, b, ca, cb, precision=None):
    return lax.dot_general(
        a, b, (((ca,), (cb,)), ((), ())), preferred_element_type=f32, precision=precision
    )


def inverse_rms(values):
    return lax.rsqrt(jnp.mean(values * values, axis=-1, keepdims=True) + epsilon)


def norm_rows(values, gain_row):
    inv_rms = inverse_rms(values)
    return (values * inv_rms * gain_row, inv_rms)


def norm_back(values, inv_rms, gain_row, upstream):
    scaled = upstream * gain_row
    inner_sum = jnp.mean(scaled * values, axis=-1, keepdims=True)
    return inv_rms * scaled - values * (inv_rms * inv_rms * inv_rms) * inner_sum


def rotary_tables(sequence_length, head_width):
    half_width = head_width // 2
    freqs = theta ** (-(jnp.arange(half_width).astype(jnp.float32) * 2.0 / head_width))
    angles = freqs[:, None] * jnp.arange(sequence_length).astype(jnp.float32)[None, :]
    return (jnp.cos(angles), jnp.sin(angles))


def split_two(values):
    high = lax.reduce_precision(values, 8, 7)
    return high, values - high


def shift_tensor(values, step):
    return lax.ppermute(values, "tensor", [(i, (i + step) % 4) for i in range(4)])


def gather_near(mine, halves):
    if not halves:
        return shift_tensor(mine, 1), shift_tensor(mine, -1)
    half = mine.shape[0] // 2
    top, low = mine[:half], mine[half:]
    left_top, right_low = shift_tensor(top, 1), shift_tensor(low, -1)
    return left_top, right_low, shift_tensor(low, 1), shift_tensor(top, -1)


def gather_far(mine, near, place):
    rows = mine.shape[0]
    half = rows // 2
    if len(near) == 2:
        left, right = near
        far = shift_tensor(left[:half], 1), shift_tensor(right[half:], -1)
        pieces = [(mine, 0, 0), (left, 3, 0), (right, 1, 0)]
    else:
        far = shift_tensor(near[0], 1), shift_tensor(near[1], -1)
        pieces = [(mine, 0, 0), (near[0], 3, 0), (near[2], 3, half)]
        pieces += [(near[3], 1, 0), (near[1], 1, half)]
    pieces += [(far[0], 2, 0), (far[1], 2, half)]
    return [
        (piece, lax.rem(place + owner, 4) * rows + offset) for piece, owner, offset in pieces
    ]


def scatter_far(chunk):
    far = chunk(2).astype(bf16)
    half = far.shape[0] // 2
    return shift_tensor(far[:half], 1), shift_tensor(far[half:], -1)


def scatter_plain(chunk):
    right, left = chunk(1), chunk(3)
    half = right.shape[0] // 2
    return shift_tensor(right[half:].astype(bf16), 1), shift_tensor(left[:half].astype(bf16), -1)


def scatter_summed(chunk, from_left, from_right):
    right, left = chunk(1), chunk(3)
    half = right.shape[0] // 2
    return (
        shift_tensor((right[:half] + from_left.astype(f32)).astype(bf16), 1),
        shift_tensor((left[half:] + from_right.astype(f32)).astype(bf16), -1),
    )


def scatter_near(chunk, from_left, from_right):
    left_low, right_top = scatter_plain(chunk)
    left_top, right_low = scatter_summed(chunk, from_left, from_right)
    return left_top, left_low, right_top, right_low


def scatter_whole(chunk, from_left, from_right):
    right, left = chunk(1), chunk(3)
    half = right.shape[0] // 2
    right = jnp.concatenate([right[:half] + from_left, right[half:]], axis=0).astype(bf16)
    left = jnp.concatenate([left[:half], left[half:] + from_right], axis=0).astype(bf16)
    return shift_tensor(right, 1), shift_tensor(left, -1)


def add_near(mine, near):
    left_top, left_low, right_top, right_low = near
    return mine + jnp.concatenate(
        [left_top.astype(f32) + right_top, left_low.astype(f32) + right_low], axis=0
    )


def exchange_tensor(values):
    parts = values.reshape(4, values.shape[0] // 4, values.shape[1])
    return lax.all_to_all(parts, "tensor", split_axis=0, concat_axis=0, tiled=True)


def add_terms(terms):
    return jnp.sum(terms.astype(f32), axis=0)


def sync(*values):
    return lax.optimization_barrier(values)


def dp_index(y, z, core):
    return (y % 4) * 8 + (z % 4) * 2 + core


def move(values, axes, step, cross):
    pairs = []
    for y in range(4):
        for z in range(4):
            for core in range(2):
                there = (y + step, z) if axes[core] == 0 else (y, z + step)
                pairs.append((dp_index(y, z, core), dp_index(*there, core ^ cross)))
    return lax.ppermute(values, "dp", pairs)


ALONG, ACROSS = (0, 1), (1, 0)


def swap_core(values):
    return move(values, ALONG, 0, 1)


def spread_near(values, extra, core):
    mine = lax.dynamic_slice_in_dim(values, core * HALF, HALF, 1)
    other = lax.dynamic_slice_in_dim(values, (1 - core) * HALF, HALF, 1)
    mine = jnp.concatenate([mine, extra], axis=1)
    other = jnp.concatenate([other, extra], axis=1)
    return mine, other, move(mine, ALONG, 1, 0), move(other, ACROSS, -1, 1), swap_core(other)


def spread_far(mine, other, back_mine, ahead_other, swapped):
    ahead_mine = move(mine, ALONG, -1, 0)
    back_other = move(other, ACROSS, 1, 1)
    far_mine = move(back_mine, ALONG, 1, 0)
    far_other = move(ahead_other, ALONG, -1, 0)
    return [mine, swapped, back_mine, back_other, far_mine, far_other, ahead_mine, ahead_other]


def send_first(chunks):
    middle = [move(chunks[2][0], ACROSS, 1, 0), move(chunks[2][1], ACROSS, -1, 0)]
    return middle, move(chunks[1][0], ACROSS, 1, 0), move(chunks[3][0], ACROSS, -1, 0)


def send_cross(chunks):
    return (
        swap_core(chunks[0][1]),
        move(chunks[1][1], ACROSS, 1, 1),
        move(chunks[3][1], ACROSS, -1, 1),
    )


def send_far(middle):
    return move(middle[0], ACROSS, 1, 0), move(middle[1], ACROSS, -1, 1)


def gather_rows(chunks, first, cross, far):
    _, near, wide = first
    swapped, other_near, other_wide = cross
    return [chunks[0][0], near, far[0], wide], [swapped, other_near, far[1], other_wide]


def send_rest(chunks, middle, near, wide):
    return gather_rows(chunks, (middle, near, wide), send_cross(chunks), send_far(middle))


def return_first(mine, other):
    middle = [move(mine[2], ACROSS, 1, 0), move(other[2], ALONG, -1, 1)]
    return middle, move(mine[1], ACROSS, -1, 0), move(mine[3], ACROSS, 1, 0)


def return_rest(mine, other, middle, near, wide):
    other_near = move(other[1], ALONG, -1, 1)
    other_wide = move(other[3], ALONG, 1, 1)
    far = [move(middle[0], ACROSS, 1, 0), move(middle[1], ACROSS, -1, 0)]
    return [[mine[0], swap_core(other[0])], [near, other_near], far, [wide, other_wide]]


def sum_far(blocks):
    return move(blocks[4], ALONG, 1, 0), move(blocks[5], ALONG, -1, 0)


def sum_near(blocks, passing, core):
    here, back, ahead = blocks[0:2], blocks[2:4], blocks[6:8]
    add = lambda a, b: (a.astype(f32) + b.astype(f32)).astype(bf16)
    far_one, far_two = passing
    mine_two = move(back[0], ALONG, -1, 0)
    other_one = move(ahead[1], ALONG, 1, 1)
    other_here = swap_core(here[1])
    mine_one = move(add(ahead[0], far_one), ALONG, 1, 0)
    other_two = move(add(back[1], far_two), ALONG, -1, 1)
    mine = here[0].astype(f32) + mine_one.astype(f32) + mine_two.astype(f32)
    other = other_here.astype(f32) + other_one.astype(f32) + other_two.astype(f32)
    first = core == 0
    left = jnp.where(first, mine[:, :HALF], other[:, :HALF])
    right = jnp.where(first, other[:, :HALF], mine[:, :HALF])
    return jnp.concatenate([left, right], axis=1), mine[:, HALF:] + other[:, HALF:]


def exchange(values):
    return lax.all_to_all(values, "dp", split_axis=0, concat_axis=0, tiled=True)


def turn(values, cos, sin):
    half = values.shape[0] // 2
    low, high = values[:half], values[half:]
    return jnp.concatenate([low * cos - high * sin, high * cos + low * sin], axis=0)


def diagonal_mask(size):
    key = lax.broadcasted_iota(jnp.int32, (size, size), 0)
    query = lax.broadcasted_iota(jnp.int32, (size, size), 1)
    return key <= query


def attend_kernel(
    q_ref, k_ref, v_ref, inverse_ref, cos_ref, sin_ref, out_ref, total_ref, turned_ref, key_s
):
    group, member = pl.program_id(0), pl.program_id(1)
    inverse = inverse_ref[...]
    cos, sin = cos_ref[...] * inverse, sin_ref[...] * inverse

    @pl.when(member == 0)
    def _():
        keys = turn(k_ref[...], cos, sin)
        key_s[...] = keys.T.astype(bf16)
        first = pl.multiple_of((QUERY_LOCAL + group) * HEAD_DIM, HEAD_DIM)
        turned_ref[pl.ds(first, HEAD_DIM), :] = keys.astype(bf16)
        second = pl.multiple_of((QUERY_LOCAL + KEY_LOCAL + group) * HEAD_DIM, HEAD_DIM)
        turned_ref[pl.ds(second, HEAD_DIM), :] = (v_ref[...] * inverse).astype(bf16)

    queries = turn(q_ref[...], cos, sin).astype(bf16)
    values = (v_ref[...] * inverse).astype(bf16)
    head = pl.multiple_of((group * GROUP + member) * HEAD_DIM, HEAD_DIM)
    turned_ref[pl.ds(head, HEAD_DIM), :] = queries
    causal = diagonal_mask(FORWARD)
    for j in range(queries.shape[1] // FORWARD):
        columns = slice(j * FORWARD, (j + 1) * FORWARD)
        query = queries[:, columns]
        tiles = []
        top = None
        for i in range(j + 1):
            tile = dot(key_s[i * FORWARD : (i + 1) * FORWARD, :], query, 1, 0) * SCALE
            if i == j:
                tile = jnp.where(causal, tile, -1e30)
            tiles.append(tile)
            peak = jnp.max(tile, axis=0, keepdims=True)
            top = peak if top is None else jnp.maximum(top, peak)
        total = jnp.zeros_like(top)
        summed = jnp.zeros((HEAD_DIM, FORWARD), f32)
        for i in range(j + 1):
            tile = jnp.exp2(tiles[i] - top)
            total = total + jnp.sum(tile, axis=0, keepdims=True)
            summed = summed + dot(values[:, i * FORWARD : (i + 1) * FORWARD], tile.astype(bf16), 1, 0)
        out_ref[pl.ds(head, HEAD_DIM), columns] = (summed / total).astype(bf16)
        total_ref[0, :, columns] = top + jnp.log2(total)


def attend_back_kernel(*refs):
    q_ref, k_ref, v_ref, out_ref, grad_ref, total_ref, inverse_ref, cos_ref, sin_ref = refs[:9]
    back_ref, scaled_ref, key_s, val_s, gk_s, gv_s = refs[9:]
    inverse = inverse_ref[...]

    def put(row, values):
        row = pl.multiple_of(row * HEAD_DIM, HEAD_DIM)
        back_ref[pl.ds(row, HEAD_DIM), :] = values.astype(bf16)
        scaled_ref[pl.ds(row, HEAD_DIM), :] = (values * inverse).astype(bf16)

    group, member = pl.program_id(0), pl.program_id(1)
    cos, sin = cos_ref[...], sin_ref[...]

    @pl.when(member == 0)
    def _():
        key_s[...] = k_ref[...].astype(f32).T.astype(bf16)
        val_s[...] = v_ref[...].astype(f32).T.astype(bf16)
        gk_s[...] = jnp.zeros_like(gk_s)
        gv_s[...] = jnp.zeros_like(gv_s)

    queries, grads, keys = q_ref[...], grad_ref[...], k_ref[...]
    inner = jnp.sum(out_ref[...].astype(f32) * grads.astype(f32), axis=0, keepdims=True)
    totals = total_ref[0]
    causal = diagonal_mask(BACKWARD)
    pieces = []
    for j in range(queries.shape[1] // BACKWARD):
        columns = slice(j * BACKWARD, (j + 1) * BACKWARD)
        query, grad = queries[:, columns], grads[:, columns]
        many = (j + 1) * BACKWARD
        scores = dot(key_s[:many, :], query, 1, 0)
        grad_all = dot(val_s[:many, :], grad, 1, 0)
        low, grads_low = [], []
        for i in range(j + 1):
            rows = slice(i * BACKWARD, (i + 1) * BACKWARD)
            probs = jnp.exp2(scores[rows] * SCALE - totals[:, columns])
            if i == j:
                probs = jnp.where(causal, probs, 0.0)
            low.append(probs.astype(bf16))
            grads_low.append((probs * (grad_all[rows] - inner[:, columns])).astype(bf16))
        low, grads_low = jnp.concatenate(low, axis=0), jnp.concatenate(grads_low, axis=0)
        gv_s[:many, :] += dot(low, grad, 1, 1)
        gk_s[:many, :] += dot(grads_low, query, 1, 1)
        query_grad = dot(keys[:, :many], grads_low, 1, 0)
        pieces.append(query_grad * FACTOR)
    put(group * GROUP + member, turn(jnp.concatenate(pieces, axis=1), cos, -sin))

    @pl.when(member == GROUP - 1)
    def _():
        put(QUERY_LOCAL + group, turn(gk_s[...].T * FACTOR, cos, -sin))
        put(QUERY_LOCAL + KEY_LOCAL + group, gv_s[...].T)


def head_block(first, per_group, tokens):
    if per_group:
        return pl.BlockSpec((HEAD_DIM, tokens), lambda g, m: (first + g * per_group + m, 0))
    return pl.BlockSpec((HEAD_DIM, tokens), lambda g, m: (first + g, 0))


def whole_block(shape):
    return pl.BlockSpec(shape, lambda g, m: (0,) * len(shape))


def project_kernel(start_ref, *refs):
    pieces, weight_ref = refs[:-4], refs[-4]
    out_ref, sequence_ref, inverse_ref = refs[-3:]
    ones = jnp.ones((8, weight_ref.shape[1]), bf16)
    for i, piece in enumerate(pieces):
        count = piece.shape[0]
        start = pl.multiple_of(start_ref[i], 128)
        rows = piece[...]
        sequence_ref[pl.ds(start, count), :] = rows
        out_ref[:, pl.ds(start, count)] = dot(weight_ref[...], rows, 1, 1)
        wide = rows.astype(f32)
        squares = dot(ones, (wide * wide).astype(bf16), 1, 1)[0:1]
        inverse_ref[:, pl.ds(start, count)] = lax.rsqrt(squares * (1.0 / rows.shape[1]) + epsilon)


def project_back_kernel(start_ref, *refs):
    pieces, weight_ref = refs[:-3], refs[-3]
    out_ref, sequence_ref = refs[-2:]
    for i, piece in enumerate(pieces):
        count = piece.shape[0]
        start = pl.multiple_of(start_ref[i], 128)
        rows = piece[...]
        sequence_ref[pl.ds(start, count), :] = rows
        out_ref[:, pl.ds(start, count)] = dot(weight_ref[...], rows, 1, 1).astype(bf16)


def project(pieces, weight, back):
    tokens = sum(piece.shape[0] for piece, _ in pieces)
    width, depth = weight.shape
    outs = [
        jax.ShapeDtypeStruct((width, tokens), bf16 if back else f32),
        jax.ShapeDtypeStruct((tokens, depth), bf16),
    ]
    if not back:
        outs.append(jax.ShapeDtypeStruct((1, tokens), f32))
    spec = pl.BlockSpec(memory_space=pltpu.VMEM)
    return pl.pallas_call(
        project_back_kernel if back else project_kernel,
        in_specs=[pl.BlockSpec(memory_space=pltpu.SMEM)] + [spec] * (len(pieces) + 1),
        out_specs=[spec] * len(outs),
        out_shape=outs,
        compiler_params=pltpu.CompilerParams(vmem_limit_bytes=20 * 2**20),
        cost_estimate=BRIEF,
        name="project_back" if back else "project",
    )(jnp.stack([start for _, start in pieces]), *[piece for piece, _ in pieces], weight)


def weight_grads_kernel(
    core_ref, one_ref, rows_ref, scale_ref, two_ref, other_ref, extra_ref, keep_ref, send_ref
):
    parts = (
        dot(one_ref[...], rows_ref[...], 1, 0) * scale_ref[...],
        dot(two_ref[...], other_ref[...], 1, 0),
        extra_ref[...],
    )
    first = core_ref[0] == 0
    at = 0
    for part in parts:
        part = part.T
        width = part.shape[1]
        even = [part[i : i + PART] for i in range(0, part.shape[0], 2 * PART)]
        odd = [part[i + PART : i + 2 * PART] for i in range(0, part.shape[0], 2 * PART)]
        even, odd = jnp.concatenate(even, axis=0), jnp.concatenate(odd, axis=0)
        keep_ref[:, at : at + width] = jnp.where(first, even, odd).astype(bf16)
        send_ref[:, at : at + width] = jnp.where(first, odd, even).astype(bf16)
        at += width


def weight_grads(core, one, rows, scale, two, other, extra):
    tokens, depth = rows.shape
    block = 384
    width = one.shape[0] + two.shape[0] + extra.shape[0]
    whole = lambda shape: pl.BlockSpec(shape, lambda d: (0, 0))
    out = pl.BlockSpec((block // 2, width), lambda d: (d, 0))
    return pl.pallas_call(
        weight_grads_kernel,
        grid=(depth // block,),
        in_specs=[
            pl.BlockSpec(memory_space=pltpu.SMEM),
            whole(one.shape),
            pl.BlockSpec((tokens, block), lambda d: (0, d)),
            pl.BlockSpec((1, block), lambda d: (0, d)),
            whole(two.shape),
            pl.BlockSpec((tokens, block), lambda d: (0, d)),
            pl.BlockSpec((extra.shape[0], block), lambda d: (0, d)),
        ],
        out_specs=[out, out],
        out_shape=[jax.ShapeDtypeStruct((depth // 2, width), bf16)] * 2,
        compiler_params=pltpu.CompilerParams(vmem_limit_bytes=30 * 2**20),
        cost_estimate=BRIEF,
        name="weight_grads",
    )(core, one, rows, scale, two, other, extra)


def expert_sums_kernel(place_ref, mine_ref, top_ref, low_ref, far_ref, near_ref, up_ref, down_ref):
    left = jnp.concatenate([top_ref[...].astype(f32), low_ref[...].astype(f32)], axis=0)
    right = jnp.concatenate([far_ref[...].astype(f32), near_ref[...].astype(f32)], axis=0)
    total = mine_ref[...].astype(f32) + left + right
    up_ref[...] = total[:, : 2 * FF]
    down_ref[...] = total[:, 2 * FF :].T


def expert_sums(place, grads, left_top, left_low, right_top, right_low):
    half, width = left_top.shape
    rows = 2 * half
    whole = lambda shape: pl.BlockSpec(shape, lambda i, at: (0, 0))
    return pl.pallas_call(
        expert_sums_kernel,
        grid_spec=pltpu.PrefetchScalarGridSpec(
            num_scalar_prefetch=1,
            grid=(1,),
            in_specs=[pl.BlockSpec((rows, width), lambda i, at: (at[0], 0))] + [whole((half, width))] * 4,
            out_specs=[whole((rows, 2 * FF)), whole((FF, rows))],
        ),
        out_shape=[
            jax.ShapeDtypeStruct((rows, 2 * FF), f32),
            jax.ShapeDtypeStruct((FF, rows), f32),
        ],
        compiler_params=pltpu.CompilerParams(vmem_limit_bytes=24 * 2**20),
        cost_estimate=BRIEF,
        name="expert_sums",
    )(place, grads, left_top, left_low, right_top, right_low)


def attend(projected, inverse, cos, sin):
    width, tokens = projected.shape
    total_block = pl.BlockSpec((1, 1, tokens), lambda g, m: (g * GROUP + m, 0, 0))
    return pl.pallas_call(
        attend_kernel,
        grid=(KEY_LOCAL, GROUP),
        in_specs=[
            head_block(0, GROUP, tokens),
            head_block(QUERY_LOCAL, 0, tokens),
            head_block(QUERY_LOCAL + KEY_LOCAL, 0, tokens),
            whole_block(inverse.shape),
            whole_block(cos.shape),
            whole_block(sin.shape),
        ],
        out_specs=(
            whole_block((QUERY_LOCAL * HEAD_DIM, tokens)),
            total_block,
            whole_block((width, tokens)),
        ),
        out_shape=(
            jax.ShapeDtypeStruct((QUERY_LOCAL * HEAD_DIM, tokens), bf16),
            jax.ShapeDtypeStruct((QUERY_LOCAL, 1, tokens), f32),
            jax.ShapeDtypeStruct((width, tokens), bf16),
        ),
        scratch_shapes=[pltpu.VMEM((tokens, HEAD_DIM), bf16)],
        compiler_params=pltpu.CompilerParams(vmem_limit_bytes=20 * 2**20),
        cost_estimate=BRIEF,
        name="attend",
    )(projected, projected, projected, inverse, cos, sin)


def attend_back(turned, out, grad, totals, inverse, cos, sin):
    width, tokens = turned.shape
    total_block = pl.BlockSpec((1, 1, tokens), lambda g, m: (g * GROUP + m, 0, 0))
    return pl.pallas_call(
        attend_back_kernel,
        grid=(KEY_LOCAL, GROUP),
        in_specs=[
            head_block(0, GROUP, tokens),
            head_block(QUERY_LOCAL, 0, tokens),
            head_block(QUERY_LOCAL + KEY_LOCAL, 0, tokens),
            head_block(0, GROUP, tokens),
            head_block(0, GROUP, tokens),
            total_block,
            whole_block(inverse.shape),
            whole_block(cos.shape),
            whole_block(sin.shape),
        ],
        out_specs=[whole_block((width, tokens))] * 2,
        out_shape=[jax.ShapeDtypeStruct((width, tokens), bf16)] * 2,
        scratch_shapes=[
            pltpu.VMEM((tokens, HEAD_DIM), bf16),
            pltpu.VMEM((tokens, HEAD_DIM), bf16),
            pltpu.VMEM((tokens, HEAD_DIM), f32),
            pltpu.VMEM((tokens, HEAD_DIM), f32),
        ],
        compiler_params=pltpu.CompilerParams(vmem_limit_bytes=20 * 2**20),
        cost_estimate=LONG,
        name="attend_back",
    )(turned, turned, turned, out, grad, totals, inverse, cos, sin)


def build_kernel(gated, refs):
    tokens, (expand_ref, pick_ref, core_ref) = refs[:8], refs[8:11]
    outs, token_s = refs[11:19], refs[19]
    step = pl.program_id(0)
    for r in range(4):

        @pl.when(step == r)
        def _(r=r):
            token_s[0] = tokens[2 * r][...]
            token_s[1] = tokens[2 * r + 1][...]

    count = tokens[0].shape[0]
    index = lax.broadcasted_iota(jnp.int32, (ROWS, count), 0).astype(f32)
    below = lax.broadcasted_iota(jnp.int32, (8, 128), 0)
    across = lax.broadcasted_iota(jnp.int32, (8, 128), 1)
    pieces = []
    for s in (core_ref[0], 1 - core_ref[0]):
        slots = dot(expand_ref[...], token_s[s, :, HALF:], 1, 1)
        hot = jnp.concatenate(
            [
                jnp.where(slots[k * ROWS : (k + 1) * ROWS] == index, 1.0, 0.0)
                for k in range(8)
            ],
            axis=0,
        ).astype(bf16)
        rows = dot(hot, token_s[s, :, :HALF], 1, 0)
        parts = [rows[k * ROWS : (k + 1) * ROWS] for k in range(8)]
        if gated:
            gates = dot(pick_ref[...], token_s[s, :, HALF:], 1, 1).astype(bf16)
            for d in range(4):
                values = dot(gates, hot[d * PAIR : d * PAIR + 128], 1, 1)
                high, low = values[2 * d : 2 * d + 1], values[2 * d + 1 : 2 * d + 2]
                spare = jnp.where(below == 4, high, jnp.where(below == 5, low, 0.0))
                spare = jnp.where(across < ROWS, spare, 0.0)
                part = parts[2 * d]
                last = jnp.concatenate([part[64:, :128] + spare, part[64:, 128:]], axis=1)
                parts[2 * d] = jnp.concatenate([part[:64], last], axis=0)
        pieces.append(parts)
    for k in range(8):
        outs[k][0] = jnp.concatenate([pieces[0][k], pieces[1][k]], axis=0).astype(bf16)


def build(core, blocks, expand, pick, gated):
    count, width = blocks[0].shape
    whole = lambda shape: pl.BlockSpec(shape, lambda r: (0,) * len(shape))
    outs = pl.pallas_call(
        lambda *refs: build_kernel(gated, refs),
        grid=(4,),
        in_specs=[whole((count, width))] * 8
        + [whole(expand.shape), whole(pick.shape), pl.BlockSpec(memory_space=pltpu.SMEM)],
        out_specs=[pl.BlockSpec((1, PAIR, HALF), lambda r: (r, 0, 0))] * 8,
        out_shape=[jax.ShapeDtypeStruct((4, PAIR, HALF), bf16)] * 8,
        scratch_shapes=[pltpu.VMEM((2, count, width), bf16)],
        compiler_params=pltpu.CompilerParams(vmem_limit_bytes=VMEM_LIMIT),
        cost_estimate=BRIEF if gated else LONG,
        name="build_rows",
    )(*blocks, expand, pick, core)
    return [[outs[2 * d], outs[2 * d + 1]] for d in range(4)]


def combine_kernel(gated, refs):
    given, slots, (expand_ref, aim_ref, pick_ref, core_ref) = refs[:8], refs[8:16], refs[16:20]
    outs, total_s, slot_s = refs[20:28], refs[28], refs[29]
    core = core_ref[0]
    step = pl.program_id(0)
    for r in range(4):

        @pl.when(step == r)
        def _(r=r):
            slot_s[0] = slots[2 * r][...]
            slot_s[1] = slots[2 * r + 1][...]

    rows = jnp.concatenate([ref[0] for ref in given], axis=0)
    if gated:
        own = lax.broadcasted_iota(jnp.int32, (ROWS, 128), 0)
        own = own == lax.broadcasted_iota(jnp.int32, (ROWS, 128), 1)
        columns = []
        for d in range(4):
            head = given[2 * d][0, :, :128].astype(f32)
            for s in range(2):
                at = s * ROWS + CAP
                high = jnp.sum(jnp.where(own, head[at : at + 1], 0.0), axis=1, keepdims=True)
                low = jnp.sum(jnp.where(own, head[at + 1 : at + 2], 0.0), axis=1, keepdims=True)
                columns.append(
                    high * pick_ref[2 * d : 2 * d + 1] + low * pick_ref[2 * d + 1 : 2 * d + 2]
                )
            columns.append(jnp.zeros((PAIR, EXTRA), f32))
        rows = jnp.concatenate([rows, jnp.concatenate(columns, axis=0).astype(bf16)], axis=1)
    hots = []
    for s in range(2):
        hot = dot(slot_s[core if s == 0 else 1 - core], expand_ref[...], 1, 0)
        hot = hot == aim_ref[s : s + 1]
        hots.append(jnp.where(hot, 1.0, 0.0).astype(bf16))
    total = dot(jnp.concatenate(hots, axis=0), rows, 1, 0).astype(bf16)
    count = slot_s.shape[1]
    total_s[0] = total[:count]
    total_s[1] = total[count:]
    for r in range(4):

        @pl.when(step == r)
        def _(r=r):
            outs[2 * r][...] = total_s[core]
            outs[2 * r + 1][...] = total_s[1 - core]


def combine(core, chunks, blocks, expand, aim, pick, gated):
    count = blocks[0].shape[0]
    width = HALF + (EXTRA if gated else 0)
    whole = lambda shape: pl.BlockSpec(shape, lambda r: (0,) * len(shape))
    return pl.pallas_call(
        lambda *refs: combine_kernel(gated, refs),
        grid=(4,),
        in_specs=[pl.BlockSpec((1, PAIR, HALF), lambda r: (r, 0, 0))] * 8
        + [pl.BlockSpec((count, EXTRA), lambda r: (0, HALF // EXTRA))] * 8
        + [
            whole(expand.shape),
            whole(aim.shape),
            whole(pick.shape),
            pl.BlockSpec(memory_space=pltpu.SMEM),
        ],
        out_specs=[whole((count, width))] * 8,
        out_shape=[jax.ShapeDtypeStruct((count, width), bf16)] * 8,
        scratch_shapes=[
            pltpu.VMEM((2, count, width), bf16),
            pltpu.VMEM((2, count, EXTRA), bf16),
        ],
        compiler_params=pltpu.CompilerParams(vmem_limit_bytes=VMEM_LIMIT),
        cost_estimate=LONG,
        name="combine_rows",
    )(*[piece for chunk in chunks for piece in chunk], *blocks, expand, aim, pick, core)


def whole_rows(core_ref, mine, other, mine_s):
    step = pl.program_id(0)
    for d in range(4):

        @pl.when(step == d)
        def _(d=d):
            for r in range(4):
                mine_s[r * PAIR : (r + 1) * PAIR, :] = mine[d][r]

    one = mine_s[...]
    two = jnp.concatenate([ref[0] for ref in other], axis=0)
    first = core_ref[0] == 0
    return one, jnp.concatenate([jnp.where(first, one, two), jnp.where(first, two, one)], axis=1)


def store_halves(core_ref, values, spare, mine, other):
    step = pl.program_id(0)
    first = core_ref[0] == 0
    one = jnp.where(first, values[:, :HALF], values[:, HALF:])
    two = jnp.where(first, values[:, HALF:], values[:, :HALF]).astype(bf16)
    if spare is not None:
        one = jnp.concatenate([one[:, :128] + spare, one[:, 128:]], axis=1)
    one = one.astype(bf16)
    for d in range(4):

        @pl.when(step == d)
        def _(d=d):
            for r in range(4):
                mine[d][r] = one[r * PAIR : (r + 1) * PAIR]

    for r in range(4):
        other[r][0] = two[r * PAIR : (r + 1) * PAIR]


def cotangent_kernel(*refs):
    core_ref, mine, other = refs[0], refs[1:5], refs[5:9]
    down_ref, rows_ref, hidden_ref, mine_s = refs[9:]
    _, rows = whole_rows(core_ref, mine, other, mine_s)
    rows_ref[0] = rows
    hidden_ref[0] = dot(rows, down_ref[...], 1, 1)


def expert_kernel(*refs):
    core_ref, mine, other, up_ref, back_ref = refs[0], refs[1:5], refs[5:9], refs[9], refs[10]
    rows_ref, grad_ref, hidden_ref = refs[11:14]
    mine_out, other_out, mine_s = refs[14:18], refs[18:22], refs[22]
    one, rows = whole_rows(core_ref, mine, other, mine_s)
    rows_ref[0] = rows
    own = lax.broadcasted_iota(jnp.int32, (ROWS, 128), 0)
    own = own == lax.broadcasted_iota(jnp.int32, (ROWS, 128), 1)
    head = one[:, :128].astype(f32)
    gates = []
    for i in range(LINE // ROWS):
        at = i * ROWS + CAP
        line = head[at : at + 1] + head[at + 1 : at + 2]
        gates.append(jnp.sum(jnp.where(own, line, 0.0), axis=1, keepdims=True))
    gate = jnp.concatenate(gates, axis=0)
    low, high = slice(0, FF), slice(FF, 2 * FF)
    gate_part = dot(rows, up_ref[:, low], 1, 0)
    up_part = dot(rows, up_ref[:, high], 1, 0)
    sigmoid = 1.0 / (1.0 + jnp.exp(-gate_part))
    silu = gate_part * sigmoid
    hidden = silu * up_part
    back = back_ref[0]
    inner = jnp.sum(hidden * back, axis=1, keepdims=True)
    hidden_ref[0] = (gate * hidden).astype(bf16)
    back = gate * back
    grad_one = (back * up_part * (sigmoid + silu * (1.0 - sigmoid))).astype(bf16)
    grad_two = (back * silu).astype(bf16)
    grad_ref[0, :, low] = grad_one
    grad_ref[0, :, high] = grad_two
    total = dot(grad_one, up_ref[:, low], 1, 1) + dot(grad_two, up_ref[:, high], 1, 1)
    below = lax.broadcasted_iota(jnp.int32, (8, 128), 0)
    spares = []
    for i in range(LINE // ROWS):
        line = jnp.where(own, inner[i * ROWS : (i + 1) * ROWS], 0.0)
        line = jnp.sum(line, axis=0, keepdims=True)
        high = line.astype(bf16).astype(f32)
        spare = jnp.where(below == 4, high, jnp.where(below == 5, line - high, 0.0))
        spares += [jnp.zeros((ROWS - 8, 128), f32), spare]
    store_halves(
        core_ref, total, jnp.concatenate(spares, axis=0), mine_out, other_out
    )


def result_kernel(*refs):
    core_ref, hidden_ref, down_ref = refs[:3]
    store_halves(core_ref, dot(hidden_ref[0], down_ref[...], 1, 0), None, refs[3:7], refs[7:11])


def whole_spec(shape):
    return pl.BlockSpec(shape, lambda d: (0,) * len(shape))


def line_spec(rows, width):
    return pl.BlockSpec((1, rows, width), lambda d: (d, 0, 0))


CORE_SPEC = pl.BlockSpec(memory_space=pltpu.SMEM)
EXPERT_PARAMS = dict(compiler_params=pltpu.CompilerParams(vmem_limit_bytes=VMEM_LIMIT))


def cotangent_rows(core, mine, other, down):
    return pl.pallas_call(
        cotangent_kernel,
        grid=(4,),
        in_specs=[CORE_SPEC]
        + [whole_spec((4, PAIR, HALF))] * 4
        + [line_spec(PAIR, HALF)] * 4
        + [whole_spec(down.shape)],
        out_specs=(line_spec(LINE, 2 * HALF), line_spec(LINE, FF)),
        out_shape=(
            jax.ShapeDtypeStruct((4, LINE, 2 * HALF), bf16),
            jax.ShapeDtypeStruct((4, LINE, FF), f32),
        ),
        scratch_shapes=[pltpu.VMEM((LINE, HALF), bf16)],
        cost_estimate=BRIEF,
        name="cotangent_rows",
        compiler_params=pltpu.CompilerParams(vmem_limit_bytes=28 * 2**20),
    )(core, *mine, *other, down)


def expert_rows(core, mine, other, up, back):
    outs = pl.pallas_call(
        expert_kernel,
        grid=(4,),
        in_specs=[CORE_SPEC]
        + [whole_spec((4, PAIR, HALF))] * 4
        + [line_spec(PAIR, HALF)] * 4
        + [whole_spec(up.shape), line_spec(LINE, FF)],
        out_specs=[line_spec(LINE, 2 * HALF), line_spec(LINE, 2 * FF), line_spec(LINE, FF)]
        + [whole_spec((4, PAIR, HALF))] * 4
        + [line_spec(PAIR, HALF)] * 4,
        out_shape=[
            jax.ShapeDtypeStruct((4, LINE, 2 * HALF), bf16),
            jax.ShapeDtypeStruct((4, LINE, 2 * FF), bf16),
            jax.ShapeDtypeStruct((4, LINE, FF), bf16),
        ]
        + [jax.ShapeDtypeStruct((4, PAIR, HALF), bf16)] * 8,
        scratch_shapes=[pltpu.VMEM((LINE, HALF), bf16)],
        cost_estimate=BRIEF,
        name="expert_rows",
        **EXPERT_PARAMS,
    )(core, *mine, *other, up, back)
    return outs[0], outs[1], outs[2], outs[3:7], outs[7:11]


def result_rows(core, hidden, down):
    outs = pl.pallas_call(
        result_kernel,
        grid=(4,),
        in_specs=[CORE_SPEC, line_spec(LINE, FF), whole_spec(down.shape)],
        out_specs=[whole_spec((4, PAIR, HALF))] * 4 + [line_spec(PAIR, HALF)] * 4,
        out_shape=[jax.ShapeDtypeStruct((4, PAIR, HALF), bf16)] * 8,
        cost_estimate=LONG,
        name="result_rows",
        **EXPERT_PARAMS,
    )(core, hidden, down)
    return outs[:4], outs[4:]


def per_device(
    tokens,
    norm_gains,
    query_matrix,
    key_value_weight,
    output_weight,
    router,
    expert_up,
    expert_down,
    routes,
    cotangent,
):
    local_rows, model_width = tokens.shape
    query_width = query_matrix.shape[1]
    keyval_width = key_value_weight.shape[2]
    experts_all = router.shape[0]
    place = lax.axis_index("tensor")
    group = lax.axis_index("dp")

    expert_index = jnp.arange(experts_all, dtype=jnp.int32)
    picked = jnp.any(routes[:, :, None] == expert_index[None, None, :], axis=1)
    token_index = jnp.arange(local_rows, dtype=jnp.int32)
    before = (token_index[:, None] > token_index[None, :]).astype(bf16)
    rank = dot(before, picked.astype(bf16), 1, 0)
    slot = jnp.where(picked, rank, -1.0)
    core = lax.rem(group, 2)
    line_y, line_z = group // 8, lax.rem(group // 2, 4)
    core_scalar = jnp.reshape(core, (1,)).astype(jnp.int32)

    distance = jnp.arange(4, dtype=jnp.int32)
    chip = jnp.where(
        core == 0, line_y * 4 + (line_z + distance) % 4, ((line_y + distance) % 4) * 4 + line_z
    )
    partner = jnp.stack([2 * chip + core, 2 * chip + 1 - core], axis=1).reshape(8)
    lane = jnp.arange(EXTRA, dtype=jnp.int32)
    hit = lane[None, :] == partner[:, None] + 64
    expand = jnp.repeat(hit, ROWS, axis=0).astype(bf16)
    expand_turned = jnp.repeat(hit, PAIR, axis=0).T.astype(bf16)
    near = partner.reshape(4, 2)[:, 0]
    pick = jnp.stack([near, near + 32], axis=1).reshape(8)
    pick = jnp.pad((lane[None, :] == pick[:, None]).astype(bf16), ((0, 8), (0, 0)))
    pick_wide = pick.astype(f32)
    spot = jnp.arange(8 * PAIR, dtype=jnp.int32)
    aim = jnp.stack(
        [
            jnp.where((spot // ROWS) % 2 == s, spot % ROWS, -5 if s < 2 else -6).astype(f32)
            for s in range(8)
        ],
        axis=0,
    )

    def wide(values):
        return jnp.pad(values, ((0, 0), (0, EXTRA - values.shape[1])))

    up_matrix, down_matrix = expert_up[0], expert_down[0]

    inputs = tokens.astype(jnp.float32)
    inv_rms_one = inverse_rms(inputs)
    near = gather_near(tokens, False)
    cot_near = spread_near(
        cotangent, wide(jnp.concatenate([jnp.zeros((local_rows, 64), f32), slot], axis=1).astype(bf16)), core
    )
    sequence_length = 4 * local_rows
    joined_weight = jnp.concatenate(
        [query_matrix, key_value_weight.reshape(model_width, 2 * keyval_width)], axis=1
    )
    weight_turned = joined_weight.T
    gained_turned = (norm_gains[0][:, None] * joined_weight.astype(f32)).astype(bf16).T
    cos, sin = rotary_tables(sequence_length, HEAD_DIM)
    near, gained_turned, weight_turned, cos, sin, expand_turned, aim, pick_wide = sync(
        near, gained_turned, weight_turned, cos, sin, expand_turned, aim, pick_wide
    )
    pieces = gather_far(tokens, near, place)
    cot_chunks = build(core_scalar, spread_far(*cot_near), expand, pick, False)
    pieces, cot_chunks = sync(pieces, cot_chunks)
    cot_first = send_first(cot_chunks)
    projected, sequence, inverse = project(pieces, gained_turned, False)
    attended, log_totals, turned = attend(projected, inverse, cos, sin)
    def output_chunk(k):
        start = lax.rem(place + k, 4) * local_rows
        return dot(lax.dynamic_slice_in_dim(attended, start, local_rows, 1), output_weight, 0, 0)

    attended, cot_first = sync(attended, cot_first)
    far = scatter_far(output_chunk)
    cot_swapped = send_cross(cot_chunks)
    near = scatter_whole(output_chunk, *far)
    near, cot_swapped, cot_far = sync(near, cot_swapped, send_far(cot_first[0]))
    cot_got = gather_rows(cot_chunks, cot_first, cot_swapped, cot_far)
    middle = inputs + output_chunk(0) + near[0].astype(f32) + near[1].astype(f32)
    mixed_norm, inv_rms_two = norm_rows(middle, norm_gains[1])
    mixed_low = mixed_norm.astype(jnp.bfloat16)
    logits = dot(mixed_low, router, 1, 1)
    chosen = jnp.where(picked, logits, -jnp.inf)
    chosen_exp = jnp.exp(chosen - jnp.max(chosen, axis=1, keepdims=True))
    gates = chosen_exp / jnp.sum(chosen_exp, axis=1, keepdims=True)

    gates_high, gates_low = split_two(gates)
    mixed_near = spread_near(
        mixed_low, wide(jnp.concatenate([gates_high, gates_low, slot], axis=1).astype(bf16)), core
    )
    mixed_blocks = spread_far(*mixed_near)
    mixed_chunks = build(core_scalar, mixed_blocks, expand, pick, True)
    cot_rows, grad_hidden_one = cotangent_rows(core_scalar, *cot_got, down_matrix)
    mixed_first, grad_hidden_one = sync(send_first(mixed_chunks), grad_hidden_one)
    mixed_got = send_rest(mixed_chunks, *mixed_first)
    mixed_got, grad_hidden_one = sync(mixed_got, grad_hidden_one)
    rows_in, grad_gate_up, hidden_gated, grad_mine, grad_other = expert_rows(
        core_scalar, *mixed_got, up_matrix, grad_hidden_one
    )

    rows_in = rows_in.reshape(4 * LINE, model_width)
    cot_rows = cot_rows.reshape(4 * LINE, model_width)
    grad_gate_up = grad_gate_up.reshape(4 * LINE, 2 * FF)
    hidden_flat = hidden_gated.reshape(4 * LINE, FF)
    up_grad = dot(rows_in, grad_gate_up, 0, 0).astype(bf16)
    grad_first, up_grad = sync(return_first(grad_mine, grad_other), up_grad)
    down_grad = dot(cot_rows, hidden_flat, 0, 0).astype(bf16)
    grad_chunks = return_rest(grad_mine, grad_other, *grad_first)
    expert_grads = jnp.concatenate([up_grad, down_grad], axis=1)
    grad_chunks, expert_grads, hidden_gated = sync(grad_chunks, expert_grads, hidden_gated)
    expert_rows_out = model_width // 4

    def expert_chunk(k):
        start = lax.rem(place + k, 4) * expert_rows_out
        return lax.dynamic_slice_in_dim(expert_grads, start, expert_rows_out, 0)

    grad_blocks = combine(core_scalar, grad_chunks, mixed_blocks, expand_turned, aim, pick_wide, True)
    grad_blocks, expert_far, hidden_gated = sync(
        grad_blocks, scatter_far(expert_chunk), hidden_gated
    )
    result_mine, result_other = result_rows(core_scalar, hidden_gated, down_matrix)
    passing, expert_plain = sync(sum_far(grad_blocks), scatter_plain(expert_chunk))
    grad_mixed, grad_gate = sum_near(grad_blocks, passing, core)
    grad_mixed, grad_gate, result_mine, result_other = sync(
        grad_mixed, grad_gate, result_mine, result_other
    )
    grad_gate = grad_gate[:, :32] + grad_gate[:, 32:64]

    grad_logits = gates * (grad_gate - jnp.sum(gates * grad_gate, axis=1, keepdims=True))
    grad_mixed = grad_mixed + dot(grad_logits, router.astype(f32), 1, 0, highest)
    router_part = dot(grad_logits, mixed_low.astype(f32), 0, 0, highest)
    grad_out = cotangent.astype(jnp.float32)
    grad_middle = grad_out + norm_back(middle, inv_rms_two, norm_gains[1], grad_mixed)
    gain_two_part = jnp.sum(grad_mixed * middle * inv_rms_two, axis=0)

    grad_low = grad_middle.astype(bf16)
    router_part, result_mine, result_other = sync(router_part, result_mine, result_other)
    near = gather_near(grad_low, False)
    middle_rows = [move(result_mine[2], ACROSS, 1, 0), move(result_other[2], ALONG, -1, 1)]
    back_near = move(result_mine[1], ACROSS, -1, 0)
    near, middle_rows, back_near = sync(near, middle_rows, back_near)
    pieces = gather_far(grad_low, near, place)
    back_wide = move(result_mine[3], ACROSS, 1, 0)
    other_near = move(result_other[1], ALONG, -1, 1)
    other_wide = move(result_other[3], ALONG, 1, 1)
    grad_attended, grad_attn_seq = project(pieces, output_weight, True)
    small_high, small_low = split_two(
        jnp.concatenate([router_part, gain_two_part[None], jnp.zeros((31, model_width), f32)], axis=0)
    )
    small_rows = jnp.concatenate([small_high, small_low], axis=0)
    dp_size = 32
    dp_rows = model_width // dp_size
    grad_attended, back_wide, other_near, other_wide, expert_far = sync(
        grad_attended, back_wide, other_near, other_wide, expert_far
    )
    far_rows = [move(middle_rows[0], ACROSS, 1, 0), move(middle_rows[1], ACROSS, -1, 0)]
    swapped = swap_core(result_other[0])
    expert_near = scatter_summed(expert_chunk, *expert_far)
    grad_projected, grad_scaled = attend_back(
        turned, attended, grad_attended, log_totals, inverse, cos, sin
    )
    grad_projected, grad_scaled, far_rows, swapped, expert_near = sync(
        grad_projected, grad_scaled, far_rows, swapped, expert_near
    )
    joined_keep, joined_send = weight_grads(
        core_scalar, grad_scaled, sequence, norm_gains[0:1], attended, grad_attn_seq, small_rows
    )
    joined_grad = (joined_keep.astype(f32) + swap_core(joined_send).astype(f32)).astype(bf16)
    grad_projected, joined_grad, far_rows, swapped = sync(
        grad_projected, joined_grad, far_rows, swapped
    )

    def normed_chunk(grads, k):
        start = lax.rem(place + k, 4) * local_rows
        piece = lax.dynamic_slice_in_dim(grads, start, local_rows, 1)
        return dot(piece, weight_turned, 0, 0)

    far = scatter_far(lambda k: normed_chunk(grad_projected, k))
    near = scatter_whole(lambda k: normed_chunk(grad_projected, k), *far)
    result_chunks = [
        [result_mine[0], swapped],
        [back_near, other_near],
        far_rows,
        [back_wide, other_wide],
    ]
    joined_terms = lax.all_to_all(
        joined_grad.reshape(dp_size // 2, dp_rows, joined_grad.shape[1]),
        "dp",
        split_axis=0,
        concat_axis=0,
        tiled=True,
        axis_index_groups=[[2 * i + c for i in range(16)] for c in range(2)],
    )
    result_blocks = combine(
        core_scalar, result_chunks, mixed_blocks, expand_turned, aim, pick_wide, False
    )
    result_far, joined_terms, near = sync(sum_far(result_blocks), joined_terms, near)
    moe_sum, _ = sum_near(result_blocks, result_far, core)
    grad_normed = normed_chunk(grad_projected, 0) + near[0].astype(f32) + near[1].astype(f32)
    weight_all = add_terms(joined_terms)
    joined_all = weight_all[:, : query_width + 2 * keyval_width]
    output_all = weight_all[:, query_width + 2 * keyval_width :]
    expert_up_grad, expert_down_grad = expert_sums(
        jnp.reshape(place, (1,)),
        expert_grads,
        expert_near[0],
        expert_plain[0],
        expert_plain[1],
        expert_near[1],
    )
    expert_up_grad, expert_down_grad = expert_up_grad[None], expert_down_grad[None]
    query_weight_grad = joined_all[:, :query_width]
    keyval_weight_grad = joined_all[:, query_width:].reshape(dp_rows, 2, keyval_width)
    output_weight_grad = output_all[:, :query_width].T
    tokens_grad = grad_middle + norm_back(inputs, inv_rms_one, norm_gains[0], grad_normed)

    weight_rows = lax.dynamic_slice_in_dim(joined_weight, group * dp_rows, dp_rows, 0)
    gain_rows = lax.dynamic_slice_in_dim(norm_gains[0], group * dp_rows, dp_rows, 0)
    gain_one_part = jnp.sum(weight_rows.astype(f32) * joined_all, axis=1) / gain_rows
    base = query_width
    small = jnp.concatenate(
        [
            output_all[:, base : base + 33] + output_all[:, base + 64 : base + 97],
            gain_one_part[:, None],
            jnp.zeros((dp_rows, 94), f32),
        ],
        axis=1,
    ).reshape(4, dp_rows // 4, 128)
    small = jnp.pad(small, ((0, 0), (0, 4), (0, 0)))
    small = lax.all_to_all(small, "tensor", split_axis=0, concat_axis=0, tiled=True)
    small = jnp.sum(small, axis=0)[: dp_rows // 4].T
    router_grad = small[:experts_all]
    gains_grad = jnp.stack([small[experts_all + 1], small[experts_all]])

    layer_out = (middle + moe_sum).astype(jnp.bfloat16)
    return (
        layer_out,
        tokens_grad,
        gains_grad,
        query_weight_grad,
        keyval_weight_grad,
        output_weight_grad,
        router_grad,
        expert_up_grad,
        expert_down_grad,
    )


def solution(mesh):
    placed = (
        P(("dp", "tensor"), None),
        P(),
        P(None, "tensor"),
        P(None, None, "tensor"),
        P("tensor", None),
        P(),
        P("dp", None, None),
        P("dp", None, None),
        P(("dp", "tensor"), None),
        P(("dp", "tensor"), None),
    )
    return jax.shard_map(
        per_device,
        mesh=mesh,
        in_specs=placed,
        out_specs=(
            P(("dp", "tensor"), None),
            P(("dp", "tensor"), None),
            P(None, ("dp", "tensor")),
            P("dp", "tensor"),
            P("dp", None, "tensor"),
            P("tensor", "dp"),
            P(None, ("dp", "tensor")),
            P("dp", "tensor", None),
            P("dp", None, "tensor"),
        ),
        check_vma=False,
    )
```

```python
import jax
import jax.numpy as jnp
from jax import lax
from jax.experimental import pallas as pl
from jax.experimental.pallas import tpu as pltpu
from jax.sharding import PartitionSpec as P

QUERY_HEADS = 24
KEY_VALUE_HEADS = 8
HEAD_DIM = 64
FF = 512
CAP = 68
PART = 48
ROWS = 72
PAIR = 2 * ROWS
LINE = 4 * PAIR
HALF = 768
EXTRA = 128


epsilon = 1e-06
theta = 10000.0
FORWARD = 512
BACKWARD = 256
GROUP = QUERY_HEADS // KEY_VALUE_HEADS
QUERY_LOCAL = QUERY_HEADS // 4
KEY_LOCAL = KEY_VALUE_HEADS // 4
FACTOR = HEAD_DIM**-0.5
SCALE = FACTOR * 1.4426950408889634
highest = lax.Precision.HIGHEST
BRIEF = pl.CostEstimate(flops=1, bytes_accessed=1, transcendentals=0)
LONG = pl.CostEstimate(flops=10**11, bytes_accessed=1, transcendentals=0)
VMEM_LIMIT = 56 * 2**20
f32 = jnp.float32
bf16 = jnp.bfloat16


def dot(a, b, ca, cb, precision=None):
    return lax.dot_general(
        a, b, (((ca,), (cb,)), ((), ())), preferred_element_type=f32, precision=precision
    )


def inverse_rms(values):
    return lax.rsqrt(jnp.mean(values * values, axis=-1, keepdims=True) + epsilon)


def norm_rows(values, gain_row):
    inv_rms = inverse_rms(values)
    return (values * inv_rms * gain_row, inv_rms)


def norm_back(values, inv_rms, gain_row, upstream):
    scaled = upstream * gain_row
    inner_sum = jnp.mean(scaled * values, axis=-1, keepdims=True)
    return inv_rms * scaled - values * (inv_rms * inv_rms * inv_rms) * inner_sum


def rotary_tables(sequence_length, head_width):
    half_width = head_width // 2
    freqs = theta ** (-(jnp.arange(half_width).astype(jnp.float32) * 2.0 / head_width))
    angles = freqs[:, None] * jnp.arange(sequence_length).astype(jnp.float32)[None, :]
    return (jnp.cos(angles), jnp.sin(angles))


def split_two(values):
    high = lax.reduce_precision(values, 8, 7)
    return high, values - high


def shift_tensor(values, step):
    return lax.ppermute(values, "tensor", [(i, (i + step) % 4) for i in range(4)])


def gather_near(mine, halves):
    if not halves:
        return shift_tensor(mine, 1), shift_tensor(mine, -1)
    half = mine.shape[0] // 2
    top, low = mine[:half], mine[half:]
    left_top, right_low = shift_tensor(top, 1), shift_tensor(low, -1)
    return left_top, right_low, shift_tensor(low, 1), shift_tensor(top, -1)


def gather_far(mine, near, place):
    rows = mine.shape[0]
    half = rows // 2
    if len(near) == 2:
        left, right = near
        far = shift_tensor(left[:half], 1), shift_tensor(right[half:], -1)
        pieces = [(mine, 0, 0), (left, 3, 0), (right, 1, 0)]
    else:
        far = shift_tensor(near[0], 1), shift_tensor(near[1], -1)
        pieces = [(mine, 0, 0), (near[0], 3, 0), (near[2], 3, half)]
        pieces += [(near[3], 1, 0), (near[1], 1, half)]
    pieces += [(far[0], 2, 0), (far[1], 2, half)]
    return [
        (piece, lax.rem(place + owner, 4) * rows + offset) for piece, owner, offset in pieces
    ]


def scatter_far(chunk):
    far = chunk(2).astype(bf16)
    half = far.shape[0] // 2
    return shift_tensor(far[:half], 1), shift_tensor(far[half:], -1)


def scatter_plain(chunk):
    right, left = chunk(1), chunk(3)
    half = right.shape[0] // 2
    return shift_tensor(right[half:].astype(bf16), 1), shift_tensor(left[:half].astype(bf16), -1)


def scatter_summed(chunk, from_left, from_right):
    right, left = chunk(1), chunk(3)
    half = right.shape[0] // 2
    return (
        shift_tensor((right[:half] + from_left.astype(f32)).astype(bf16), 1),
        shift_tensor((left[half:] + from_right.astype(f32)).astype(bf16), -1),
    )


def scatter_near(chunk, from_left, from_right):
    left_low, right_top = scatter_plain(chunk)
    left_top, right_low = scatter_summed(chunk, from_left, from_right)
    return left_top, left_low, right_top, right_low


def scatter_whole(chunk, from_left, from_right):
    right, left = chunk(1), chunk(3)
    half = right.shape[0] // 2
    right = jnp.concatenate([right[:half] + from_left, right[half:]], axis=0).astype(bf16)
    left = jnp.concatenate([left[:half], left[half:] + from_right], axis=0).astype(bf16)
    return shift_tensor(right, 1), shift_tensor(left, -1)


def add_near(mine, near):
    left_top, left_low, right_top, right_low = near
    return mine + jnp.concatenate(
        [left_top.astype(f32) + right_top, left_low.astype(f32) + right_low], axis=0
    )


def exchange_tensor(values):
    parts = values.reshape(4, values.shape[0] // 4, values.shape[1])
    return lax.all_to_all(parts, "tensor", split_axis=0, concat_axis=0, tiled=True)


def add_terms(terms):
    return jnp.sum(terms.astype(f32), axis=0)


def sync(*values):
    return lax.optimization_barrier(values)


def dp_index(y, z, core):
    return (y % 4) * 8 + (z % 4) * 2 + core


def move(values, axes, step, cross):
    pairs = []
    for y in range(4):
        for z in range(4):
            for core in range(2):
                there = (y + step, z) if axes[core] == 0 else (y, z + step)
                pairs.append((dp_index(y, z, core), dp_index(*there, core ^ cross)))
    return lax.ppermute(values, "dp", pairs)


ALONG, ACROSS = (0, 1), (1, 0)


def swap_core(values):
    return move(values, ALONG, 0, 1)


def spread_near(values, extra, core):
    mine = lax.dynamic_slice_in_dim(values, core * HALF, HALF, 1)
    other = lax.dynamic_slice_in_dim(values, (1 - core) * HALF, HALF, 1)
    mine = jnp.concatenate([mine, extra], axis=1)
    other = jnp.concatenate([other, extra], axis=1)
    return mine, other, move(mine, ALONG, 1, 0), move(other, ACROSS, -1, 1), swap_core(other)


def spread_far(mine, other, back_mine, ahead_other, swapped):
    ahead_mine = move(mine, ALONG, -1, 0)
    back_other = move(other, ACROSS, 1, 1)
    far_mine = move(back_mine, ALONG, 1, 0)
    far_other = move(ahead_other, ALONG, -1, 0)
    return [mine, swapped, back_mine, back_other, far_mine, far_other, ahead_mine, ahead_other]


def send_first(chunks):
    middle = [move(chunks[2][0], ACROSS, 1, 0), move(chunks[2][1], ACROSS, -1, 0)]
    return middle, move(chunks[1][0], ACROSS, 1, 0), move(chunks[3][0], ACROSS, -1, 0)


def send_cross(chunks):
    return (
        swap_core(chunks[0][1]),
        move(chunks[1][1], ACROSS, 1, 1),
        move(chunks[3][1], ACROSS, -1, 1),
    )


def send_far(middle):
    return move(middle[0], ACROSS, 1, 0), move(middle[1], ACROSS, -1, 1)


def gather_rows(chunks, first, cross, far):
    _, near, wide = first
    swapped, other_near, other_wide = cross
    return [chunks[0][0], near, far[0], wide], [swapped, other_near, far[1], other_wide]


def send_rest(chunks, middle, near, wide):
    return gather_rows(chunks, (middle, near, wide), send_cross(chunks), send_far(middle))


def return_first(mine, other):
    middle = [move(mine[2], ACROSS, 1, 0), move(other[2], ALONG, -1, 1)]
    return middle, move(mine[1], ACROSS, -1, 0), move(mine[3], ACROSS, 1, 0)


def return_rest(mine, other, middle, near, wide):
    other_near = move(other[1], ALONG, -1, 1)
    other_wide = move(other[3], ALONG, 1, 1)
    far = [move(middle[0], ACROSS, 1, 0), move(middle[1], ACROSS, -1, 0)]
    return [[mine[0], swap_core(other[0])], [near, other_near], far, [wide, other_wide]]


def sum_far(blocks):
    return move(blocks[4], ALONG, 1, 0), move(blocks[5], ALONG, -1, 0)


def sum_near(blocks, passing, core):
    here, back, ahead = blocks[0:2], blocks[2:4], blocks[6:8]
    add = lambda a, b: (a.astype(f32) + b.astype(f32)).astype(bf16)
    far_one, far_two = passing
    mine_two = move(back[0], ALONG, -1, 0)
    other_one = move(ahead[1], ALONG, 1, 1)
    other_here = swap_core(here[1])
    mine_one = move(add(ahead[0], far_one), ALONG, 1, 0)
    other_two = move(add(back[1], far_two), ALONG, -1, 1)
    mine = here[0].astype(f32) + mine_one.astype(f32) + mine_two.astype(f32)
    other = other_here.astype(f32) + other_one.astype(f32) + other_two.astype(f32)
    first = core == 0
    left = jnp.where(first, mine[:, :HALF], other[:, :HALF])
    right = jnp.where(first, other[:, :HALF], mine[:, :HALF])
    return jnp.concatenate([left, right], axis=1), mine[:, HALF:] + other[:, HALF:]


def exchange(values):
    return lax.all_to_all(values, "dp", split_axis=0, concat_axis=0, tiled=True)


def turn(values, cos, sin):
    half = values.shape[0] // 2
    low, high = values[:half], values[half:]
    return jnp.concatenate([low * cos - high * sin, high * cos + low * sin], axis=0)


def diagonal_mask(size):
    key = lax.broadcasted_iota(jnp.int32, (size, size), 0)
    query = lax.broadcasted_iota(jnp.int32, (size, size), 1)
    return key <= query


def attend_kernel(
    q_ref, k_ref, v_ref, inverse_ref, cos_ref, sin_ref, out_ref, total_ref, turned_ref, key_s
):
    group, member = pl.program_id(0), pl.program_id(1)
    inverse = inverse_ref[...]
    cos, sin = cos_ref[...] * inverse, sin_ref[...] * inverse

    @pl.when(member == 0)
    def _():
        keys = turn(k_ref[...], cos, sin)
        key_s[...] = keys.T.astype(bf16)
        first = pl.multiple_of((QUERY_LOCAL + group) * HEAD_DIM, HEAD_DIM)
        turned_ref[pl.ds(first, HEAD_DIM), :] = keys.astype(bf16)
        second = pl.multiple_of((QUERY_LOCAL + KEY_LOCAL + group) * HEAD_DIM, HEAD_DIM)
        turned_ref[pl.ds(second, HEAD_DIM), :] = (v_ref[...] * inverse).astype(bf16)

    queries = turn(q_ref[...], cos, sin).astype(bf16)
    values = (v_ref[...] * inverse).astype(bf16)
    head = pl.multiple_of((group * GROUP + member) * HEAD_DIM, HEAD_DIM)
    turned_ref[pl.ds(head, HEAD_DIM), :] = queries
    causal = diagonal_mask(FORWARD)
    for j in range(queries.shape[1] // FORWARD):
        columns = slice(j * FORWARD, (j + 1) * FORWARD)
        query = queries[:, columns]
        tiles = []
        top = None
        for i in range(j + 1):
            tile = dot(key_s[i * FORWARD : (i + 1) * FORWARD, :], query, 1, 0) * SCALE
            if i == j:
                tile = jnp.where(causal, tile, -1e30)
            tiles.append(tile)
            peak = jnp.max(tile, axis=0, keepdims=True)
            top = peak if top is None else jnp.maximum(top, peak)
        total = jnp.zeros_like(top)
        summed = jnp.zeros((HEAD_DIM, FORWARD), f32)
        for i in range(j + 1):
            tile = jnp.exp2(tiles[i] - top)
            total = total + jnp.sum(tile, axis=0, keepdims=True)
            summed = summed + dot(values[:, i * FORWARD : (i + 1) * FORWARD], tile.astype(bf16), 1, 0)
        out_ref[pl.ds(head, HEAD_DIM), columns] = (summed / total).astype(bf16)
        total_ref[0, :, columns] = top + jnp.log2(total)


def attend_back_kernel(*refs):
    q_ref, k_ref, v_ref, out_ref, grad_ref, total_ref, inverse_ref, cos_ref, sin_ref = refs[:9]
    back_ref, scaled_ref, key_s, val_s, gk_s, gv_s = refs[9:]
    inverse = inverse_ref[...]

    def put(row, values):
        row = pl.multiple_of(row * HEAD_DIM, HEAD_DIM)
        back_ref[pl.ds(row, HEAD_DIM), :] = values.astype(bf16)
        scaled_ref[pl.ds(row, HEAD_DIM), :] = (values * inverse).astype(bf16)

    group, member = pl.program_id(0), pl.program_id(1)
    cos, sin = cos_ref[...], sin_ref[...]

    @pl.when(member == 0)
    def _():
        key_s[...] = k_ref[...].astype(f32).T.astype(bf16)
        val_s[...] = v_ref[...].astype(f32).T.astype(bf16)
        gk_s[...] = jnp.zeros_like(gk_s)
        gv_s[...] = jnp.zeros_like(gv_s)

    queries, grads, keys = q_ref[...], grad_ref[...], k_ref[...]
    inner = jnp.sum(out_ref[...].astype(f32) * grads.astype(f32), axis=0, keepdims=True)
    totals = total_ref[0]
    causal = diagonal_mask(BACKWARD)
    pieces = []
    for j in range(queries.shape[1] // BACKWARD):
        columns = slice(j * BACKWARD, (j + 1) * BACKWARD)
        query, grad = queries[:, columns], grads[:, columns]
        many = (j + 1) * BACKWARD
        scores = dot(key_s[:many, :], query, 1, 0)
        grad_all = dot(val_s[:many, :], grad, 1, 0)
        low, grads_low = [], []
        for i in range(j + 1):
            rows = slice(i * BACKWARD, (i + 1) * BACKWARD)
            probs = jnp.exp2(scores[rows] * SCALE - totals[:, columns])
            if i == j:
                probs = jnp.where(causal, probs, 0.0)
            low.append(probs.astype(bf16))
            grads_low.append((probs * (grad_all[rows] - inner[:, columns])).astype(bf16))
        low, grads_low = jnp.concatenate(low, axis=0), jnp.concatenate(grads_low, axis=0)
        gv_s[:many, :] += dot(low, grad, 1, 1)
        gk_s[:many, :] += dot(grads_low, query, 1, 1)
        query_grad = dot(keys[:, :many], grads_low, 1, 0)
        pieces.append(query_grad * FACTOR)
    put(group * GROUP + member, turn(jnp.concatenate(pieces, axis=1), cos, -sin))

    @pl.when(member == GROUP - 1)
    def _():
        put(QUERY_LOCAL + group, turn(gk_s[...].T * FACTOR, cos, -sin))
        put(QUERY_LOCAL + KEY_LOCAL + group, gv_s[...].T)


def head_block(first, per_group, tokens):
    if per_group:
        return pl.BlockSpec((HEAD_DIM, tokens), lambda g, m: (first + g * per_group + m, 0))
    return pl.BlockSpec((HEAD_DIM, tokens), lambda g, m: (first + g, 0))


def whole_block(shape):
    return pl.BlockSpec(shape, lambda g, m: (0,) * len(shape))


def project_kernel(start_ref, *refs):
    pieces, weight_ref = refs[:-4], refs[-4]
    out_ref, sequence_ref, inverse_ref = refs[-3:]
    ones = jnp.ones((8, weight_ref.shape[1]), bf16)
    for i, piece in enumerate(pieces):
        count = piece.shape[0]
        start = pl.multiple_of(start_ref[i], 128)
        rows = piece[...]
        sequence_ref[pl.ds(start, count), :] = rows
        out_ref[:, pl.ds(start, count)] = dot(weight_ref[...], rows, 1, 1)
        wide = rows.astype(f32)
        squares = dot(ones, (wide * wide).astype(bf16), 1, 1)[0:1]
        inverse_ref[:, pl.ds(start, count)] = lax.rsqrt(squares * (1.0 / rows.shape[1]) + epsilon)


def project_back_kernel(start_ref, *refs):
    pieces, weight_ref = refs[:-3], refs[-3]
    out_ref, sequence_ref = refs[-2:]
    for i, piece in enumerate(pieces):
        count = piece.shape[0]
        start = pl.multiple_of(start_ref[i], 128)
        rows = piece[...]
        sequence_ref[pl.ds(start, count), :] = rows
        out_ref[:, pl.ds(start, count)] = dot(weight_ref[...], rows, 1, 1).astype(bf16)


def project(pieces, weight, back):
    tokens = sum(piece.shape[0] for piece, _ in pieces)
    width, depth = weight.shape
    outs = [
        jax.ShapeDtypeStruct((width, tokens), bf16 if back else f32),
        jax.ShapeDtypeStruct((tokens, depth), bf16),
    ]
    if not back:
        outs.append(jax.ShapeDtypeStruct((1, tokens), f32))
    spec = pl.BlockSpec(memory_space=pltpu.VMEM)
    return pl.pallas_call(
        project_back_kernel if back else project_kernel,
        in_specs=[pl.BlockSpec(memory_space=pltpu.SMEM)] + [spec] * (len(pieces) + 1),
        out_specs=[spec] * len(outs),
        out_shape=outs,
        compiler_params=pltpu.CompilerParams(vmem_limit_bytes=20 * 2**20),
        cost_estimate=BRIEF,
        name="project_back" if back else "project",
    )(jnp.stack([start for _, start in pieces]), *[piece for piece, _ in pieces], weight)


def weight_grads_kernel(
    core_ref, one_ref, rows_ref, scale_ref, two_ref, other_ref, extra_ref, keep_ref, send_ref
):
    parts = (
        dot(one_ref[...], rows_ref[...], 1, 0) * scale_ref[...],
        dot(two_ref[...], other_ref[...], 1, 0),
        extra_ref[...],
    )
    first = core_ref[0] == 0
    at = 0
    for part in parts:
        part = part.T
        width = part.shape[1]
        even = [part[i : i + PART] for i in range(0, part.shape[0], 2 * PART)]
        odd = [part[i + PART : i + 2 * PART] for i in range(0, part.shape[0], 2 * PART)]
        even, odd = jnp.concatenate(even, axis=0), jnp.concatenate(odd, axis=0)
        keep_ref[:, at : at + width] = jnp.where(first, even, odd).astype(bf16)
        send_ref[:, at : at + width] = jnp.where(first, odd, even).astype(bf16)
        at += width


def weight_grads(core, one, rows, scale, two, other, extra):
    tokens, depth = rows.shape
    block = 384
    width = one.shape[0] + two.shape[0] + extra.shape[0]
    whole = lambda shape: pl.BlockSpec(shape, lambda d: (0, 0))
    out = pl.BlockSpec((block // 2, width), lambda d: (d, 0))
    return pl.pallas_call(
        weight_grads_kernel,
        grid=(depth // block,),
        in_specs=[
            pl.BlockSpec(memory_space=pltpu.SMEM),
            whole(one.shape),
            pl.BlockSpec((tokens, block), lambda d: (0, d)),
            pl.BlockSpec((1, block), lambda d: (0, d)),
            whole(two.shape),
            pl.BlockSpec((tokens, block), lambda d: (0, d)),
            pl.BlockSpec((extra.shape[0], block), lambda d: (0, d)),
        ],
        out_specs=[out, out],
        out_shape=[jax.ShapeDtypeStruct((depth // 2, width), bf16)] * 2,
        compiler_params=pltpu.CompilerParams(vmem_limit_bytes=30 * 2**20),
        cost_estimate=BRIEF,
        name="weight_grads",
    )(core, one, rows, scale, two, other, extra)


def expert_sums_kernel(place_ref, mine_ref, top_ref, low_ref, far_ref, near_ref, up_ref, down_ref):
    left = jnp.concatenate([top_ref[...].astype(f32), low_ref[...].astype(f32)], axis=0)
    right = jnp.concatenate([far_ref[...].astype(f32), near_ref[...].astype(f32)], axis=0)
    total = mine_ref[...].astype(f32) + left + right
    up_ref[...] = total[:, : 2 * FF]
    down_ref[...] = total[:, 2 * FF :].T


def expert_sums(place, grads, left_top, left_low, right_top, right_low):
    half, width = left_top.shape
    rows = 2 * half
    whole = lambda shape: pl.BlockSpec(shape, lambda i, at: (0, 0))
    return pl.pallas_call(
        expert_sums_kernel,
        grid_spec=pltpu.PrefetchScalarGridSpec(
            num_scalar_prefetch=1,
            grid=(1,),
            in_specs=[pl.BlockSpec((rows, width), lambda i, at: (at[0], 0))] + [whole((half, width))] * 4,
            out_specs=[whole((rows, 2 * FF)), whole((FF, rows))],
        ),
        out_shape=[
            jax.ShapeDtypeStruct((rows, 2 * FF), f32),
            jax.ShapeDtypeStruct((FF, rows), f32),
        ],
        compiler_params=pltpu.CompilerParams(vmem_limit_bytes=24 * 2**20),
        cost_estimate=BRIEF,
        name="expert_sums",
    )(place, grads, left_top, left_low, right_top, right_low)


def attend(projected, inverse, cos, sin):
    width, tokens = projected.shape
    total_block = pl.BlockSpec((1, 1, tokens), lambda g, m: (g * GROUP + m, 0, 0))
    return pl.pallas_call(
        attend_kernel,
        grid=(KEY_LOCAL, GROUP),
        in_specs=[
            head_block(0, GROUP, tokens),
            head_block(QUERY_LOCAL, 0, tokens),
            head_block(QUERY_LOCAL + KEY_LOCAL, 0, tokens),
            whole_block(inverse.shape),
            whole_block(cos.shape),
            whole_block(sin.shape),
        ],
        out_specs=(
            whole_block((QUERY_LOCAL * HEAD_DIM, tokens)),
            total_block,
            whole_block((width, tokens)),
        ),
        out_shape=(
            jax.ShapeDtypeStruct((QUERY_LOCAL * HEAD_DIM, tokens), bf16),
            jax.ShapeDtypeStruct((QUERY_LOCAL, 1, tokens), f32),
            jax.ShapeDtypeStruct((width, tokens), bf16),
        ),
        scratch_shapes=[pltpu.VMEM((tokens, HEAD_DIM), bf16)],
        compiler_params=pltpu.CompilerParams(vmem_limit_bytes=20 * 2**20),
        cost_estimate=BRIEF,
        name="attend",
    )(projected, projected, projected, inverse, cos, sin)


def attend_back(turned, out, grad, totals, inverse, cos, sin):
    width, tokens = turned.shape
    total_block = pl.BlockSpec((1, 1, tokens), lambda g, m: (g * GROUP + m, 0, 0))
    return pl.pallas_call(
        attend_back_kernel,
        grid=(KEY_LOCAL, GROUP),
        in_specs=[
            head_block(0, GROUP, tokens),
            head_block(QUERY_LOCAL, 0, tokens),
            head_block(QUERY_LOCAL + KEY_LOCAL, 0, tokens),
            head_block(0, GROUP, tokens),
            head_block(0, GROUP, tokens),
            total_block,
            whole_block(inverse.shape),
            whole_block(cos.shape),
            whole_block(sin.shape),
        ],
        out_specs=[whole_block((width, tokens))] * 2,
        out_shape=[jax.ShapeDtypeStruct((width, tokens), bf16)] * 2,
        scratch_shapes=[
            pltpu.VMEM((tokens, HEAD_DIM), bf16),
            pltpu.VMEM((tokens, HEAD_DIM), bf16),
            pltpu.VMEM((tokens, HEAD_DIM), f32),
            pltpu.VMEM((tokens, HEAD_DIM), f32),
        ],
        compiler_params=pltpu.CompilerParams(vmem_limit_bytes=20 * 2**20),
        cost_estimate=LONG,
        name="attend_back",
    )(turned, turned, turned, out, grad, totals, inverse, cos, sin)


def build_kernel(gated, refs):
    tokens, (expand_ref, pick_ref, core_ref) = refs[:8], refs[8:11]
    outs, token_s = refs[11:19], refs[19]
    step = pl.program_id(0)
    for r in range(4):

        @pl.when(step == r)
        def _(r=r):
            token_s[0] = tokens[2 * r][...]
            token_s[1] = tokens[2 * r + 1][...]

    count = tokens[0].shape[0]
    index = lax.broadcasted_iota(jnp.int32, (ROWS, count), 0).astype(f32)
    below = lax.broadcasted_iota(jnp.int32, (8, 128), 0)
    across = lax.broadcasted_iota(jnp.int32, (8, 128), 1)
    pieces = []
    for s in (core_ref[0], 1 - core_ref[0]):
        slots = dot(expand_ref[...], token_s[s, :, HALF:], 1, 1)
        hot = jnp.concatenate(
            [
                jnp.where(slots[k * ROWS : (k + 1) * ROWS] == index, 1.0, 0.0)
                for k in range(8)
            ],
            axis=0,
        ).astype(bf16)
        rows = dot(hot, token_s[s, :, :HALF], 1, 0)
        parts = [rows[k * ROWS : (k + 1) * ROWS] for k in range(8)]
        if gated:
            gates = dot(pick_ref[...], token_s[s, :, HALF:], 1, 1).astype(bf16)
            for d in range(4):
                values = dot(gates, hot[d * PAIR : d * PAIR + 128], 1, 1)
                high, low = values[2 * d : 2 * d + 1], values[2 * d + 1 : 2 * d + 2]
                spare = jnp.where(below == 4, high, jnp.where(below == 5, low, 0.0))
                spare = jnp.where(across < ROWS, spare, 0.0)
                part = parts[2 * d]
                last = jnp.concatenate([part[64:, :128] + spare, part[64:, 128:]], axis=1)
                parts[2 * d] = jnp.concatenate([part[:64], last], axis=0)
        pieces.append(parts)
    for k in range(8):
        outs[k][0] = jnp.concatenate([pieces[0][k], pieces[1][k]], axis=0).astype(bf16)


def build(core, blocks, expand, pick, gated):
    count, width = blocks[0].shape
    whole = lambda shape: pl.BlockSpec(shape, lambda r: (0,) * len(shape))
    outs = pl.pallas_call(
        lambda *refs: build_kernel(gated, refs),
        grid=(4,),
        in_specs=[whole((count, width))] * 8
        + [whole(expand.shape), whole(pick.shape), pl.BlockSpec(memory_space=pltpu.SMEM)],
        out_specs=[pl.BlockSpec((1, PAIR, HALF), lambda r: (r, 0, 0))] * 8,
        out_shape=[jax.ShapeDtypeStruct((4, PAIR, HALF), bf16)] * 8,
        scratch_shapes=[pltpu.VMEM((2, count, width), bf16)],
        compiler_params=pltpu.CompilerParams(vmem_limit_bytes=VMEM_LIMIT),
        cost_estimate=BRIEF if gated else LONG,
        name="build_rows",
    )(*blocks, expand, pick, core)
    return [[outs[2 * d], outs[2 * d + 1]] for d in range(4)]


def combine_kernel(gated, refs):
    given, slots, (expand_ref, aim_ref, pick_ref, core_ref) = refs[:8], refs[8:16], refs[16:20]
    outs, total_s, slot_s = refs[20:28], refs[28], refs[29]
    core = core_ref[0]
    step = pl.program_id(0)
    for r in range(4):

        @pl.when(step == r)
        def _(r=r):
            slot_s[0] = slots[2 * r][...]
            slot_s[1] = slots[2 * r + 1][...]

    rows = jnp.concatenate([ref[0] for ref in given], axis=0)
    if gated:
        own = lax.broadcasted_iota(jnp.int32, (ROWS, 128), 0)
        own = own == lax.broadcasted_iota(jnp.int32, (ROWS, 128), 1)
        columns = []
        for d in range(4):
            head = given[2 * d][0, :, :128].astype(f32)
            for s in range(2):
                at = s * ROWS + CAP
                high = jnp.sum(jnp.where(own, head[at : at + 1], 0.0), axis=1, keepdims=True)
                low = jnp.sum(jnp.where(own, head[at + 1 : at + 2], 0.0), axis=1, keepdims=True)
                columns.append(
                    high * pick_ref[2 * d : 2 * d + 1] + low * pick_ref[2 * d + 1 : 2 * d + 2]
                )
            columns.append(jnp.zeros((PAIR, EXTRA), f32))
        rows = jnp.concatenate([rows, jnp.concatenate(columns, axis=0).astype(bf16)], axis=1)
    hots = []
    for s in range(2):
        hot = dot(slot_s[core if s == 0 else 1 - core], expand_ref[...], 1, 0)
        hot = hot == aim_ref[s : s + 1]
        hots.append(jnp.where(hot, 1.0, 0.0).astype(bf16))
    total = dot(jnp.concatenate(hots, axis=0), rows, 1, 0).astype(bf16)
    count = slot_s.shape[1]
    total_s[0] = total[:count]
    total_s[1] = total[count:]
    for r in range(4):

        @pl.when(step == r)
        def _(r=r):
            outs[2 * r][...] = total_s[core]
            outs[2 * r + 1][...] = total_s[1 - core]


def combine(core, chunks, blocks, expand, aim, pick, gated):
    count = blocks[0].shape[0]
    width = HALF + (EXTRA if gated else 0)
    whole = lambda shape: pl.BlockSpec(shape, lambda r: (0,) * len(shape))
    return pl.pallas_call(
        lambda *refs: combine_kernel(gated, refs),
        grid=(4,),
        in_specs=[pl.BlockSpec((1, PAIR, HALF), lambda r: (r, 0, 0))] * 8
        + [pl.BlockSpec((count, EXTRA), lambda r: (0, HALF // EXTRA))] * 8
        + [
            whole(expand.shape),
            whole(aim.shape),
            whole(pick.shape),
            pl.BlockSpec(memory_space=pltpu.SMEM),
        ],
        out_specs=[whole((count, width))] * 8,
        out_shape=[jax.ShapeDtypeStruct((count, width), bf16)] * 8,
        scratch_shapes=[
            pltpu.VMEM((2, count, width), bf16),
            pltpu.VMEM((2, count, EXTRA), bf16),
        ],
        compiler_params=pltpu.CompilerParams(vmem_limit_bytes=VMEM_LIMIT),
        cost_estimate=LONG,
        name="combine_rows",
    )(*[piece for chunk in chunks for piece in chunk], *blocks, expand, aim, pick, core)


def whole_rows(core_ref, mine, other, mine_s):
    step = pl.program_id(0)
    for d in range(4):

        @pl.when(step == d)
        def _(d=d):
            for r in range(4):
                mine_s[r * PAIR : (r + 1) * PAIR, :] = mine[d][r]

    one = mine_s[...]
    two = jnp.concatenate([ref[0] for ref in other], axis=0)
    first = core_ref[0] == 0
    return one, jnp.concatenate([jnp.where(first, one, two), jnp.where(first, two, one)], axis=1)


def store_halves(core_ref, values, spare, mine, other):
    step = pl.program_id(0)
    first = core_ref[0] == 0
    one = jnp.where(first, values[:, :HALF], values[:, HALF:])
    two = jnp.where(first, values[:, HALF:], values[:, :HALF]).astype(bf16)
    if spare is not None:
        one = jnp.concatenate([one[:, :128] + spare, one[:, 128:]], axis=1)
    one = one.astype(bf16)
    for d in range(4):

        @pl.when(step == d)
        def _(d=d):
            for r in range(4):
                mine[d][r] = one[r * PAIR : (r + 1) * PAIR]

    for r in range(4):
        other[r][0] = two[r * PAIR : (r + 1) * PAIR]


def cotangent_kernel(*refs):
    core_ref, mine, other = refs[0], refs[1:5], refs[5:9]
    down_ref, rows_ref, hidden_ref, mine_s = refs[9:]
    _, rows = whole_rows(core_ref, mine, other, mine_s)
    rows_ref[0] = rows
    hidden_ref[0] = dot(rows, down_ref[...], 1, 1).astype(bf16)


def expert_kernel(*refs):
    core_ref, mine, other, up_ref, back_ref = refs[0], refs[1:5], refs[5:9], refs[9], refs[10]
    rows_ref, grad_ref, hidden_ref = refs[11:14]
    mine_out, other_out, mine_s = refs[14:18], refs[18:22], refs[22]
    one, rows = whole_rows(core_ref, mine, other, mine_s)
    rows_ref[0] = rows
    own = lax.broadcasted_iota(jnp.int32, (ROWS, 128), 0)
    own = own == lax.broadcasted_iota(jnp.int32, (ROWS, 128), 1)
    head = one[:, :128].astype(f32)
    gates = []
    for i in range(LINE // ROWS):
        at = i * ROWS + CAP
        line = head[at : at + 1] + head[at + 1 : at + 2]
        gates.append(jnp.sum(jnp.where(own, line, 0.0), axis=1, keepdims=True))
    gate = jnp.concatenate(gates, axis=0)
    low, high = slice(0, FF), slice(FF, 2 * FF)
    gate_part = dot(rows, up_ref[:, low], 1, 0)
    up_part = dot(rows, up_ref[:, high], 1, 0)
    sigmoid = 1.0 / (1.0 + jnp.exp(-gate_part))
    silu = gate_part * sigmoid
    hidden = silu * up_part
    back = back_ref[0].astype(f32)
    inner = jnp.sum(hidden * back, axis=1, keepdims=True)
    hidden_ref[0] = (gate * hidden).astype(bf16)
    back = gate * back
    grad_one = (back * up_part * (sigmoid + silu * (1.0 - sigmoid))).astype(bf16)
    grad_two = (back * silu).astype(bf16)
    grad_ref[0, :, low] = grad_one
    grad_ref[0, :, high] = grad_two
    total = dot(grad_one, up_ref[:, low], 1, 1) + dot(grad_two, up_ref[:, high], 1, 1)
    below = lax.broadcasted_iota(jnp.int32, (8, 128), 0)
    spares = []
    for i in range(LINE // ROWS):
        line = jnp.where(own, inner[i * ROWS : (i + 1) * ROWS], 0.0)
        line = jnp.sum(line, axis=0, keepdims=True)
        high = line.astype(bf16).astype(f32)
        spare = jnp.where(below == 4, high, jnp.where(below == 5, line - high, 0.0))
        spares += [jnp.zeros((ROWS - 8, 128), f32), spare]
    store_halves(
        core_ref, total, jnp.concatenate(spares, axis=0), mine_out, other_out
    )


def result_kernel(*refs):
    core_ref, hidden_ref, down_ref = refs[:3]
    store_halves(core_ref, dot(hidden_ref[0], down_ref[...], 1, 0), None, refs[3:7], refs[7:11])


def whole_spec(shape):
    return pl.BlockSpec(shape, lambda d: (0,) * len(shape))


def line_spec(rows, width):
    return pl.BlockSpec((1, rows, width), lambda d: (d, 0, 0))


CORE_SPEC = pl.BlockSpec(memory_space=pltpu.SMEM)
EXPERT_PARAMS = dict(compiler_params=pltpu.CompilerParams(vmem_limit_bytes=VMEM_LIMIT))


def cotangent_rows(core, mine, other, down):
    return pl.pallas_call(
        cotangent_kernel,
        grid=(4,),
        in_specs=[CORE_SPEC]
        + [whole_spec((4, PAIR, HALF))] * 4
        + [line_spec(PAIR, HALF)] * 4
        + [whole_spec(down.shape)],
        out_specs=(line_spec(LINE, 2 * HALF), line_spec(LINE, FF)),
        out_shape=(
            jax.ShapeDtypeStruct((4, LINE, 2 * HALF), bf16),
            jax.ShapeDtypeStruct((4, LINE, FF), bf16),
        ),
        scratch_shapes=[pltpu.VMEM((LINE, HALF), bf16)],
        cost_estimate=BRIEF,
        name="cotangent_rows",
        compiler_params=pltpu.CompilerParams(vmem_limit_bytes=VMEM_LIMIT),
    )(core, *mine, *other, down)


def expert_rows(core, mine, other, up, back):
    outs = pl.pallas_call(
        expert_kernel,
        grid=(4,),
        in_specs=[CORE_SPEC]
        + [whole_spec((4, PAIR, HALF))] * 4
        + [line_spec(PAIR, HALF)] * 4
        + [whole_spec(up.shape), line_spec(LINE, FF)],
        out_specs=[line_spec(LINE, 2 * HALF), line_spec(LINE, 2 * FF), line_spec(LINE, FF)]
        + [whole_spec((4, PAIR, HALF))] * 4
        + [line_spec(PAIR, HALF)] * 4,
        out_shape=[
            jax.ShapeDtypeStruct((4, LINE, 2 * HALF), bf16),
            jax.ShapeDtypeStruct((4, LINE, 2 * FF), bf16),
            jax.ShapeDtypeStruct((4, LINE, FF), bf16),
        ]
        + [jax.ShapeDtypeStruct((4, PAIR, HALF), bf16)] * 8,
        scratch_shapes=[pltpu.VMEM((LINE, HALF), bf16)],
        cost_estimate=BRIEF,
        name="expert_rows",
        **EXPERT_PARAMS,
    )(core, *mine, *other, up, back)
    return outs[0], outs[1], outs[2], outs[3:7], outs[7:11]


def result_rows(core, hidden, down):
    outs = pl.pallas_call(
        result_kernel,
        grid=(4,),
        in_specs=[CORE_SPEC, line_spec(LINE, FF), whole_spec(down.shape)],
        out_specs=[whole_spec((4, PAIR, HALF))] * 4 + [line_spec(PAIR, HALF)] * 4,
        out_shape=[jax.ShapeDtypeStruct((4, PAIR, HALF), bf16)] * 8,
        cost_estimate=LONG,
        name="result_rows",
        **EXPERT_PARAMS,
    )(core, hidden, down)
    return outs[:4], outs[4:]


def per_device(
    tokens,
    norm_gains,
    query_matrix,
    key_value_weight,
    output_weight,
    router,
    expert_up,
    expert_down,
    routes,
    cotangent,
):
    local_rows, model_width = tokens.shape
    query_width = query_matrix.shape[1]
    keyval_width = key_value_weight.shape[2]
    experts_all = router.shape[0]
    place = lax.axis_index("tensor")
    group = lax.axis_index("dp")

    expert_index = jnp.arange(experts_all, dtype=jnp.int32)
    picked = jnp.any(routes[:, :, None] == expert_index[None, None, :], axis=1)
    token_index = jnp.arange(local_rows, dtype=jnp.int32)
    before = (token_index[:, None] > token_index[None, :]).astype(bf16)
    rank = dot(before, picked.astype(bf16), 1, 0)
    slot = jnp.where(picked, rank, -1.0)
    core = lax.rem(group, 2)
    line_y, line_z = group // 8, lax.rem(group // 2, 4)
    core_scalar = jnp.reshape(core, (1,)).astype(jnp.int32)

    distance = jnp.arange(4, dtype=jnp.int32)
    chip = jnp.where(
        core == 0, line_y * 4 + (line_z + distance) % 4, ((line_y + distance) % 4) * 4 + line_z
    )
    partner = jnp.stack([2 * chip + core, 2 * chip + 1 - core], axis=1).reshape(8)
    lane = jnp.arange(EXTRA, dtype=jnp.int32)
    hit = lane[None, :] == partner[:, None] + 64
    expand = jnp.repeat(hit, ROWS, axis=0).astype(bf16)
    expand_turned = jnp.repeat(hit, PAIR, axis=0).T.astype(bf16)
    near = partner.reshape(4, 2)[:, 0]
    pick = jnp.stack([near, near + 32], axis=1).reshape(8)
    pick = jnp.pad((lane[None, :] == pick[:, None]).astype(bf16), ((0, 8), (0, 0)))
    pick_wide = pick.astype(f32)
    spot = jnp.arange(8 * PAIR, dtype=jnp.int32)
    aim = jnp.stack(
        [
            jnp.where((spot // ROWS) % 2 == s, spot % ROWS, -5 if s < 2 else -6).astype(f32)
            for s in range(8)
        ],
        axis=0,
    )

    def wide(values):
        return jnp.pad(values, ((0, 0), (0, EXTRA - values.shape[1])))

    up_matrix, down_matrix = expert_up[0], expert_down[0]

    inputs = tokens.astype(jnp.float32)
    inv_rms_one = inverse_rms(inputs)
    near = gather_near(tokens, False)
    cot_near = spread_near(
        cotangent, wide(jnp.concatenate([jnp.zeros((local_rows, 64), f32), slot], axis=1).astype(bf16)), core
    )
    sequence_length = 4 * local_rows
    joined_weight = jnp.concatenate(
        [query_matrix, key_value_weight.reshape(model_width, 2 * keyval_width)], axis=1
    )
    weight_turned = joined_weight.T
    gained_turned = (norm_gains[0][:, None] * joined_weight.astype(f32)).astype(bf16).T
    cos, sin = rotary_tables(sequence_length, HEAD_DIM)
    near, gained_turned, weight_turned, cos, sin, expand_turned, aim, pick_wide = sync(
        near, gained_turned, weight_turned, cos, sin, expand_turned, aim, pick_wide
    )
    pieces = gather_far(tokens, near, place)
    cot_chunks = build(core_scalar, spread_far(*cot_near), expand, pick, False)
    pieces, cot_chunks = sync(pieces, cot_chunks)
    cot_first = send_first(cot_chunks)
    projected, sequence, inverse = project(pieces, gained_turned, False)
    attended, log_totals, turned = attend(projected, inverse, cos, sin)
    def output_chunk(k):
        start = lax.rem(place + k, 4) * local_rows
        return dot(lax.dynamic_slice_in_dim(attended, start, local_rows, 1), output_weight, 0, 0)

    attended, cot_first = sync(attended, cot_first)
    far = scatter_far(output_chunk)
    cot_swapped = send_cross(cot_chunks)
    near = scatter_whole(output_chunk, *far)
    near, cot_swapped, cot_far = sync(near, cot_swapped, send_far(cot_first[0]))
    cot_got = gather_rows(cot_chunks, cot_first, cot_swapped, cot_far)
    middle = inputs + output_chunk(0) + near[0].astype(f32) + near[1].astype(f32)
    mixed_norm, inv_rms_two = norm_rows(middle, norm_gains[1])
    mixed_low = mixed_norm.astype(jnp.bfloat16)
    logits = dot(mixed_low, router, 1, 1)
    chosen = jnp.where(picked, logits, -jnp.inf)
    chosen_exp = jnp.exp(chosen - jnp.max(chosen, axis=1, keepdims=True))
    gates = chosen_exp / jnp.sum(chosen_exp, axis=1, keepdims=True)

    gates_high, gates_low = split_two(gates)
    mixed_near = spread_near(
        mixed_low, wide(jnp.concatenate([gates_high, gates_low, slot], axis=1).astype(bf16)), core
    )
    mixed_blocks = spread_far(*mixed_near)
    mixed_chunks = build(core_scalar, mixed_blocks, expand, pick, True)
    cot_rows, grad_hidden_one = cotangent_rows(core_scalar, *cot_got, down_matrix)
    mixed_first, grad_hidden_one = sync(send_first(mixed_chunks), grad_hidden_one)
    mixed_got = send_rest(mixed_chunks, *mixed_first)
    mixed_got, grad_hidden_one = sync(mixed_got, grad_hidden_one)
    rows_in, grad_gate_up, hidden_gated, grad_mine, grad_other = expert_rows(
        core_scalar, *mixed_got, up_matrix, grad_hidden_one
    )

    rows_in = rows_in.reshape(4 * LINE, model_width)
    cot_rows = cot_rows.reshape(4 * LINE, model_width)
    grad_gate_up = grad_gate_up.reshape(4 * LINE, 2 * FF)
    hidden_flat = hidden_gated.reshape(4 * LINE, FF)
    up_grad = dot(rows_in, grad_gate_up, 0, 0).astype(bf16)
    grad_first, up_grad = sync(return_first(grad_mine, grad_other), up_grad)
    down_grad = dot(cot_rows, hidden_flat, 0, 0).astype(bf16)
    grad_chunks = return_rest(grad_mine, grad_other, *grad_first)
    expert_grads = jnp.concatenate([up_grad, down_grad], axis=1)
    grad_chunks, expert_grads, hidden_gated = sync(grad_chunks, expert_grads, hidden_gated)
    expert_rows_out = model_width // 4

    def expert_chunk(k):
        start = lax.rem(place + k, 4) * expert_rows_out
        return lax.dynamic_slice_in_dim(expert_grads, start, expert_rows_out, 0)

    grad_blocks = combine(core_scalar, grad_chunks, mixed_blocks, expand_turned, aim, pick_wide, True)
    grad_blocks, expert_far, hidden_gated = sync(
        grad_blocks, scatter_far(expert_chunk), hidden_gated
    )
    result_mine, result_other = result_rows(core_scalar, hidden_gated, down_matrix)
    passing, expert_plain = sync(sum_far(grad_blocks), scatter_plain(expert_chunk))
    grad_mixed, grad_gate = sum_near(grad_blocks, passing, core)
    grad_mixed, grad_gate, result_mine, result_other = sync(
        grad_mixed, grad_gate, result_mine, result_other
    )
    grad_gate = grad_gate[:, :32] + grad_gate[:, 32:64]

    grad_logits = gates * (grad_gate - jnp.sum(gates * grad_gate, axis=1, keepdims=True))
    grad_mixed = grad_mixed + dot(grad_logits, router.astype(f32), 1, 0, highest)
    router_part = dot(grad_logits, mixed_low.astype(f32), 0, 0, highest)
    grad_out = cotangent.astype(jnp.float32)
    grad_middle = grad_out + norm_back(middle, inv_rms_two, norm_gains[1], grad_mixed)
    gain_two_part = jnp.sum(grad_mixed * middle * inv_rms_two, axis=0)

    grad_low = grad_middle.astype(bf16)
    router_part, result_mine, result_other = sync(router_part, result_mine, result_other)
    near = gather_near(grad_low, False)
    middle_rows = [move(result_mine[2], ACROSS, 1, 0), move(result_other[2], ALONG, -1, 1)]
    back_near = move(result_mine[1], ACROSS, -1, 0)
    near, middle_rows, back_near = sync(near, middle_rows, back_near)
    pieces = gather_far(grad_low, near, place)
    back_wide = move(result_mine[3], ACROSS, 1, 0)
    other_near = move(result_other[1], ALONG, -1, 1)
    other_wide = move(result_other[3], ALONG, 1, 1)
    grad_attended, grad_attn_seq = project(pieces, output_weight, True)
    small_high, small_low = split_two(
        jnp.concatenate([router_part, gain_two_part[None], jnp.zeros((31, model_width), f32)], axis=0)
    )
    small_rows = jnp.concatenate([small_high, small_low], axis=0)
    dp_size = 32
    dp_rows = model_width // dp_size
    grad_attended, back_wide, other_near, other_wide, expert_far = sync(
        grad_attended, back_wide, other_near, other_wide, expert_far
    )
    far_rows = [move(middle_rows[0], ACROSS, 1, 0), move(middle_rows[1], ACROSS, -1, 0)]
    swapped = swap_core(result_other[0])
    expert_near = scatter_summed(expert_chunk, *expert_far)
    grad_projected, grad_scaled = attend_back(
        turned, attended, grad_attended, log_totals, inverse, cos, sin
    )
    grad_projected, grad_scaled, far_rows, swapped, expert_near = sync(
        grad_projected, grad_scaled, far_rows, swapped, expert_near
    )
    joined_keep, joined_send = weight_grads(
        core_scalar, grad_scaled, sequence, norm_gains[0:1], attended, grad_attn_seq, small_rows
    )
    joined_grad = (joined_keep.astype(f32) + swap_core(joined_send).astype(f32)).astype(bf16)
    grad_projected, joined_grad, far_rows, swapped = sync(
        grad_projected, joined_grad, far_rows, swapped
    )

    def normed_chunk(grads, k):
        start = lax.rem(place + k, 4) * local_rows
        piece = lax.dynamic_slice_in_dim(grads, start, local_rows, 1)
        return dot(piece, weight_turned, 0, 0)

    far = scatter_far(lambda k: normed_chunk(grad_projected, k))
    near = scatter_whole(lambda k: normed_chunk(grad_projected, k), *far)
    result_chunks = [
        [result_mine[0], swapped],
        [back_near, other_near],
        far_rows,
        [back_wide, other_wide],
    ]
    joined_terms = lax.all_to_all(
        joined_grad.reshape(dp_size // 2, dp_rows, joined_grad.shape[1]),
        "dp",
        split_axis=0,
        concat_axis=0,
        tiled=True,
        axis_index_groups=[[2 * i + c for i in range(16)] for c in range(2)],
    )
    result_blocks = combine(
        core_scalar, result_chunks, mixed_blocks, expand_turned, aim, pick_wide, False
    )
    result_far, joined_terms, near = sync(sum_far(result_blocks), joined_terms, near)
    moe_sum, _ = sum_near(result_blocks, result_far, core)
    grad_normed = normed_chunk(grad_projected, 0) + near[0].astype(f32) + near[1].astype(f32)
    weight_all = add_terms(joined_terms)
    joined_all = weight_all[:, : query_width + 2 * keyval_width]
    output_all = weight_all[:, query_width + 2 * keyval_width :]
    expert_up_grad, expert_down_grad = expert_sums(
        jnp.reshape(place, (1,)),
        expert_grads,
        expert_near[0],
        expert_plain[0],
        expert_plain[1],
        expert_near[1],
    )
    expert_up_grad, expert_down_grad = expert_up_grad[None], expert_down_grad[None]
    query_weight_grad = joined_all[:, :query_width]
    keyval_weight_grad = joined_all[:, query_width:].reshape(dp_rows, 2, keyval_width)
    output_weight_grad = output_all[:, :query_width].T
    tokens_grad = grad_middle + norm_back(inputs, inv_rms_one, norm_gains[0], grad_normed)

    weight_rows = lax.dynamic_slice_in_dim(joined_weight, group * dp_rows, dp_rows, 0)
    gain_rows = lax.dynamic_slice_in_dim(norm_gains[0], group * dp_rows, dp_rows, 0)
    gain_one_part = jnp.sum(weight_rows.astype(f32) * joined_all, axis=1) / gain_rows
    base = query_width
    small = jnp.concatenate(
        [
            output_all[:, base : base + 33] + output_all[:, base + 64 : base + 97],
            gain_one_part[:, None],
            jnp.zeros((dp_rows, 94), f32),
        ],
        axis=1,
    ).reshape(4, dp_rows // 4, 128)
    small = jnp.pad(small, ((0, 0), (0, 4), (0, 0)))
    small = lax.all_to_all(small, "tensor", split_axis=0, concat_axis=0, tiled=True)
    small = jnp.sum(small, axis=0)[: dp_rows // 4].T
    router_grad = small[:experts_all]
    gains_grad = jnp.stack([small[experts_all + 1], small[experts_all]])

    layer_out = (middle + moe_sum).astype(jnp.bfloat16)
    return (
        layer_out,
        tokens_grad,
        gains_grad,
        query_weight_grad,
        keyval_weight_grad,
        output_weight_grad,
        router_grad,
        expert_up_grad,
        expert_down_grad,
    )


def solution(mesh):
    placed = (
        P(("dp", "tensor"), None),
        P(),
        P(None, "tensor"),
        P(None, None, "tensor"),
        P("tensor", None),
        P(),
        P("dp", None, None),
        P("dp", None, None),
        P(("dp", "tensor"), None),
        P(("dp", "tensor"), None),
    )
    return jax.shard_map(
        per_device,
        mesh=mesh,
        in_specs=placed,
        out_specs=(
            P(("dp", "tensor"), None),
            P(("dp", "tensor"), None),
            P(None, ("dp", "tensor")),
            P("dp", "tensor"),
            P("dp", None, "tensor"),
            P("tensor", "dp"),
            P(None, ("dp", "tensor")),
            P("dp", "tensor", None),
            P("dp", None, "tensor"),
        ),
        check_vma=False,
    )
```
